32 devices in a mesh: fsdp: 8 (over z, y), ctx: 4 (over x, core).
Axes of the slice: x: 2, y: 2, z: 4, core: 2. Of those that a mesh axis runs over, the one named last changes fastest.
Arguments:
- tokens: bfloat16 [8, 1024, 2048], P('fsdp', 'ctx'), may hold values from -6 to 6
- positions: int32 [8, 1024], P('fsdp', 'ctx'), may hold values from 0 to 1021, as said below
- attn_gain: bfloat16 [2048], P(('fsdp', 'ctx')), may hold values from 0.25 to 1.75
- w_query: bfloat16 [2048, 2048], P(('fsdp', 'ctx')), may hold values from -0.125 to 0.125
- w_key: bfloat16 [2048, 2048], P(('fsdp', 'ctx')), may hold values from -0.125 to 0.125
- w_value: bfloat16 [2048, 2048], P(('fsdp', 'ctx')), may hold values from -0.125 to 0.125
- w_out: bfloat16 [2048, 2048], P(None, ('fsdp', 'ctx')), may hold values from -1 to 1
- mlp_gain: bfloat16 [2048], P(('fsdp', 'ctx')), may hold values from 0.25 to 1.75
- w_gate: bfloat16 [2048, 8192], P(('fsdp', 'ctx')), may hold values from -0.125 to 0.125
- w_up: bfloat16 [2048, 8192], P(('fsdp', 'ctx')), may hold values from -0.125 to 0.125
- w_down: bfloat16 [8192, 2048], P(None, ('fsdp', 'ctx')), may hold values from -0.0625 to 0.0625
- out_grad: bfloat16 [8, 1024, 2048], P('fsdp', 'ctx'), may hold values from -6 to 6
Outputs:
- block_out: bfloat16 [8, 1024, 2048], P('fsdp', 'ctx')
- tokens_grad: bfloat16 [8, 1024, 2048], P('fsdp', 'ctx')
- attn_gain_grad: float32 [2048], P(('fsdp', 'ctx'))
- w_query_grad: float32 [2048, 2048], P(('fsdp', 'ctx'))
- w_key_grad: float32 [2048, 2048], P(('fsdp', 'ctx'))
- w_value_grad: float32 [2048, 2048], P(('fsdp', 'ctx'))
- w_out_grad: float32 [2048, 2048], P(None, ('fsdp', 'ctx'))
- mlp_gain_grad: float32 [2048], P(('fsdp', 'ctx'))
- w_gate_grad: float32 [2048, 8192], P(('fsdp', 'ctx'))
- w_up_grad: float32 [2048, 8192], P(('fsdp', 'ctx'))
- w_down_grad: float32 [8192, 2048], P(None, ('fsdp', 'ctx'))
The draws below stay inside these ranges and needn't reach their ends.
Inputs may be any that keep to these rules, and one draw needn't show every extreme that they name: `positions`: each sequence holds three documents laid end to end, and a token's position counts the tokens before it in its own document. The first document has 1 to 128 tokens, the last one likewise, and the middle one holds the rest. In at least one sequence the first and the last documents hold one token each.
All inputs are finite; a program needn't handle non-finite values.
Results may differ from the reference program's by a relative error of at most 0.015.
Values may be sent and summed in bfloat16 or wider, within the bound.
No kernel may reach another device: no remote copies, remote signals or barrier semaphores. Data moves between devices by JAX's collectives and lax.ppermute only.
A program may use at most 768 MiB of HBM per device.

```python
import jax
import jax.numpy as jnp
from jax import lax

D = 2048
H = 32
HD = 64
FF = 8192
SEQ_LEN = 1024
TOK_DEV = 256
SEQS = 8


def draw_positions(key, part):
    key = jax.random.fold_in(key, 11)
    start_key, end_key, pick_key = jax.random.split(key, 3)
    first_end = jax.random.randint(start_key, (SEQS, 1), 1, TOK_DEV // 2 + 1)
    last_start = SEQ_LEN - jax.random.randint(end_key, (SEQS, 1), 1, TOK_DEV // 2 + 1)
    chosen = jax.random.randint(pick_key, (), 0, SEQS)
    rows = jnp.arange(SEQS, dtype=jnp.int32)[:, None]
    first_end = jnp.where(rows == chosen, 1, first_end)
    last_start = jnp.where(rows == chosen, SEQ_LEN - 1, last_start)
    places = jnp.arange(SEQ_LEN, dtype=jnp.int32)[None, :]
    begins = jnp.where(places >= last_start, last_start, jnp.where(places >= first_end, first_end, 0))
    return (places - begins).astype(jnp.int32)


def levels(key, dims, cuts, least, high):
    factor_of = 1.0
    for dim, parts in cuts:
        draws = jax.random.uniform(jax.random.fold_in(jax.random.fold_in(key, 6), dim), (parts,), jnp.float32, least / len(cuts), high / len(cuts))
        factor_of = factor_of * jnp.repeat(jnp.exp(draws), dims[dim] // parts).reshape((-1,) + (1,) * (len(dims) - 1 - dim))
    return factor_of


def scatter_about(key, dims, scale, reach, cuts=(), held_as=jnp.bfloat16):
    entries = scale * jax.random.normal(key, dims, jnp.float32)
    if cuts:
        entries = entries * levels(key, dims, cuts, -0.22, 0.18)
    return jnp.clip(entries, -reach, reach).astype(held_as)


def setup_inputs(seed: int = 0) -> dict:
    seeds = jax.random.split(jax.random.key(seed), 13)
    tokens = scatter_about(seeds[0], (SEQS, SEQ_LEN, D), 1.0, 6.0, ((0, 8), (1, 4)))
    positions = draw_positions(jax.random.fold_in(seeds[12], 71), 0)
    attn_gain = jnp.clip(1.0 + 0.15 * jax.random.normal(seeds[2], (D,), jnp.float32), 0.25, 1.75).astype(jnp.bfloat16)
    w_query = scatter_about(seeds[3], (D, D), D ** -0.5, 0.125, ((0, 32),))
    w_key = scatter_about(seeds[4], (D, D), D ** -0.5, 0.125, ((0, 32),))
    w_value = scatter_about(seeds[5], (D, D), D ** -0.5, 0.125, ((0, 32),))
    w_out = scatter_about(seeds[6], (D, D), (D // 64) ** -0.5, 1.0, ((1, 32),))
    mlp_gain = jnp.clip(1.0 + 0.15 * jax.random.normal(seeds[7], (D,), jnp.float32), 0.25, 1.75).astype(jnp.bfloat16)
    w_gate = scatter_about(seeds[8], (D, FF), D ** -0.5, 0.125, ((0, 32),))
    w_up = scatter_about(seeds[9], (D, FF), D ** -0.5, 0.125, ((0, 32),))
    w_down = scatter_about(seeds[10], (FF, D), FF ** -0.5, 0.0625, ((1, 32),))
    out_grad = scatter_about(seeds[11], (SEQS, SEQ_LEN, D), 1.0, 6.0, ((0, 8), (1, 4)))
    return dict(tokens=tokens, positions=positions, attn_gain=attn_gain, w_query=w_query, w_key=w_key, w_value=w_value, w_out=w_out, mlp_gain=mlp_gain, w_gate=w_gate, w_up=w_up, w_down=w_down, out_grad=out_grad)


@jax.custom_vjp
def low(v):
    return lax.optimization_barrier(v.astype(jnp.bfloat16)).astype(jnp.float32)

@jax.custom_vjp
def low_back(v):
    return v

def low_keep(v):
    return (low(v), None)

def low_pass(kept, grad):
    return (grad,)

def back_keep(v):
    return (v, None)

def back_low(kept, grad):
    return (low(grad),)
low.defvjp(low_keep, low_pass)
low_back.defvjp(back_keep, back_low)
EPSILON = 1e-05
ROPE_BASE = 130000.0
MASKED_SCORE = -1e+30

def matmul(left_side, right_side):
    return jnp.dot(left_side, right_side, precision=lax.Precision.HIGHEST, preferred_element_type=jnp.float32)

def rms_gain(values, gain_vec):
    return values * lax.rsqrt(lax.optimization_barrier(jnp.mean(values * values, axis=-1, keepdims=True)) + EPSILON) * gain_vec

def angle_tables(positions):
    inverse_freq = 1.0 / ROPE_BASE ** (jnp.arange(0, HD, 2, dtype=jnp.float32) / HD)
    angles = positions.astype(jnp.float32)[:, None] * inverse_freq[None, :]
    return (jnp.cos(angles)[:, None, :], jnp.sin(angles)[:, None, :])

def rotate(values, cosine_table, sine_table):
    half_dim = values.shape[-1] // 2
    first = values[..., :half_dim]
    second = values[..., half_dim:]
    return jnp.concatenate([first * cosine_table - second * sine_table, second * cosine_table + first * sine_table], axis=-1)

def one_sequence(weights, sequence):
    attn_gain, w_query, w_key, w_value, w_out, mlp_gain, w_gate, w_up, w_down = weights
    inputs, positions = sequence
    normed = low(rms_gain(inputs, attn_gain))
    cosine_table, sine_table = angle_tables(positions)
    queries = low(rotate(low_back(matmul(normed, w_query)).reshape(SEQ_LEN, H, HD), cosine_table, sine_table))
    key_rows = low(rotate(low_back(matmul(normed, w_key)).reshape(SEQ_LEN, H, HD), cosine_table, sine_table))
    value_rows = low(low_back(matmul(normed, w_value))).reshape(SEQ_LEN, H, HD)
    raw_scores = jnp.einsum('the,jhe->htj', queries, key_rows, precision=lax.Precision.HIGHEST) * HD ** (-0.5)
    scores = low_back(raw_scores)
    places = jnp.arange(SEQ_LEN, dtype=jnp.int32)
    visible = (places[None, :] <= places[:, None]) & (places[None, :] >= (places - positions)[:, None])
    probs = jax.nn.softmax(jnp.where(visible[None], scores, MASKED_SCORE), axis=-1)
    mixed_heads = jnp.einsum('htj,jhe->the', low(probs), value_rows, precision=lax.Precision.HIGHEST)
    mixed_heads = low(low_back(mixed_heads.reshape(SEQ_LEN, D)))
    first_sum = inputs + low_back(matmul(mixed_heads, w_out))
    normed_two = low(rms_gain(first_sum, mlp_gain))
    gate_proj = low_back(matmul(normed_two, w_gate))
    up_proj = low_back(matmul(normed_two, w_up))
    hidden = low(jax.nn.silu(gate_proj) * up_proj)
    return first_sum + low_back(matmul(hidden, w_down))

def reference(tokens, positions, attn_gain, w_query, w_key, w_value, w_out, mlp_gain, w_gate, w_up, w_down, out_grad):
    floats = tuple((item.astype(jnp.float32) for item in (tokens, attn_gain, w_query, w_key, w_value, w_out, mlp_gain, w_gate, w_up, w_down)))
    per_sequence = jax.checkpoint(one_sequence)

    def forward(inputs, *weights):

        def apply_one(sequence):
            return per_sequence(weights, sequence)
        return lax.map(apply_one, (inputs, positions))
    block_out, pullback = jax.vjp(forward, *floats)
    gradients = pullback(out_grad.astype(jnp.float32))
    return (block_out.astype(jnp.bfloat16), gradients[0].astype(jnp.bfloat16), gradients[1], gradients[2], gradients[3], gradients[4], gradients[5], gradients[6], gradients[7], gradients[8], gradients[9])
```

```python
import functools

import jax
import jax.numpy as jnp
from jax import lax
from jax.experimental import pallas as pl
from jax.experimental.pallas import tpu as pltpu
from jax.sharding import Mesh
from jax.sharding import PartitionSpec as P

H = 32
HD = 64
EPSILON = 1e-05
ROPE_BASE = 130000.0
MASKED_SCORE = -1e30
SCALE = HD ** (-0.5)
LANES = 128
MIB = 1 << 20
BF16 = jnp.bfloat16
F32 = jnp.float32
AXES = ("r", "zh", "zl", "y", "x", "c")
NT = (((1,), (1,)), ((), ()))
TN = (((0,), (0,)), ((), ()))


def dot_nn(a, b):
    return jnp.dot(a, b, preferred_element_type=F32)


def dot_nt(a, b):
    return lax.dot_general(a, b, NT, preferred_element_type=F32)


def dot_tn(a, b):
    return lax.dot_general(a, b, TN, preferred_element_type=F32)


def swap(x, axis):
    return lax.ppermute(x, axis, [(0, 1), (1, 0)])


def swap_slot(x, axes, slot):
    if slot == 0:
        return x
    return lax.ppermute(x, axes, [(i, i ^ slot) for i in range(8)])


class Group:
    def __init__(self, d1, d2, g1, g2):
        self.d1, self.d2, self.g1, self.g2 = d1, d2, g1, g2
        self.axes = (d1, d2, "c")

    def index(self):
        return lax.axis_index(self.d1) * 4 + lax.axis_index(self.d2) * 2 + lax.axis_index("c")

    def column_chunks(self, outer):
        names = ("zh", "zl", "y", "x")
        strides = dict(zip(names, (8, 4, 2, 1)))
        order = []
        for r in range(outer):
            for slot in range(16):
                bits = dict(zip((self.g2, self.g1, self.d1, self.d2), ((slot >> 3) & 1, (slot >> 2) & 1, (slot >> 1) & 1, slot & 1)))
                order.append(r * 16 + sum(strides[n] * bits[n] for n in names))
        return order

    def reorder(self, x, order):
        if order == list(range(len(order))):
            return x
        width = x.shape[1] // len(order)
        return jnp.concatenate([x[:, i * width : (i + 1) * width] for i in order], axis=1)

    def flip_blocks(self, x, outer):
        mine = lax.axis_index(self.g2) * 2 + lax.axis_index(self.g1)
        width = x.shape[1] // (4 * outer)
        return jnp.concatenate(
            [
                lax.dynamic_slice_in_dim(x, (r * 4 + (slot ^ mine)) * width, width, axis=1)
                for r in range(outer)
                for slot in range(4)
            ],
            axis=1,
        )

    def to_slots(self, x, outer):
        return self.flip_blocks(self.reorder(x, self.column_chunks(outer)), outer)

    def from_slots(self, x, outer):
        order = self.column_chunks(outer)
        back = [order.index(i) for i in range(len(order))]
        return self.reorder(self.flip_blocks(x, outer), back)

    def gather_tokens(self, x):
        half = x.shape[0] // 2
        from_one = swap(x, self.d1)
        from_two = swap(x, self.d2)
        own_core = swap(x, "c")
        top = swap(from_two[:half], self.d1)
        bottom = swap(from_one[half:], self.d2)
        pieces = [x, own_core, from_two, swap(from_two, "c"), from_one, swap(from_one, "c")]
        pieces += [top, bottom, swap(top, "c"), swap(bottom, "c")]
        return jnp.concatenate(pieces, axis=0)

    def scatter_tokens(self, partial):
        def over_cores(i):
            both = partial(i)
            count = both.shape[0] // 2
            return both[:count] + swap(both[count:].astype(BF16), "c").astype(F32)

        far = over_cores(3)
        half = far.shape[0] // 2
        top = swap(far[:half].astype(BF16), self.d1).astype(F32)
        bottom = swap(far[half:].astype(BF16), self.d2).astype(F32)
        two = over_cores(1)
        one = over_cores(2)
        two_bottom = swap(two[half:].astype(BF16), self.d2)
        one_top = swap(one[:half].astype(BF16), self.d1)
        two_top = swap((two[:half] + top).astype(BF16), self.d2)
        one_bottom = swap((one[half:] + bottom).astype(BF16), self.d1)
        own = over_cores(0)
        from_two = jnp.concatenate([two_top, two_bottom], axis=0).astype(F32)
        from_one = jnp.concatenate([one_top, one_bottom], axis=0).astype(F32)
        return own + from_two + from_one

    def gather_weight(self, blocks):
        rows = [swap_slot(b, self.axes, s) for s, b in enumerate(blocks)]
        mine = join_rows(rows, self.index())
        one = swap(mine, self.g1)
        two = swap(mine, self.g2)
        both = swap(one, self.g2)
        whole = jnp.concatenate([mine, one, two, both], axis=0)
        if lax.axis_size("r") > 1:
            whole = lax.all_gather(whole, "r", axis=0, tiled=True)
        return whole

    def scatter_weight(self, left, right):
        width = left.shape[1] // 4
        if lax.axis_size("r") > 1:
            whole = lax.psum_scatter(dot_tn(left, right), "r", scatter_dimension=0, tiled=True)
            width = whole.shape[0] // 4

            def term(slot):
                return whole[slot * width : (slot + 1) * width]

        else:

            def term(slot):
                return dot_tn(left[:, slot * width : (slot + 1) * width], right)

        both = swap(term(3).astype(BF16), self.g2).astype(F32)
        one = swap((term(1) + both).astype(BF16), self.g1).astype(F32)
        two = swap(term(2).astype(BF16), self.g2).astype(F32)
        mine = (term(0) + two + one).astype(BF16)
        blocks = split_rows(mine, self.index())
        return [swap_slot(b, self.axes, s) for s, b in enumerate(blocks)]


def scalar(value):
    return jnp.reshape(value, (1,)).astype(jnp.int32)


SMEM_SPEC = pl.BlockSpec(memory_space=pltpu.SMEM)
VMEM_SPEC = pl.BlockSpec(memory_space=pltpu.VMEM)


def cost(flops, moved):
    return pl.CostEstimate(flops=flops, bytes_accessed=moved, transcendentals=0)


def parts_of(widths):
    if len(widths) == 1:
        return [(0, 0, widths[0])]
    return [(i, p * LANES, LANES) for p in range(widths[0] // LANES) for i in range(len(widths))]


def split_columns(weights, gain, index):
    rows = weights[0].shape[0]
    widths = [w.shape[1] // 8 for w in weights]
    total = sum(widths)
    parts = parts_of(widths)

    def body(index_ref, *refs):
        ins, outs = refs[: len(weights)], refs[-8:]
        factor = refs[len(weights)][...] if gain is not None else None
        me = index_ref[0]
        for slot in range(8):
            at = 0
            for i, offset, width in parts:
                start = pl.multiple_of((me ^ slot) * widths[i] + offset, LANES)
                piece = ins[i][:, pl.ds(start, width)]
                if factor is not None:
                    piece = (piece.astype(F32) * factor).astype(BF16)
                outs[slot][:, at : at + width] = piece
                at += width

    args = list(weights) + ([gain] if gain is not None else [])
    return pl.pallas_call(
        body,
        out_shape=[jax.ShapeDtypeStruct((rows, total), BF16)] * 8,
        in_specs=[SMEM_SPEC] + [VMEM_SPEC] * len(args),
        out_specs=[VMEM_SPEC] * 8,
        cost_estimate=cost(0, 32 * rows * total),
        name="split_columns",
    )(scalar(index), *args)


def join_rows(blocks, index):
    rows, total = blocks[0].shape

    def body(index_ref, *refs):
        me = index_ref[0]
        for slot in range(8):
            refs[8][pl.ds(pl.multiple_of((me ^ slot) * rows, rows), rows), :] = refs[slot][...]

    return pl.pallas_call(
        body,
        out_shape=jax.ShapeDtypeStruct((8 * rows, total), BF16),
        in_specs=[SMEM_SPEC] + [VMEM_SPEC] * 8,
        out_specs=VMEM_SPEC,
        cost_estimate=cost(0, 32 * rows * total),
        name="join_rows",
    )(scalar(index), *blocks)


def split_rows(whole, index):
    rows, total = whole.shape[0] // 8, whole.shape[1]

    def body(index_ref, whole_ref, *outs):
        me = index_ref[0]
        for slot in range(8):
            outs[slot][...] = whole_ref[pl.ds(pl.multiple_of((me ^ slot) * rows, rows), rows), :]

    return pl.pallas_call(
        body,
        out_shape=[jax.ShapeDtypeStruct((rows, total), BF16)] * 8,
        in_specs=[SMEM_SPEC, VMEM_SPEC],
        out_specs=[VMEM_SPEC] * 8,
        cost_estimate=cost(0, 32 * rows * total),
        name="split_rows",
    )(scalar(index), whole)


def join_columns(blocks, weights, gain, index, count):
    rows, total = blocks[0].shape
    widths = [total // count] * count
    parts = parts_of(widths)

    def body(index_ref, *refs):
        ins = refs[:8]
        outs = refs[-count:] if gain is None else refs[-count - 1 : -1]
        me = index_ref[0]
        acc = jnp.zeros((rows, LANES), F32)
        for slot in range(8):
            at = 0
            for i, offset, width in parts:
                start = pl.multiple_of((me ^ slot) * widths[i] + offset, LANES)
                value = ins[slot][:, at : at + width].astype(F32)
                if gain is not None:
                    term = refs[9 + i][:, pl.ds(start, width)].astype(F32) * value
                    for p in range(width // LANES):
                        acc = acc + term[:, p * LANES : (p + 1) * LANES]
                    value = value * refs[8][...]
                outs[i][:, pl.ds(start, width)] = value
                at += width
        if gain is not None:
            refs[-1][...] = jnp.sum(acc, axis=1, keepdims=True)

    args = list(blocks) + ([gain] + list(weights) if gain is not None else [])
    shapes = [jax.ShapeDtypeStruct((rows, 8 * w), F32) for w in widths]
    if gain is not None:
        shapes.append(jax.ShapeDtypeStruct((rows, 1), F32))
    return pl.pallas_call(
        body,
        out_shape=shapes,
        in_specs=[SMEM_SPEC] + [VMEM_SPEC] * len(args),
        out_specs=[VMEM_SPEC] * len(shapes),
        cost_estimate=cost(0, 64 * rows * total),
        name="join_columns",
    )(scalar(index), *args)


def rope(x, cosine, sine):
    lane = lax.broadcasted_iota(jnp.int32, x.shape, 1)
    other = jnp.where(lane % HD < HD // 2, pltpu.roll(x, LANES - HD // 2, 1), pltpu.roll(x, HD // 2, 1))
    return x * cosine + other * sine


def head_masks(shape):
    lane = lax.broadcasted_iota(jnp.int32, shape, 1)
    return [lane < HD, lane >= HD]


def attend_body(place_ref, proj_ref, cos_ref, sin_ref, start_ref, saved_ref, mixed_ref, lse_ref, *, blocks, size):
    place = place_ref[0]

    def slot_rows(j):
        return pl.ds(pl.multiple_of((place ^ j) * size, size), size)

    for j in range(blocks):
        rows = slot_rows(j)
        here = slice(j * size, (j + 1) * size)
        cosine, sine = cos_ref[rows, :], sin_ref[rows, :]
        for p in range(2):
            value = proj_ref[rows, p * LANES : (p + 1) * LANES]
            saved_ref[here, p * LANES : (p + 1) * LANES] = rope(value, cosine, sine).astype(BF16)
        saved_ref[here, 2 * LANES :] = proj_ref[rows, 2 * LANES :].astype(BF16)
    for j in range(blocks):
        here = slice(j * size, (j + 1) * size)
        upto = (j + 1) * size
        query = saved_ref[here, :LANES]
        keys = saved_ref[:upto, LANES : 2 * LANES]
        values = saved_ref[:upto, 2 * LANES :]
        row = lax.broadcasted_iota(jnp.int32, (size, upto), 0) + j * size
        col = lax.broadcasted_iota(jnp.int32, (size, upto), 1)
        visible = (col <= row) & (col >= start_ref[slot_rows(j), :])
        q_heads = head_masks(query.shape)
        v_heads = head_masks(values.shape)
        mixed, totals = [], []
        for h in range(2):
            scores = dot_nt(jnp.where(q_heads[h], query, jnp.zeros_like(query)), keys) * SCALE
            scores = jnp.where(visible, scores, MASKED_SCORE)
            top = jnp.max(scores, axis=1, keepdims=True)
            weights = jnp.exp(scores - top)
            total = jnp.sum(weights, axis=1, keepdims=True)
            probs = (weights * (1.0 / total)).astype(BF16)
            mixed.append(dot_nn(probs, jnp.where(v_heads[h], values, jnp.zeros_like(values))))
            totals.append(jnp.broadcast_to(top + jnp.log(total), query.shape))
        mixed_ref[slot_rows(j), :] = (mixed[0] + mixed[1]).astype(BF16)
        lse_ref[here, :] = jnp.where(q_heads[0], totals[0], totals[1])


def attend_back_body(place_ref, saved_ref, lse_ref, grad_ref, cos_ref, sin_ref, start_ref, out_ref, dk_ref, dv_ref, *, blocks, size):
    place = place_ref[0]

    def slot_rows(j):
        return pl.ds(pl.multiple_of((place ^ j) * size, size), size)

    dk_ref[...] = jnp.zeros_like(dk_ref)
    dv_ref[...] = jnp.zeros_like(dv_ref)
    for j in range(blocks):
        here = slice(j * size, (j + 1) * size)
        upto = (j + 1) * size
        rows = slot_rows(j)
        query = saved_ref[here, :LANES]
        keys = saved_ref[:upto, LANES : 2 * LANES]
        values = saved_ref[:upto, 2 * LANES :]
        grad = grad_ref[rows, :]
        row = lax.broadcasted_iota(jnp.int32, (size, upto), 0) + j * size
        col = lax.broadcasted_iota(jnp.int32, (size, upto), 1)
        visible = (col <= row) & (col >= start_ref[rows, :])
        q_heads = head_masks(query.shape)
        k_heads = head_masks(keys.shape)
        dq = jnp.zeros(query.shape, F32)
        dk = jnp.zeros(keys.shape, F32)
        dv = jnp.zeros(keys.shape, F32)
        for h in range(2):
            q_head = jnp.where(q_heads[h], query, jnp.zeros_like(query))
            g_head = jnp.where(q_heads[h], grad, jnp.zeros_like(grad))
            scores = dot_nt(q_head, keys) * SCALE
            log_total = lse_ref[here, h * HD : h * HD + 1]
            probs = jnp.exp(jnp.where(visible, scores, MASKED_SCORE) - log_total)
            d_probs = dot_nt(g_head, values)
            inner = jnp.sum(probs * d_probs, axis=1, keepdims=True)
            d_scores = (probs * (d_probs - inner)).astype(BF16)
            dq += dot_nn(d_scores, jnp.where(k_heads[h], keys, jnp.zeros_like(keys)))
            dk += dot_tn(d_scores, q_head)
            dv += dot_tn(probs.astype(BF16), g_head)
        out_ref[rows, :LANES] = rope(dq * SCALE, cos_ref[rows, :], -sin_ref[rows, :]).astype(BF16)
        dk_ref[:upto, :] += dk
        dv_ref[:upto, :] += dv
    for j in range(blocks):
        here = slice(j * size, (j + 1) * size)
        rows = slot_rows(j)
        out_ref[rows, LANES : 2 * LANES] = rope(dk_ref[here, :] * SCALE, cos_ref[rows, :], -sin_ref[rows, :]).astype(BF16)
        out_ref[rows, 2 * LANES :] = dv_ref[here, :].astype(BF16)


def attention_specs(length, width):
    return pl.BlockSpec((length, width), lambda s, p, place: (s, p))


def table_specs(length, width):
    return pl.BlockSpec((length, width), lambda s, p, place: (s, 0))


def attend(proj, cosine, sine, start, place, size, length):
    tokens = proj.shape[0]
    pairs = proj.shape[1] // (3 * LANES)
    seqs = tokens // length
    body = functools.partial(attend_body, blocks=length // size, size=size)
    return pl.pallas_call(
        body,
        grid_spec=pltpu.PrefetchScalarGridSpec(
            num_scalar_prefetch=1,
            grid=(seqs, pairs),
            in_specs=[attention_specs(length, 3 * LANES), table_specs(length, LANES), table_specs(length, LANES), table_specs(length, 1)],
            out_specs=[attention_specs(length, 3 * LANES), attention_specs(length, LANES), attention_specs(length, LANES)],
        ),
        out_shape=[
            jax.ShapeDtypeStruct(proj.shape, BF16),
            jax.ShapeDtypeStruct((tokens, pairs * LANES), BF16),
            jax.ShapeDtypeStruct((tokens, pairs * LANES), F32),
        ],
        compiler_params=pltpu.CompilerParams(vmem_limit_bytes=48 * MIB),
        cost_estimate=cost(16 * tokens * length * pairs * LANES, 16 * tokens * pairs * LANES),
        name="attend",
    )(scalar(place), proj, cosine, sine, start)


def attend_back(saved, lse, grad, cosine, sine, start, place, size, length):
    tokens = saved.shape[0]
    pairs = saved.shape[1] // (3 * LANES)
    seqs = tokens // length
    body = functools.partial(attend_back_body, blocks=length // size, size=size)
    return pl.pallas_call(
        body,
        grid_spec=pltpu.PrefetchScalarGridSpec(
            num_scalar_prefetch=1,
            grid=(seqs, pairs),
            in_specs=[
                attention_specs(length, 3 * LANES),
                attention_specs(length, LANES),
                attention_specs(length, LANES),
                table_specs(length, LANES),
                table_specs(length, LANES),
                table_specs(length, 1),
            ],
            out_specs=attention_specs(length, 3 * LANES),
            scratch_shapes=[pltpu.VMEM((length, LANES), F32), pltpu.VMEM((length, LANES), F32)],
        ),
        out_shape=jax.ShapeDtypeStruct(saved.shape, BF16),
        compiler_params=pltpu.CompilerParams(vmem_limit_bytes=48 * MIB),
        cost_estimate=cost(40 * tokens * length * pairs * LANES, 16 * tokens * pairs * LANES),
        name="attend_back",
    )(scalar(place), saved, lse, grad, cosine, sine, start)


def rms_rows(values):
    factor = lax.rsqrt(jnp.mean(values * values, axis=-1, keepdims=True) + EPSILON)
    return values * factor, factor


def norm_input(inner, normed, factor):
    return factor * (inner - normed * jnp.mean(inner * normed, axis=-1, keepdims=True))


def rope_tables(positions):
    inverse_freq = 1.0 / ROPE_BASE ** (jnp.arange(0, HD, 2, dtype=F32) / HD)
    angles = positions.astype(F32)[:, None] * inverse_freq
    cosine, sine = jnp.cos(angles), jnp.sin(angles)
    return (
        jnp.concatenate([cosine] * 4, axis=1),
        jnp.concatenate([-sine, sine, -sine, sine], axis=1),
    )


ATTN = Group("y", "x", "zh", "zl")
MLP = Group("y", "x", "zh", "zl")


def local(tokens, positions, attn_gain, w_query, w_key, w_value, w_out, mlp_gain, w_gate, w_up, w_down, out_grad):
    own = tokens.shape[1]
    model = tokens.shape[2]
    length = own * lax.axis_size("x") * lax.axis_size("c")
    outer = lax.axis_size("r")
    shape = tokens.shape
    gain_one = attn_gain.astype(F32)[:, None]
    gain_two = mlp_gain.astype(F32)[:, None]
    attn_at = ATTN.index()
    mlp_at = MLP.index()
    place = lax.axis_index("x") * 2 + lax.axis_index("c")

    qkv_all = ATTN.gather_weight(split_columns([w_query, w_key, w_value], gain_one, attn_at))
    out_all = ATTN.gather_weight(split_columns([jnp.transpose(w_out)], None, attn_at))
    gate_all = MLP.gather_weight(split_columns([w_gate], gain_two, mlp_at))
    up_all = MLP.gather_weight(split_columns([w_up], gain_two, mlp_at))
    down_all = MLP.gather_weight(split_columns([jnp.transpose(w_down)], None, mlp_at))

    inputs = tokens.reshape(own, model).astype(F32)
    normed_one, factor_one = rms_rows(inputs)
    one_all = ATTN.gather_tokens(ATTN.to_slots(normed_one.astype(BF16), outer))
    where = positions.reshape(own, 1)
    for axis in ("c", "x", "y"):
        where = jnp.concatenate([where, swap(where, axis)], axis=0)
    where = where.reshape(-1)
    cosine, sine = rope_tables(where)
    slot = (jnp.arange(length, dtype=jnp.int32) // own) ^ place
    at = slot * own + jnp.arange(length, dtype=jnp.int32) % own
    start = (jnp.tile(at, where.shape[0] // length) - where)[:, None]
    saved, mixed, lse = attend(dot_nn(one_all, qkv_all), cosine, sine, start, place, own, length)
    pair = 2 * own

    def piece(array, i):
        return array[i * pair : (i + 1) * pair]

    attn_out = ATTN.scatter_tokens(lambda i: dot_nt(piece(mixed, i), out_all))
    first_sum = inputs + ATTN.from_slots(attn_out, outer)

    grad_rows = out_grad.reshape(own, model)
    dy_all = MLP.gather_tokens(MLP.to_slots(grad_rows, outer))
    normed_two, factor_two = rms_rows(first_sum)
    two_all = MLP.gather_tokens(MLP.to_slots(normed_two.astype(BF16), outer))
    gate = dot_nn(two_all, gate_all)
    up = dot_nn(two_all, up_all)
    sigmoid = jax.nn.sigmoid(gate)
    hidden = (gate * sigmoid * up).astype(BF16)
    down_blocks = MLP.scatter_weight(dy_all, hidden)
    d_hidden = dot_nn(dy_all, down_all)
    d_up = (d_hidden * gate * sigmoid).astype(BF16)
    d_gate = (d_hidden * up * sigmoid * (1.0 + gate * (1.0 - sigmoid))).astype(BF16)
    inner_two = MLP.scatter_tokens(lambda i: dot_nt(piece(d_gate, i), gate_all) + dot_nt(piece(d_up, i), up_all))
    mlp_out = MLP.scatter_tokens(lambda i: dot_nt(piece(hidden, i), down_all))
    block_out = (first_sum + MLP.from_slots(mlp_out, outer)).astype(BF16)
    gate_blocks = MLP.scatter_weight(two_all, d_gate)
    up_blocks = MLP.scatter_weight(two_all, d_up)

    d_first = grad_rows.astype(F32) + norm_input(MLP.from_slots(inner_two, outer), normed_two, factor_two)
    d_attn_all = ATTN.gather_tokens(ATTN.to_slots(d_first.astype(BF16), outer))
    d_mixed = dot_nn(d_attn_all, out_all).astype(BF16)
    out_blocks = ATTN.scatter_weight(d_attn_all, mixed)
    d_qkv = attend_back(saved, lse, d_mixed, cosine, sine, start, place, own, length)
    inner_one = ATTN.scatter_tokens(lambda i: dot_nt(piece(d_qkv, i), qkv_all))
    qkv_blocks = ATTN.scatter_weight(one_all, d_qkv)
    tokens_grad = d_first + norm_input(ATTN.from_slots(inner_one, outer), normed_one, factor_one)

    (down_grad,) = join_columns(down_blocks, None, None, mlp_at, 1)
    gate_grad, gain_gate = join_columns(gate_blocks, [w_gate], gain_two, mlp_at, 1)
    up_grad, gain_up = join_columns(up_blocks, [w_up], gain_two, mlp_at, 1)
    (out_w_grad,) = join_columns(out_blocks, None, None, attn_at, 1)
    q_grad, k_grad, v_grad, gain_attn = join_columns(qkv_blocks, [w_query, w_key, w_value], gain_one, attn_at, 3)
    return (
        block_out.reshape(shape),
        tokens_grad.astype(BF16).reshape(shape),
        gain_attn.reshape(-1),
        q_grad,
        k_grad,
        v_grad,
        jnp.transpose(out_w_grad),
        (gain_gate + gain_up).reshape(-1),
        gate_grad,
        up_grad,
        jnp.transpose(down_grad),
    )


def solution(mesh):
    fsdp = mesh.shape["fsdp"]
    sizes = (fsdp // 8, 2, 2, 2, mesh.shape["ctx"] // 2, 2)
    fine = Mesh(mesh.devices.reshape(sizes), AXES)
    rows, cols = AXES[:4], AXES[4:]
    tokens, places, vector = P(rows, cols, None), P(rows, cols), P(AXES)
    first, second = P(AXES, None), P(None, AXES)
    in_specs = (tokens, places, vector, first, first, first, second, vector, first, first, second, tokens)
    out_specs = (tokens, tokens, vector, first, first, first, second, vector, first, first, second)
    return jax.shard_map(local, mesh=fine, in_specs=in_specs, out_specs=out_specs, check_vma=False)
```

```python
import functools

import jax
import jax.numpy as jnp
from jax import lax
from jax.experimental import pallas as pl
from jax.experimental.pallas import tpu as pltpu
from jax.sharding import Mesh
from jax.sharding import PartitionSpec as P

H = 32
HD = 64
EPSILON = 1e-05
ROPE_BASE = 130000.0
MASKED_SCORE = -1e30
SCALE = HD ** (-0.5)
LANES = 128
MIB = 1 << 20
BF16 = jnp.bfloat16
F32 = jnp.float32
AXES = ("r", "zh", "zl", "y", "x", "c")
NT = (((1,), (1,)), ((), ()))
TN = (((0,), (0,)), ((), ()))


def dot_nn(a, b):
    return jnp.dot(a, b, preferred_element_type=F32)


def dot_nt(a, b):
    return lax.dot_general(a, b, NT, preferred_element_type=F32)


def dot_tn(a, b):
    return lax.dot_general(a, b, TN, preferred_element_type=F32)


def flip(x, axes, masks):
    return lax.ppermute(x, axes, [(i, i ^ masks[i & 1]) for i in range(8)])


def swap(x, axis):
    return lax.ppermute(x, axis, [(0, 1), (1, 0)])


PLACES = ((0, 1, 2, 3, 5, 4, 6, 7), (0, 1, 4, 5, 3, 2, 6, 7))


class Group:
    def __init__(self, d1, d2, half, spread):
        self.axes = (d1, d2, "c")
        self.half, self.spread = half, spread

    def column_order(self, outer):
        names = ("r", "zh", "zl", "y", "x")
        sizes = dict(zip(names, (outer, 2, 2, 2, 2)))
        sequence = ([self.half] if self.half else []) + list(self.spread) + list(self.axes[:2])
        order = [0]
        for name in sequence:
            step = 1
            for later in names[names.index(name) + 1 :]:
                step *= sizes[later]
            order = [base + step * i for base in order for i in range(sizes[name])]
        return order

    def reorder(self, x, order):
        if order == list(range(len(order))):
            return x
        width = x.shape[1] // len(order)
        return jnp.concatenate([x[:, i * width : (i + 1) * width] for i in order], axis=1)

    def flip_halves(self, x):
        if not self.half:
            return x
        width = x.shape[1] // 2
        at = lax.axis_index(self.half)
        first = lax.dynamic_slice_in_dim(x, at * width, width, axis=1)
        return jnp.concatenate([first, lax.dynamic_slice_in_dim(x, (1 - at) * width, width, axis=1)], axis=1)

    def to_slots(self, x, outer):
        return self.flip_halves(self.reorder(x, self.column_order(outer)))

    def from_slots(self, x, outer):
        order = self.column_order(outer)
        return self.reorder(self.flip_halves(x), [order.index(i) for i in range(len(order))])

    def other_core(self, x):
        return flip(x, self.axes, (1, 1))

    def near(self, x):
        return flip(x, self.axes, (2, 4))

    def far(self, x):
        return flip(x, self.axes, (4, 2))

    def gather_tokens(self, x):
        partner = self.other_core(x)
        near_one = self.near(x)
        near_two = self.near(partner)
        far_one = self.far(near_one)
        parts = [x, partner, near_one, near_two, self.other_core(near_one), self.other_core(near_two)]
        return jnp.concatenate(parts + [far_one, self.other_core(far_one)], axis=0)

    def scatter_tokens(self, partial):
        def cut(whole):
            size = whole.shape[0] // 2
            return whole[:size], whole[size:]

        six, seven = cut(partial(6, 8))
        six = six + self.other_core(seven.astype(BF16)).astype(F32)
        far_one = self.far(six.astype(BF16)).astype(F32)
        four, five = cut(partial(4, 6))
        four = self.other_core(four.astype(BF16)).astype(F32)
        five = self.other_core(five.astype(BF16)).astype(F32)
        two, three = cut(partial(2, 4))
        near_two = self.near((three + five).astype(BF16)).astype(F32)
        near_one = self.near((two + four + far_one).astype(BF16)).astype(F32)
        zero, one = cut(partial(0, 2))
        partner = self.other_core((one + near_two).astype(BF16)).astype(F32)
        return zero + near_one + partner

    def share_columns(self, weight):
        return lax.all_to_all(weight, self.axes, split_axis=1, concat_axis=0, tiled=True)

    def gather_weight(self, rows):
        rows = lax.all_gather(rows, self.spread, axis=0, tiled=True)
        if self.half:
            rows = jnp.concatenate([rows, swap(rows, self.half)], axis=0)
        return rows

    def scatter_weight(self, left, right):
        if self.half:
            width = left.shape[1] // 2
            away = swap(dot_tn(left[:, width:], right).astype(BF16), self.half)
            grad = (dot_tn(left[:, :width], right) + away.astype(F32)).astype(BF16)
        else:
            grad = dot_tn(left, right).astype(BF16)
        return lax.psum_scatter(grad, self.spread, scatter_dimension=0, tiled=True)

    def return_columns(self, grad):
        return lax.all_to_all(grad, self.axes, split_axis=0, concat_axis=1, tiled=True)


def scalars(values):
    return jnp.stack(values).astype(jnp.int32)


VMEM_SPEC = pl.BlockSpec(memory_space=pltpu.VMEM)


def cost(flops, moved):
    return pl.CostEstimate(flops=flops, bytes_accessed=moved, transcendentals=0)


def parts_of(width, count, unit):
    out = []
    at = 0
    for device in range(8):
        for p in range(width // unit):
            for i in range(count):
                out.append((i, device * width + p * unit, at))
                at += unit
    return out


def mix_columns(weights, gain, unit):
    rows, width = weights[0].shape[0], weights[0].shape[1] // 8
    parts = parts_of(width, len(weights), unit)

    def body(gain_ref, *refs):
        factor = gain_ref[...]
        for i, source, at in parts:
            refs[-1][:, at : at + unit] = (refs[i][:, source : source + unit].astype(F32) * factor).astype(BF16)

    total = 8 * width * len(weights)
    return pl.pallas_call(
        body,
        out_shape=jax.ShapeDtypeStruct((rows, total), BF16),
        in_specs=[VMEM_SPEC] * (1 + len(weights)),
        out_specs=VMEM_SPEC,
        cost_estimate=cost(rows * total, 4 * rows * total),
        name="mix_columns",
    )(gain, *weights)


def part_columns(mixed, weights, gain, unit):
    count = len(weights)
    rows, width = weights[0].shape[0], weights[0].shape[1] // 8
    parts = parts_of(width, count, unit)

    def body(mixed_ref, gain_ref, *refs):
        ins, outs = refs[:count], refs[count:-1]
        factor = gain_ref[...]
        acc = jnp.zeros((rows, LANES), F32)
        for i, source, at in parts:
            value = mixed_ref[:, at : at + unit].astype(F32)
            term = ins[i][:, source : source + unit].astype(F32) * value
            for p in range(unit // LANES):
                acc = acc + term[:, p * LANES : (p + 1) * LANES]
            outs[i][:, source : source + unit] = value * factor
        refs[-1][...] = jnp.sum(acc, axis=1, keepdims=True)

    return pl.pallas_call(
        body,
        out_shape=[jax.ShapeDtypeStruct(w.shape, F32) for w in weights] + [jax.ShapeDtypeStruct((rows, 1), F32)],
        in_specs=[VMEM_SPEC] * (2 + count),
        out_specs=[VMEM_SPEC] * (count + 1),
        cost_estimate=cost(4 * rows * width * 8 * count, 8 * rows * width * 8 * count),
        name="part_columns",
    )(mixed, gain, *weights)


def rope(x, cosine, sine):
    lane = lax.broadcasted_iota(jnp.int32, x.shape, 1)
    other = jnp.where(lane % HD < HD // 2, pltpu.roll(x, LANES - HD // 2, 1), pltpu.roll(x, HD // 2, 1))
    return x * cosine + other * sine


def head_masks(shape):
    lane = lax.broadcasted_iota(jnp.int32, shape, 1)
    return [lane < HD, lane >= HD]


def attend_body(place_ref, proj_ref, cos_ref, sin_ref, start_ref, saved_ref, mixed_ref, lse_ref, *, blocks, size):
    base = pl.program_id(1) * blocks

    def slot_rows(j):
        return pl.ds(pl.multiple_of(place_ref[base + j] * size, size), size)

    for j in range(blocks):
        rows = slot_rows(j)
        here = slice(j * size, (j + 1) * size)
        cosine, sine = cos_ref[rows, :], sin_ref[rows, :]
        for p in range(2):
            value = proj_ref[rows, p * LANES : (p + 1) * LANES]
            saved_ref[here, p * LANES : (p + 1) * LANES] = rope(value, cosine, sine).astype(BF16)
        saved_ref[here, 2 * LANES :] = proj_ref[rows, 2 * LANES :].astype(BF16)
    for j in range(blocks):
        here = slice(j * size, (j + 1) * size)
        upto = (j + 1) * size
        query = saved_ref[here, :LANES]
        keys = saved_ref[:upto, LANES : 2 * LANES]
        values = saved_ref[:upto, 2 * LANES :]
        row = lax.broadcasted_iota(jnp.int32, (size, upto), 0) + j * size
        col = lax.broadcasted_iota(jnp.int32, (size, upto), 1)
        visible = (col <= row) & (col >= start_ref[slot_rows(j), :])
        q_heads = head_masks(query.shape)
        v_heads = head_masks(values.shape)
        mixed, totals = [], []
        for h in range(2):
            scores = dot_nt(jnp.where(q_heads[h], query, jnp.zeros_like(query)), keys) * SCALE
            scores = jnp.where(visible, scores, MASKED_SCORE)
            top = jnp.max(scores, axis=1, keepdims=True)
            weights = jnp.exp(scores - top)
            total = jnp.sum(weights, axis=1, keepdims=True)
            probs = (weights * (1.0 / total)).astype(BF16)
            mixed.append(dot_nn(probs, jnp.where(v_heads[h], values, jnp.zeros_like(values))))
            totals.append(jnp.broadcast_to(top + jnp.log(total), query.shape))
        mixed_ref[slot_rows(j), :] = (mixed[0] + mixed[1]).astype(BF16)
        lse_ref[here, :] = jnp.where(q_heads[0], totals[0], totals[1])


def attend_back_body(place_ref, saved_ref, lse_ref, grad_ref, cos_ref, sin_ref, start_ref, out_ref, dk_ref, dv_ref, *, blocks, size):
    base = pl.program_id(1) * blocks

    def slot_rows(j):
        return pl.ds(pl.multiple_of(place_ref[base + j] * size, size), size)

    dk_ref[...] = jnp.zeros_like(dk_ref)
    dv_ref[...] = jnp.zeros_like(dv_ref)
    for j in range(blocks):
        here = slice(j * size, (j + 1) * size)
        upto = (j + 1) * size
        rows = slot_rows(j)
        query = saved_ref[here, :LANES]
        keys = saved_ref[:upto, LANES : 2 * LANES]
        values = saved_ref[:upto, 2 * LANES :]
        grad = grad_ref[rows, :]
        row = lax.broadcasted_iota(jnp.int32, (size, upto), 0) + j * size
        col = lax.broadcasted_iota(jnp.int32, (size, upto), 1)
        visible = (col <= row) & (col >= start_ref[rows, :])
        q_heads = head_masks(query.shape)
        k_heads = head_masks(keys.shape)
        dq = jnp.zeros(query.shape, F32)
        dk = jnp.zeros(keys.shape, F32)
        dv = jnp.zeros(keys.shape, F32)
        for h in range(2):
            q_head = jnp.where(q_heads[h], query, jnp.zeros_like(query))
            g_head = jnp.where(q_heads[h], grad, jnp.zeros_like(grad))
            scores = dot_nt(q_head, keys) * SCALE
            log_total = lse_ref[here, h * HD : h * HD + 1]
            probs = jnp.exp(jnp.where(visible, scores, MASKED_SCORE) - log_total)
            d_probs = dot_nt(g_head, values)
            inner = jnp.sum(probs * d_probs, axis=1, keepdims=True)
            d_scores = (probs * (d_probs - inner)).astype(BF16)
            dq += dot_nn(d_scores, jnp.where(k_heads[h], keys, jnp.zeros_like(keys)))
            dk += dot_tn(d_scores, q_head)
            dv += dot_tn(probs.astype(BF16), g_head)
        out_ref[rows, :LANES] = rope(dq * SCALE, cos_ref[rows, :], -sin_ref[rows, :]).astype(BF16)
        dk_ref[:upto, :] += dk
        dv_ref[:upto, :] += dv
    for j in range(blocks):
        here = slice(j * size, (j + 1) * size)
        rows = slot_rows(j)
        out_ref[rows, LANES : 2 * LANES] = rope(dk_ref[here, :] * SCALE, cos_ref[rows, :], -sin_ref[rows, :]).astype(BF16)
        out_ref[rows, 2 * LANES :] = dv_ref[here, :].astype(BF16)


def by_pair(tokens, width):
    return pl.BlockSpec((tokens, width), lambda p, s, places: (0, p))


def by_sequence(length, width):
    return pl.BlockSpec((length, width), lambda p, s, places: (s, p))


def table(tokens, width):
    return pl.BlockSpec((tokens, width), lambda p, s, places: (0, 0))


def attend(proj, cosine, sine, start, places, size, length):
    tokens = proj.shape[0]
    pairs = proj.shape[1] // (3 * LANES)
    body = functools.partial(attend_body, blocks=length // size, size=size)
    return pl.pallas_call(
        body,
        grid_spec=pltpu.PrefetchScalarGridSpec(
            num_scalar_prefetch=1,
            grid=(pairs, tokens // length),
            in_specs=[by_pair(tokens, 3 * LANES), table(tokens, LANES), table(tokens, LANES), table(tokens, 1)],
            out_specs=[by_sequence(length, 3 * LANES), by_pair(tokens, LANES), by_sequence(length, LANES)],
        ),
        out_shape=[
            jax.ShapeDtypeStruct(proj.shape, BF16),
            jax.ShapeDtypeStruct((tokens, pairs * LANES), BF16),
            jax.ShapeDtypeStruct((tokens, pairs * LANES), F32),
        ],
        compiler_params=pltpu.CompilerParams(vmem_limit_bytes=48 * MIB),
        cost_estimate=cost(16 * tokens * length * pairs * LANES, 16 * tokens * pairs * LANES),
        name="attend",
    )(places, proj, cosine, sine, start)


def attend_back(saved, lse, grad, cosine, sine, start, places, size, length):
    tokens = saved.shape[0]
    pairs = saved.shape[1] // (3 * LANES)
    body = functools.partial(attend_back_body, blocks=length // size, size=size)
    return pl.pallas_call(
        body,
        grid_spec=pltpu.PrefetchScalarGridSpec(
            num_scalar_prefetch=1,
            grid=(pairs, tokens // length),
            in_specs=[
                by_sequence(length, 3 * LANES),
                by_sequence(length, LANES),
                by_pair(tokens, LANES),
                table(tokens, LANES),
                table(tokens, LANES),
                table(tokens, 1),
            ],
            out_specs=by_pair(tokens, 3 * LANES),
            scratch_shapes=[pltpu.VMEM((length, LANES), F32), pltpu.VMEM((length, LANES), F32)],
        ),
        out_shape=jax.ShapeDtypeStruct(saved.shape, BF16),
        compiler_params=pltpu.CompilerParams(vmem_limit_bytes=48 * MIB),
        cost_estimate=cost(40 * tokens * length * pairs * LANES, 16 * tokens * pairs * LANES),
        name="attend_back",
    )(places, saved, lse, grad, cosine, sine, start)


def rms_rows(values):
    factor = lax.rsqrt(jnp.mean(values * values, axis=-1, keepdims=True) + EPSILON)
    return values * factor, factor


def norm_input(inner, normed, factor):
    return factor * (inner - normed * jnp.mean(inner * normed, axis=-1, keepdims=True))


def rope_tables(positions):
    inverse_freq = 1.0 / ROPE_BASE ** (jnp.arange(0, HD, 2, dtype=F32) / HD)
    angles = positions.astype(F32)[:, None] * inverse_freq
    cosine, sine = jnp.cos(angles), jnp.sin(angles)
    return (
        jnp.concatenate([cosine] * 4, axis=1),
        jnp.concatenate([-sine, sine, -sine, sine], axis=1),
    )


ATTN = Group("y", "x", None, ("r", "zh", "zl"))
MLP = Group("zl", "y", "x", ("r", "zh"))


def local(tokens, positions, attn_gain, w_query, w_key, w_value, w_out, mlp_gain, w_gate, w_up, w_down, out_grad):
    own = tokens.shape[1]
    model = tokens.shape[2]
    length = own * lax.axis_size("x") * lax.axis_size("c")
    outer = lax.axis_size("r")
    shape = tokens.shape
    gain_one = attn_gain.astype(F32)[:, None]
    gain_two = mlp_gain.astype(F32)[:, None]
    slice_width = w_gate.shape[1] // 8

    qkv_rows = ATTN.share_columns(mix_columns([w_query, w_key, w_value], gain_one, LANES))
    out_rows = ATTN.share_columns(jnp.transpose(w_out))
    gate_up_rows = MLP.share_columns(mix_columns([w_gate, w_up], gain_two, slice_width))
    down_rows = MLP.share_columns(jnp.transpose(w_down))
    qkv_all = ATTN.gather_weight(qkv_rows)
    out_all = ATTN.gather_weight(out_rows)
    gate_up_all = MLP.gather_weight(gate_up_rows)
    down_all = MLP.gather_weight(down_rows)

    inputs = tokens.reshape(own, model).astype(F32)
    normed_one, factor_one = rms_rows(inputs)
    one_all = ATTN.gather_tokens(ATTN.to_slots(normed_one.astype(BF16), outer))
    where = ATTN.gather_tokens(positions.reshape(own, 1)).reshape(-1)
    cosine, sine = rope_tables(where)
    place = lax.axis_index("x") * 2 + lax.axis_index("c")
    core = lax.axis_index("c")
    order = [jnp.where(core == 0, PLACES[0][i], PLACES[1][i]) for i in range(8)]
    slot_part = [jnp.where(core == 0, PLACES[0].index(i), PLACES[1].index(i)) for i in range(8)]
    parts = scalars(slot_part)
    places = parts[scalars([s * 4 + (j ^ place) for s in range(2) for j in range(4)])]
    first_row = (scalars(order) % 4 ^ place) * own
    start = (jnp.repeat(first_row, own) + jnp.tile(jnp.arange(own, dtype=jnp.int32), 8) - where)[:, None]
    proj = dot_nn(one_all, qkv_all)
    saved, mixed, lse = attend(proj, cosine, sine, start, places, own, length)

    def rows_of(array, begin, end):
        return array[begin * own : end * own]

    attn_out = ATTN.scatter_tokens(lambda i, j: dot_nt(rows_of(mixed, i, j), out_all))
    first_sum = inputs + ATTN.from_slots(attn_out, outer)

    grad_rows = out_grad.reshape(own, model)
    dy_all = MLP.gather_tokens(MLP.to_slots(grad_rows, outer))
    normed_two, factor_two = rms_rows(first_sum)
    two_all = MLP.gather_tokens(MLP.to_slots(normed_two.astype(BF16), outer))
    gate_up = dot_nn(two_all, gate_up_all)
    gate, up = gate_up[:, :slice_width], gate_up[:, slice_width:]
    sigmoid = jax.nn.sigmoid(gate)
    hidden = (gate * sigmoid * up).astype(BF16)
    down_grad = MLP.scatter_weight(dy_all, hidden)
    d_hidden = dot_nn(dy_all, down_all)
    d_up = (d_hidden * gate * sigmoid).astype(BF16)
    d_gate = (d_hidden * up * sigmoid * (1.0 + gate * (1.0 - sigmoid))).astype(BF16)
    d_gate_up = jnp.concatenate([d_gate, d_up], axis=1)
    inner_two = MLP.scatter_tokens(lambda i, j: dot_nt(rows_of(d_gate_up, i, j), gate_up_all))
    mlp_out = MLP.scatter_tokens(lambda i, j: dot_nt(rows_of(hidden, i, j), down_all))
    block_out = (first_sum + MLP.from_slots(mlp_out, outer)).astype(BF16)
    gate_up_grad = MLP.scatter_weight(two_all, d_gate_up)

    d_first = grad_rows.astype(F32) + norm_input(MLP.from_slots(inner_two, outer), normed_two, factor_two)
    d_attn_all = ATTN.gather_tokens(ATTN.to_slots(d_first.astype(BF16), outer))
    d_mixed = dot_nn(d_attn_all, out_all).astype(BF16)
    out_grad_rows = ATTN.scatter_weight(d_attn_all, mixed)
    d_qkv = attend_back(saved, lse, d_mixed, cosine, sine, start, places, own, length)
    inner_one = ATTN.scatter_tokens(lambda i, j: dot_nt(rows_of(d_qkv, i, j), qkv_all))
    qkv_grad = ATTN.scatter_weight(one_all, d_qkv)
    tokens_grad = d_first + norm_input(ATTN.from_slots(inner_one, outer), normed_one, factor_one)

    down_w = MLP.return_columns(down_grad)
    out_w = ATTN.return_columns(out_grad_rows)
    gate_w, up_w, gain_mlp = part_columns(MLP.return_columns(gate_up_grad), [w_gate, w_up], gain_two, slice_width)
    query_w, key_w, value_w, gain_attn = part_columns(ATTN.return_columns(qkv_grad), [w_query, w_key, w_value], gain_one, LANES)
    return (
        block_out.reshape(shape),
        tokens_grad.astype(BF16).reshape(shape),
        gain_attn.reshape(-1),
        query_w,
        key_w,
        value_w,
        jnp.transpose(out_w.astype(F32)),
        gain_mlp.reshape(-1),
        gate_w,
        up_w,
        jnp.transpose(down_w.astype(F32)),
    )


def solution(mesh):
    fsdp = mesh.shape["fsdp"]
    sizes = (fsdp // 8, 2, 2, 2, mesh.shape["ctx"] // 2, 2)
    fine = Mesh(mesh.devices.reshape(sizes), AXES)
    rows, cols = AXES[:4], AXES[4:]
    tokens, places, vector = P(rows, cols, None), P(rows, cols), P(AXES)
    first, second = P(AXES, None), P(None, AXES)
    in_specs = (tokens, places, vector, first, first, first, second, vector, first, first, second, tokens)
    out_specs = (tokens, tokens, vector, first, first, first, second, vector, first, first, second)
    return jax.shard_map(local, mesh=fine, in_specs=in_specs, out_specs=out_specs, check_vma=False)
```

```python
import functools

import jax
import jax.numpy as jnp
from jax import lax
from jax.experimental import pallas as pl
from jax.experimental.pallas import tpu as pltpu
from jax.sharding import Mesh
from jax.sharding import PartitionSpec as P

H = 32
HD = 64
EPSILON = 1e-05
ROPE_BASE = 130000.0
MASKED_SCORE = -1e30
SCALE = HD ** (-0.5)
LANES = 128
MIB = 1 << 20
BF16 = jnp.bfloat16
F32 = jnp.float32
AXES = ("r", "zh", "zl", "y", "x", "c")
NT = (((1,), (1,)), ((), ()))
TN = (((0,), (0,)), ((), ()))


def dot_nn(a, b):
    return jnp.dot(a, b, preferred_element_type=F32)


def dot_nt(a, b):
    return lax.dot_general(a, b, NT, preferred_element_type=F32)


def dot_tn(a, b):
    return lax.dot_general(a, b, TN, preferred_element_type=F32)


def flip(x, axes, masks):
    return lax.ppermute(x, axes, [(i, i ^ masks[i & 1]) for i in range(8)])


def swap(x, axis):
    return lax.ppermute(x, axis, [(0, 1), (1, 0)])


def after(x, *others):
    return lax.optimization_barrier((x,) + others)[0]


PLACES = ((0, 1, 2, 3, 5, 4, 6, 7), (0, 1, 4, 5, 3, 2, 6, 7))


class Group:
    def __init__(self, d1, d2, half, spread):
        self.axes = (d1, d2, "c")
        self.half, self.spread = half, spread

    def column_order(self, outer):
        names = ("r", "zh", "zl", "y", "x")
        sizes = dict(zip(names, (outer, 2, 2, 2, 2)))
        sequence = ([self.half] if self.half else []) + list(self.spread) + list(self.axes[:2])
        order = [0]
        for name in sequence:
            step = 1
            for later in names[names.index(name) + 1 :]:
                step *= sizes[later]
            order = [base + step * i for base in order for i in range(sizes[name])]
        return order

    def reorder(self, x, order):
        if order == list(range(len(order))):
            return x
        width = x.shape[1] // len(order)
        return jnp.concatenate([x[:, i * width : (i + 1) * width] for i in order], axis=1)

    def flip_halves(self, x):
        if not self.half:
            return x
        width = x.shape[1] // 2
        at = lax.axis_index(self.half)
        first = lax.dynamic_slice_in_dim(x, at * width, width, axis=1)
        return jnp.concatenate([first, lax.dynamic_slice_in_dim(x, (1 - at) * width, width, axis=1)], axis=1)

    def to_slots(self, x, outer):
        return self.flip_halves(self.reorder(x, self.column_order(outer)))

    def from_slots(self, x, outer):
        order = self.column_order(outer)
        return self.reorder(self.flip_halves(x), [order.index(i) for i in range(len(order))])

    def other_core(self, x):
        return flip(x, self.axes, (1, 1))

    def near(self, x):
        return flip(x, self.axes, (2, 4))

    def far(self, x):
        return flip(x, self.axes, (4, 2))

    def gather_tokens(self, x):
        partner = self.other_core(x)
        near_one = self.near(x)
        near_two = self.near(partner)
        far_one = self.far(near_one)
        parts = [x, partner, near_one, near_two, self.other_core(near_one), self.other_core(near_two)]
        return parts + [far_one, self.other_core(far_one)]

    def scatter_begin(self, array, weights, at=0):
        six, seven = rows_product(array, weights, 6, (F32, BF16), at)
        four, five = rows_product(array, weights, 4, (BF16, BF16), at)
        six = six + self.other_core(seven).astype(F32)
        far_one = self.far(six.astype(BF16)).astype(F32)
        array = after(array, six)
        two, three = rows_product(array, weights, 2, (F32, F32), at)
        zero, one = rows_product(array, weights, 0, (F32, F32), at)
        three = (three + self.other_core(five).astype(F32)).astype(BF16)
        two = (two + self.other_core(four).astype(F32) + far_one).astype(BF16)
        return after((zero, one), two, three) + (two, three)

    def scatter_end(self, sums):
        zero, one, two, three = sums
        partner = self.other_core((one + self.near(three).astype(F32)).astype(BF16))
        return zero + self.near(two).astype(F32) + partner.astype(F32)

    def scatter_tokens(self, array, weights, at=0):
        return self.scatter_end(self.scatter_begin(array, weights, at))

    def share_columns(self, weight):
        return lax.all_to_all(weight, self.axes, split_axis=1, concat_axis=0, tiled=True)

    def gather_weight(self, rows):
        rows = lax.all_gather(rows, self.spread, axis=0, tiled=True)
        return [rows, swap(rows, self.half)] if self.half else [rows]

    def weight_terms(self, parts, right):
        if self.half:
            away = swap(parts_product(parts, right, 1, 2, None), self.half)
            return parts_product(parts, right, 0, 2, away)
        return parts_product(parts, right, 0, 1, None)

    def scatter_weight(self, terms):
        return lax.psum_scatter(terms, self.spread, scatter_dimension=0, tiled=True)

    def return_columns(self, grad):
        return lax.all_to_all(grad, self.axes, split_axis=0, concat_axis=1, tiled=True)


def scalars(values):
    return jnp.stack(values).astype(jnp.int32)


VMEM_SPEC = pl.BlockSpec(memory_space=pltpu.VMEM)


SMALL = pl.CostEstimate(flops=1024, bytes_accessed=1024, transcendentals=0)


def vmem(limit):
    return pltpu.CompilerParams(vmem_limit_bytes=limit * MIB)


def parts_of(widths, tails, unit):
    out = []
    at = 0
    for device in range(8):
        for p in range(widths[0] // unit):
            for i, width in enumerate(widths):
                out.append((i, device * width + p * unit, unit, at))
                at += unit
        for i, width in enumerate(tails):
            out.append((len(widths) + i, device * width, width, at))
            at += width
    return out


def mix_columns(weights, gain, unit, tails=()):
    arrays = list(weights) + list(tails)
    rows = arrays[0].shape[0]
    parts = parts_of([w.shape[1] // 8 for w in weights], [w.shape[1] // 8 for w in tails], unit)

    def body(gain_ref, *refs):
        factor = gain_ref[...]
        for i, source, width, at in parts:
            value = refs[i][:, source : source + width]
            if i < len(weights):
                value = (value.astype(F32) * factor).astype(BF16)
            refs[-1][:, at : at + width] = value

    return pl.pallas_call(
        body,
        out_shape=jax.ShapeDtypeStruct((rows, sum(w.shape[1] for w in arrays)), BF16),
        in_specs=[VMEM_SPEC] * (1 + len(arrays)),
        out_specs=VMEM_SPEC,
        cost_estimate=SMALL,
        name="mix_columns",
    )(gain, *arrays)


def part_columns(mixed, weights, gain, unit, tail=None):
    count = len(weights)
    rows = weights[0].shape[0]
    tails = [] if tail is None else [tail]
    parts = parts_of([w.shape[1] // 8 for w in weights], [w // 8 for w in tails], unit)

    def body(mixed_ref, gain_ref, *refs):
        ins, outs = refs[:count], refs[count:-1]
        factor = gain_ref[...]
        acc = jnp.zeros((rows, LANES), F32)
        for i, source, width, at in parts:
            value = mixed_ref[:, at : at + width].astype(F32)
            if i < count:
                term = ins[i][:, source : source + width].astype(F32) * value
                for p in range(width // LANES):
                    acc = acc + term[:, p * LANES : (p + 1) * LANES]
                value = value * factor
            outs[i][:, source : source + width] = value
        refs[-1][...] = jnp.sum(acc, axis=1, keepdims=True)

    shapes = [w.shape for w in weights] + [(rows, w) for w in tails] + [(rows, 1)]
    return pl.pallas_call(
        body,
        out_shape=[jax.ShapeDtypeStruct(shape, F32) for shape in shapes],
        in_specs=[VMEM_SPEC] * (2 + count),
        out_specs=[VMEM_SPEC] * len(shapes),
        cost_estimate=SMALL,
        name="part_columns",
    )(mixed, gain, *weights)


def rows_product(array, weights, first, types, at):
    size = array.shape[0] // 8
    depth = array.shape[1]
    count = len(weights)
    each = weights[0].shape[0]
    step = min(512, each)
    inner = each // step

    def body(array_ref, *refs):
        at = pl.program_id(0) // inner
        for i in range(count):

            @pl.when(at == i)
            def _():
                both = dot_nt(array_ref[...], refs[i][...])
                refs[count][...] = both[:size].astype(types[0])
                refs[count + 1][...] = both[size:].astype(types[1])

    def weight_spec(i):
        return pl.BlockSpec((step, depth), lambda j: (jnp.clip(j - i * inner, 0, inner - 1), at))

    return pl.pallas_call(
        body,
        grid=(count * inner,),
        out_shape=[jax.ShapeDtypeStruct((size, count * each), t) for t in types],
        in_specs=[pl.BlockSpec((2 * size, depth), lambda j: (first // 2, 0))] + [weight_spec(i) for i in range(count)],
        out_specs=[pl.BlockSpec((size, step), lambda j: (0, j))] * 2,
        compiler_params=vmem(40),
        cost_estimate=SMALL,
        name="rows_product",
    )(array, *weights)


def parts_product(parts, right, which, pieces, added):
    size = parts[0].shape[0]
    tokens, width = right.shape
    model = parts[0].shape[1] // pieces
    step = 512 if width <= 1024 else 256
    offset = which * (model // step)

    def body(*refs):
        ins, right_ref = refs[:8], refs[8]
        out_ref, stacked = refs[-2], refs[-1]
        for p in range(8):
            stacked[p * size : (p + 1) * size, :] = ins[p][...]
        total = dot_tn(stacked[...], right_ref[...])
        if added is not None:
            total = total + refs[9][...].astype(F32)
        out_ref[...] = total.astype(BF16)

    block = pl.BlockSpec((step, width), lambda j: (j, 0))
    return pl.pallas_call(
        body,
        grid=(model // step,),
        out_shape=jax.ShapeDtypeStruct((model, width), BF16),
        in_specs=[pl.BlockSpec((size, step), lambda j: (0, offset + j))] * 8
        + [pl.BlockSpec((tokens, width), lambda j: (0, 0))]
        + ([block] if added is not None else []),
        out_specs=block,
        scratch_shapes=[pltpu.VMEM((tokens, step), BF16)],
        compiler_params=vmem(48),
        cost_estimate=SMALL,
        name="parts_product",
    )(*parts, right, *([added] if added is not None else []))


def attention_terms(first, right, second, other):
    size, model = first[0].shape
    tokens, width = right.shape
    rest = other.shape[1]
    step = 512

    def body(*refs):
        right_ref, other_ref, out_ref, stacked = refs[16:]
        stack_parts(refs[:8], stacked)
        out_ref[:, :width] = dot_tn(stacked[...], right_ref[...]).astype(BF16)
        stack_parts(refs[8:16], stacked)
        out_ref[:, width:] = dot_tn(stacked[...], other_ref[...]).astype(BF16)

    return pl.pallas_call(
        body,
        grid=(model // step,),
        out_shape=jax.ShapeDtypeStruct((model, width + rest), BF16),
        in_specs=[pl.BlockSpec((size, step), lambda j: (0, j))] * 16 + [whole(right), whole(other)],
        out_specs=pl.BlockSpec((step, width + rest), lambda j: (j, 0)),
        scratch_shapes=[pltpu.VMEM((tokens, step), BF16)],
        compiler_params=vmem(48),
        cost_estimate=SMALL,
        name="attention_terms",
    )(*first, *second, right, other)


UNIT = 256
CHUNK = 512


def whole(part):
    return pl.BlockSpec(part.shape, lambda *at: (0, 0))


def stack_parts(ins, stacked):
    size = ins[0].shape[0]
    for p in range(8):
        stacked[p * size : (p + 1) * size, :] = ins[p][...]


def split_product(stacked, rows, weights):
    depth = weights[0].shape[0]
    total = dot_nn(stacked[rows, :depth], weights[0][...])
    for i in range(1, len(weights)):
        total += dot_nn(stacked[rows, i * depth : (i + 1) * depth], weights[i][...])
    return total


def feed_forward(parts, weights):
    size, model = parts[0].shape
    tokens = 8 * size
    width = weights[0].shape[1]
    count = len(weights)

    def body(*refs):
        ins, ws = refs[:8], refs[8 : 8 + count]
        hidden_ref, slope_ref, stacked = refs[8 + count :]

        @pl.when(pl.program_id(0) == 0)
        def _():
            stack_parts(ins, stacked)

        @pl.loop(0, tokens // CHUNK)
        def _(i):
            rows = pl.ds(pl.multiple_of(i * CHUNK, CHUNK), CHUNK)
            both = split_product(stacked, rows, ws)
            gate, up = both[:, :UNIT], both[:, UNIT:]
            sigmoid = 1.0 / (1.0 + jnp.exp(-gate))
            silu = gate * sigmoid
            hidden_ref[rows, :] = (silu * up).astype(BF16)
            slope_ref[rows, :UNIT] = up * sigmoid * (1.0 + gate * (1.0 - sigmoid))
            slope_ref[rows, UNIT:] = silu

    return pl.pallas_call(
        body,
        grid=(width // (2 * UNIT),),
        out_shape=[jax.ShapeDtypeStruct((tokens, width // 2), BF16), jax.ShapeDtypeStruct((tokens, width), F32)],
        in_specs=[whole(p) for p in parts] + [pl.BlockSpec((w.shape[0], 2 * UNIT), lambda j: (0, j)) for w in weights],
        out_specs=[pl.BlockSpec((tokens, UNIT), lambda j: (0, j)), pl.BlockSpec((tokens, 2 * UNIT), lambda j: (0, j))],
        scratch_shapes=[pltpu.VMEM((tokens, model), BF16)],
        compiler_params=vmem(56),
        cost_estimate=SMALL,
        name="feed_forward",
    )(*parts, *weights)


def feed_back(parts, weights, slope):
    size, model = parts[0].shape
    tokens = 8 * size
    width = slope.shape[1]
    count = len(weights)

    def body(*refs):
        ins, ws = refs[:8], refs[8 : 8 + count]
        slope_ref, out_ref, stacked = refs[8 + count :]

        @pl.when(pl.program_id(0) == 0)
        def _():
            stack_parts(ins, stacked)

        @pl.loop(0, tokens // CHUNK)
        def _(i):
            rows = pl.ds(pl.multiple_of(i * CHUNK, CHUNK), CHUNK)
            grad = split_product(stacked, rows, ws)
            out_ref[rows, :UNIT] = (grad * slope_ref[rows, :UNIT]).astype(BF16)
            out_ref[rows, UNIT:] = (grad * slope_ref[rows, UNIT:]).astype(BF16)

    return pl.pallas_call(
        body,
        grid=(width // (2 * UNIT),),
        out_shape=jax.ShapeDtypeStruct((tokens, width), BF16),
        in_specs=[whole(p) for p in parts]
        + [pl.BlockSpec((w.shape[0], UNIT), lambda j: (0, j)) for w in weights]
        + [pl.BlockSpec((tokens, 2 * UNIT), lambda j: (0, j))],
        out_specs=pl.BlockSpec((tokens, 2 * UNIT), lambda j: (0, j)),
        scratch_shapes=[pltpu.VMEM((tokens, model), BF16)],
        compiler_params=vmem(56),
        cost_estimate=SMALL,
        name="feed_back",
    )(*parts, *weights, slope)


def rope(x, cosine, sine):
    lane = lax.broadcasted_iota(jnp.int32, x.shape, 1)
    other = jnp.where(lane % HD < HD // 2, pltpu.roll(x, LANES - HD // 2, 1), pltpu.roll(x, HD // 2, 1))
    return x * cosine + other * sine


def head_masks(shape):
    lane = lax.broadcasted_iota(jnp.int32, shape, 1)
    return [lane < HD, lane >= HD]


def attend_body(place_ref, *refs, blocks, size):
    ins = refs[:8]
    weight_ref, cos_ref, sin_ref, start_ref, saved_ref, mixed_ref, lse_ref, stacked, proj_ref = refs[8:]

    @pl.when((pl.program_id(0) == 0) & (pl.program_id(1) == 0))
    def _():
        stack_parts(ins, stacked)

    @pl.when(pl.program_id(1) == 0)
    def _():
        @pl.loop(0, stacked.shape[0] // CHUNK)
        def _(i):
            rows = pl.ds(pl.multiple_of(i * CHUNK, CHUNK), CHUNK)
            proj_ref[rows, :] = dot_nn(stacked[rows, :], weight_ref[...])

    base = pl.program_id(1) * blocks

    def token_rows(j):
        return pl.ds(pl.multiple_of(place_ref[base + j] * size, size), size)

    def table_rows(j):
        return pl.ds(pl.multiple_of(place_ref[8 + base + j] * size, size), size)

    for j in range(blocks):
        rows = token_rows(j)
        here = slice(j * size, (j + 1) * size)
        cosine, sine = cos_ref[table_rows(j), :], sin_ref[table_rows(j), :]
        for p in range(2):
            value = proj_ref[rows, p * LANES : (p + 1) * LANES]
            saved_ref[here, p * LANES : (p + 1) * LANES] = rope(value, cosine, sine).astype(BF16)
        saved_ref[here, 2 * LANES :] = proj_ref[rows, 2 * LANES :].astype(BF16)
    for j in range(blocks):
        here = slice(j * size, (j + 1) * size)
        upto = (j + 1) * size
        query = saved_ref[here, :LANES]
        keys = saved_ref[:upto, LANES : 2 * LANES]
        values = saved_ref[:upto, 2 * LANES :]
        row = lax.broadcasted_iota(jnp.int32, (size, upto), 0) + j * size
        col = lax.broadcasted_iota(jnp.int32, (size, upto), 1)
        visible = (col <= row) & (col >= start_ref[table_rows(j), :])
        q_heads = head_masks(query.shape)
        v_heads = head_masks(values.shape)
        mixed, totals = [], []
        for h in range(2):
            scores = dot_nt(jnp.where(q_heads[h], query, jnp.zeros_like(query)), keys) * SCALE
            scores = jnp.where(visible, scores, MASKED_SCORE)
            top = jnp.max(scores, axis=1, keepdims=True)
            weights = jnp.exp(scores - top)
            total = jnp.sum(weights, axis=1, keepdims=True)
            probs = (weights * (1.0 / total)).astype(BF16)
            mixed.append(dot_nn(probs, jnp.where(v_heads[h], values, jnp.zeros_like(values))))
            totals.append(jnp.broadcast_to(top + jnp.log(total), query.shape))
        mixed_ref[token_rows(j), :] = (mixed[0] + mixed[1]).astype(BF16)
        lse_ref[here, :] = jnp.where(q_heads[0], totals[0], totals[1])


def attend_back_body(place_ref, *refs, blocks, size):
    ins = refs[:8]
    weight_ref, saved_ref, lse_ref, cos_ref, sin_ref, start_ref, out_ref, dk_ref, dv_ref, stacked, grad_ref = refs[8:]

    @pl.when((pl.program_id(0) == 0) & (pl.program_id(1) == 0))
    def _():
        stack_parts(ins, stacked)

    @pl.when(pl.program_id(1) == 0)
    def _():
        @pl.loop(0, stacked.shape[0] // CHUNK)
        def _(i):
            rows = pl.ds(pl.multiple_of(i * CHUNK, CHUNK), CHUNK)
            grad_ref[rows, :] = dot_nn(stacked[rows, :], weight_ref[...]).astype(BF16)

    base = pl.program_id(1) * blocks

    def token_rows(j):
        return pl.ds(pl.multiple_of(place_ref[base + j] * size, size), size)

    def table_rows(j):
        return pl.ds(pl.multiple_of(place_ref[8 + base + j] * size, size), size)

    dk_ref[...] = jnp.zeros_like(dk_ref)
    dv_ref[...] = jnp.zeros_like(dv_ref)
    for j in range(blocks):
        here = slice(j * size, (j + 1) * size)
        upto = (j + 1) * size
        rows = token_rows(j)
        query = saved_ref[here, :LANES]
        keys = saved_ref[:upto, LANES : 2 * LANES]
        values = saved_ref[:upto, 2 * LANES :]
        grad = grad_ref[rows, :]
        row = lax.broadcasted_iota(jnp.int32, (size, upto), 0) + j * size
        col = lax.broadcasted_iota(jnp.int32, (size, upto), 1)
        visible = (col <= row) & (col >= start_ref[table_rows(j), :])
        q_heads = head_masks(query.shape)
        k_heads = head_masks(keys.shape)
        dq = jnp.zeros(query.shape, F32)
        dk = jnp.zeros(keys.shape, F32)
        dv = jnp.zeros(keys.shape, F32)
        for h in range(2):
            q_head = jnp.where(q_heads[h], query, jnp.zeros_like(query))
            g_head = jnp.where(q_heads[h], grad, jnp.zeros_like(grad))
            scores = dot_nt(q_head, keys) * SCALE
            log_total = lse_ref[here, h * HD : h * HD + 1]
            probs = jnp.exp(jnp.where(visible, scores, MASKED_SCORE) - log_total)
            d_probs = dot_nt(g_head, values)
            inner = jnp.sum(probs * d_probs, axis=1, keepdims=True)
            d_scores = (probs * (d_probs - inner)).astype(BF16)
            dq += dot_nn(d_scores, jnp.where(k_heads[h], keys, jnp.zeros_like(keys)))
            dk += dot_tn(d_scores, q_head)
            dv += dot_tn(probs.astype(BF16), g_head)
        out_ref[rows, :LANES] = rope(dq * SCALE, cos_ref[table_rows(j), :], -sin_ref[table_rows(j), :]).astype(BF16)
        dk_ref[:upto, :] += dk
        dv_ref[:upto, :] += dv
    for j in range(blocks):
        here = slice(j * size, (j + 1) * size)
        rows = token_rows(j)
        out_ref[rows, LANES : 2 * LANES] = rope(dk_ref[here, :] * SCALE, cos_ref[table_rows(j), :], -sin_ref[table_rows(j), :]).astype(BF16)
        out_ref[rows, 2 * LANES :] = dv_ref[here, :].astype(BF16)


def by_pair(tokens, width):
    return pl.BlockSpec((tokens, width), lambda p, s, places: (0, p))


def by_sequence(length, width):
    return pl.BlockSpec((length, width), lambda p, s, places: (s, p))


def attend(parts, weight, cosine, sine, start, places, length):
    size, model = parts[0].shape
    tokens = 8 * size
    width = weight.shape[1] * 3 // 4
    pairs = width // (3 * LANES)
    return pl.pallas_call(
        functools.partial(attend_body, blocks=length // size, size=size),
        grid_spec=pltpu.PrefetchScalarGridSpec(
            num_scalar_prefetch=1,
            grid=(pairs, tokens // length),
            in_specs=[whole(p) for p in parts] + [by_pair(model, 3 * LANES)] + [whole(t) for t in (cosine, sine, start)],
            out_specs=[by_sequence(length, 3 * LANES), by_pair(tokens, LANES), by_sequence(length, LANES)],
            scratch_shapes=[pltpu.VMEM((tokens, model), BF16), pltpu.VMEM((tokens, 3 * LANES), F32)],
        ),
        out_shape=[
            jax.ShapeDtypeStruct((tokens, width), BF16),
            jax.ShapeDtypeStruct((tokens, pairs * LANES), BF16),
            jax.ShapeDtypeStruct((tokens, pairs * LANES), F32),
        ],
        compiler_params=vmem(56),
        cost_estimate=SMALL,
        name="attend",
    )(places, *parts, weight, cosine, sine, start)


def attend_back(parts, weight, saved, lse, cosine, sine, start, places, length):
    size, model = parts[0].shape
    tokens = 8 * size
    pairs = weight.shape[1] // (4 * LANES)
    return pl.pallas_call(
        functools.partial(attend_back_body, blocks=length // size, size=size),
        grid_spec=pltpu.PrefetchScalarGridSpec(
            num_scalar_prefetch=1,
            grid=(pairs, tokens // length),
            in_specs=[whole(p) for p in parts]
            + [pl.BlockSpec((model, LANES), lambda p, s, places: (0, 3 * pairs + p)), by_sequence(length, 3 * LANES), by_sequence(length, LANES)]
            + [whole(t) for t in (cosine, sine, start)],
            out_specs=by_pair(tokens, 3 * LANES),
            scratch_shapes=[
                pltpu.VMEM((length, LANES), F32),
                pltpu.VMEM((length, LANES), F32),
                pltpu.VMEM((tokens, model), BF16),
                pltpu.VMEM((tokens, LANES), BF16),
            ],
        ),
        out_shape=jax.ShapeDtypeStruct(saved.shape, BF16),
        compiler_params=vmem(56),
        cost_estimate=SMALL,
        name="attend_back",
    )(places, *parts, weight, saved, lse, cosine, sine, start)


def rms_rows(values):
    factor = lax.rsqrt(jnp.mean(values * values, axis=-1, keepdims=True) + EPSILON)
    return values * factor, factor


def norm_input(inner, normed, factor):
    return factor * (inner - normed * jnp.mean(inner * normed, axis=-1, keepdims=True))


def rope_tables(positions):
    inverse_freq = 1.0 / ROPE_BASE ** (jnp.arange(0, HD, 2, dtype=F32) / HD)
    angles = positions.astype(F32)[:, None] * inverse_freq
    cosine, sine = jnp.cos(angles), jnp.sin(angles)
    return (
        jnp.concatenate([cosine] * 4, axis=1),
        jnp.concatenate([-sine, sine, -sine, sine], axis=1),
    )


ATTN = Group("y", "x", None, ("r", "zh", "zl"))
MLP = Group("y", "x", None, ("r", "zh", "zl"))


def local(tokens, positions, attn_gain, w_query, w_key, w_value, w_out, mlp_gain, w_gate, w_up, w_down, out_grad):
    own = tokens.shape[1]
    model = tokens.shape[2]
    length = own * lax.axis_size("x") * lax.axis_size("c")
    outer = lax.axis_size("r")
    shape = tokens.shape
    gain_one = attn_gain.astype(F32)[:, None]
    gain_two = mlp_gain.astype(F32)[:, None]

    attn_mixed = mix_columns([w_query, w_key, w_value], gain_one, LANES, [jnp.transpose(w_out)])
    attn_all = ATTN.gather_weight(ATTN.share_columns(attn_mixed))
    inputs = after(tokens, attn_mixed).reshape(own, model).astype(F32)
    normed_one, factor_one = rms_rows(inputs)
    one_low = normed_one.astype(BF16)
    gate_up_rows = MLP.share_columns(mix_columns([after(w_gate, one_low), w_up], gain_two, UNIT))
    gate_up_all = MLP.gather_weight(gate_up_rows)

    one_all = ATTN.gather_tokens(ATTN.to_slots(one_low, outer))
    where = positions.reshape(own, 1)
    for axis in ("c", "x", "y"):
        where = jnp.concatenate([where, swap(where, axis)], axis=0)
    where = where.reshape(-1)
    cosine, sine = rope_tables(where)
    place = lax.axis_index("x") * 2 + lax.axis_index("c")
    core = lax.axis_index("c")
    slot_part = scalars([jnp.where(core == 0, PLACES[0].index(i), PLACES[1].index(i)) for i in range(8)])
    slots = scalars([s * 4 + (j ^ place) for s in range(2) for j in range(4)])
    places = jnp.concatenate([slot_part[slots], slots])
    row = jnp.arange(2 * length, dtype=jnp.int32)
    start = (((row // own % 4) ^ place) * own + row % own - where)[:, None]
    saved, mixed, lse = attend(after(one_all, gate_up_rows), attn_all[0], cosine, sine, start, places, length)
    down_rows = MLP.share_columns(jnp.transpose(after(w_down, mixed)))
    down_all = MLP.gather_weight(after(down_rows, gate_up_rows))

    attn_out = ATTN.scatter_tokens(mixed, attn_all, 3)
    first_sum = inputs + ATTN.from_slots(attn_out, outer)

    grad_rows = out_grad.reshape(own, model)
    normed_two, factor_two = rms_rows(first_sum)
    two_low = MLP.to_slots(normed_two.astype(BF16), outer)
    two_all = MLP.gather_tokens(two_low)
    dy_all = MLP.gather_tokens(MLP.to_slots(after(grad_rows, one_all), outer))
    hidden, slope = feed_forward(two_all, gate_up_all)
    down_terms = MLP.weight_terms(dy_all, hidden)
    down_grad = MLP.scatter_weight(down_terms)
    d_gate_up = feed_back(after(dy_all, down_terms), down_all, slope)
    inner_sums = MLP.scatter_begin(d_gate_up, gate_up_all)
    gate_up_terms = after(MLP.weight_terms(two_all, after(d_gate_up, *inner_sums)), down_grad)
    gate_up_grad = MLP.scatter_weight(gate_up_terms)
    inner_two = MLP.scatter_end(after(inner_sums[:2], gate_up_terms) + inner_sums[2:])

    d_first = grad_rows.astype(F32) + norm_input(MLP.from_slots(inner_two, outer), normed_two, factor_two)
    d_attn_all = ATTN.gather_tokens(ATTN.to_slots(d_first.astype(BF16), outer))
    zero, one, two, three = MLP.scatter_begin(after(hidden, d_first), down_all)
    d_attn_all = after(d_attn_all, zero, one, two, three)
    d_qkv = attend_back(d_attn_all, attn_all[0], saved, lse, cosine, sine, start, places, length)
    zero, one = after((zero, one), d_qkv)
    attn_terms = after(attention_terms(one_all, d_qkv, d_attn_all, mixed), gate_up_grad)
    attn_grad = ATTN.scatter_weight(attn_terms)
    inner_one = ATTN.scatter_tokens(d_qkv, attn_all)
    tokens_grad = d_first + norm_input(ATTN.from_slots(inner_one, outer), normed_one, factor_one)
    mlp_out = MLP.scatter_end((zero, one, two, three))
    block_out = (first_sum + MLP.from_slots(mlp_out, outer)).astype(BF16)

    down_w = MLP.return_columns(down_grad)
    gate_w, up_w, gain_mlp = part_columns(MLP.return_columns(gate_up_grad), [w_gate, w_up], gain_two, UNIT)
    query_w, key_w, value_w, out_w, gain_attn = part_columns(
        ATTN.return_columns(attn_grad), [w_query, w_key, w_value], gain_one, LANES, w_out.shape[0]
    )
    return (
        block_out.reshape(shape),
        tokens_grad.astype(BF16).reshape(shape),
        gain_attn.reshape(-1),
        query_w,
        key_w,
        value_w,
        jnp.transpose(out_w),
        gain_mlp.reshape(-1),
        gate_w,
        up_w,
        jnp.transpose(down_w.astype(F32)),
    )


def solution(mesh):
    fsdp = mesh.shape["fsdp"]
    sizes = (fsdp // 8, 2, 2, 2, mesh.shape["ctx"] // 2, 2)
    fine = Mesh(mesh.devices.reshape(sizes), AXES)
    rows, cols = AXES[:4], AXES[4:]
    tokens, places, vector = P(rows, cols, None), P(rows, cols), P(AXES)
    first, second = P(AXES, None), P(None, AXES)
    in_specs = (tokens, places, vector, first, first, first, second, vector, first, first, second, tokens)
    out_specs = (tokens, tokens, vector, first, first, first, second, vector, first, first, second)
    return jax.shard_map(local, mesh=fine, in_specs=in_specs, out_specs=out_specs, check_vma=False)
```

```python
import functools

import jax
import jax.numpy as jnp
from jax import lax
from jax.experimental import pallas as pl
from jax.experimental.pallas import tpu as pltpu
from jax.sharding import Mesh
from jax.sharding import PartitionSpec as P

H = 32
HD = 64
EPSILON = 1e-05
ROPE_BASE = 130000.0
MASKED_SCORE = -1e30
SCALE = HD ** (-0.5)
LANES = 128
MIB = 1 << 20
BF16 = jnp.bfloat16
F32 = jnp.float32
AXES = ("r", "zh", "zl", "y", "x", "c")
NT = (((1,), (1,)), ((), ()))
TN = (((0,), (0,)), ((), ()))


def dot_nn(a, b):
    return jnp.dot(a, b, preferred_element_type=F32)


def dot_nt(a, b):
    return lax.dot_general(a, b, NT, preferred_element_type=F32)


def dot_tn(a, b):
    return lax.dot_general(a, b, TN, preferred_element_type=F32)


def flip(x, axes, masks):
    return lax.ppermute(x, axes, [(i, i ^ masks[i & 1]) for i in range(8)])


def swap(x, axis):
    return lax.ppermute(x, axis, [(0, 1), (1, 0)])


def after(x, *others):
    return lax.optimization_barrier((x,) + others)[0]


PLACES = ((0, 1, 2, 3, 5, 4, 6, 7), (0, 1, 4, 5, 3, 2, 6, 7))


class Group:
    def __init__(self, d1, d2, half, spread):
        self.axes = (d1, d2, "c")
        self.half, self.spread = half, spread

    def column_order(self, outer):
        names = ("r", "zh", "zl", "y", "x")
        sizes = dict(zip(names, (outer, 2, 2, 2, 2)))
        sequence = ([self.half] if self.half else []) + list(self.spread) + list(self.axes[:2])
        order = [0]
        for name in sequence:
            step = 1
            for later in names[names.index(name) + 1 :]:
                step *= sizes[later]
            order = [base + step * i for base in order for i in range(sizes[name])]
        return order

    def reorder(self, x, order):
        if order == list(range(len(order))):
            return x
        width = x.shape[1] // len(order)
        return jnp.concatenate([x[:, i * width : (i + 1) * width] for i in order], axis=1)

    def flip_halves(self, x):
        if not self.half:
            return x
        width = x.shape[1] // 2
        at = lax.axis_index(self.half)
        first = lax.dynamic_slice_in_dim(x, at * width, width, axis=1)
        return jnp.concatenate([first, lax.dynamic_slice_in_dim(x, (1 - at) * width, width, axis=1)], axis=1)

    def to_slots(self, x, outer):
        return self.flip_halves(self.reorder(x, self.column_order(outer)))

    def from_slots(self, x, outer):
        order = self.column_order(outer)
        return self.reorder(self.flip_halves(x), [order.index(i) for i in range(len(order))])

    def other_core(self, x):
        return flip(x, self.axes, (1, 1))

    def near(self, x):
        return flip(x, self.axes, (2, 4))

    def far(self, x):
        return flip(x, self.axes, (4, 2))

    def gather_tokens(self, x):
        partner = self.other_core(x)
        near_one = self.near(x)
        near_two = self.near(partner)
        far_one = self.far(near_one)
        parts = [x, partner, near_one, near_two, self.other_core(near_one), self.other_core(near_two)]
        return parts + [far_one, self.other_core(far_one)]

    def scatter_begin(self, array, weights, at=0):
        six, seven = rows_product(array, weights, 6, (F32, BF16), at)
        four, five = rows_product(array, weights, 4, (BF16, BF16), at)
        six = six + self.other_core(seven).astype(F32)
        far_one = self.far(six.astype(BF16)).astype(F32)
        array = after(array, six)
        two, three = rows_product(array, weights, 2, (F32, F32), at)
        zero, one = rows_product(array, weights, 0, (F32, F32), at)
        three = (three + self.other_core(five).astype(F32)).astype(BF16)
        two = (two + self.other_core(four).astype(F32) + far_one).astype(BF16)
        return after((zero, one), two, three) + (two, three)

    def scatter_near(self, sums):
        zero, one, two, three = sums
        return zero, one, self.near(two), self.near(three)

    def scatter_end(self, sums):
        zero, one, two, three = sums
        partner = self.other_core((one + three.astype(F32)).astype(BF16))
        return zero + two.astype(F32) + partner.astype(F32)

    def scatter_tokens(self, array, weights, at=0):
        return self.scatter_end(self.scatter_near(self.scatter_begin(array, weights, at)))

    def share_columns(self, weight):
        return lax.all_to_all(weight, self.axes, split_axis=1, concat_axis=0, tiled=True)

    def gather_weight(self, rows):
        rows = lax.all_gather(rows, self.spread, axis=0, tiled=True)
        return [rows, swap(rows, self.half)] if self.half else [rows]

    def weight_terms(self, parts, right):
        if self.half:
            away = swap(parts_product(parts, right, 1, 2, None), self.half)
            return parts_product(parts, right, 0, 2, away)
        return parts_product(parts, right, 0, 1, None)

    def scatter_weight(self, terms):
        return lax.psum_scatter(terms, self.spread, scatter_dimension=0, tiled=True)

    def return_columns(self, grad):
        return lax.all_to_all(grad, self.axes, split_axis=0, concat_axis=1, tiled=True)


def scalars(values):
    return jnp.stack(values).astype(jnp.int32)


VMEM_SPEC = pl.BlockSpec(memory_space=pltpu.VMEM)


SMALL = pl.CostEstimate(flops=1024, bytes_accessed=1024, transcendentals=0)


def cost(microseconds):
    return pl.CostEstimate(flops=int(microseconds * 1.1e9), bytes_accessed=int(microseconds * 3e6), transcendentals=0)


def vmem(limit):
    return pltpu.CompilerParams(vmem_limit_bytes=limit * MIB)


def parts_of(widths, tails, unit):
    out = []
    at = 0
    for device in range(8):
        for p in range(widths[0] // unit):
            for i, width in enumerate(widths):
                out.append((i, device * width + p * unit, unit, at))
                at += unit
        for i, width in enumerate(tails):
            out.append((len(widths) + i, device * width, width, at))
            at += width
    return out


def mix_columns(weights, gain, unit, tails=()):
    arrays = list(weights) + list(tails)
    rows = arrays[0].shape[0]
    parts = parts_of([w.shape[1] // 8 for w in weights], [w.shape[1] // 8 for w in tails], unit)

    def body(gain_ref, *refs):
        factor = gain_ref[...]
        for i, source, width, at in parts:
            value = refs[i][:, source : source + width]
            if i < len(weights):
                value = (value.astype(F32) * factor).astype(BF16)
            refs[-1][:, at : at + width] = value

    return pl.pallas_call(
        body,
        out_shape=jax.ShapeDtypeStruct((rows, sum(w.shape[1] for w in arrays)), BF16),
        in_specs=[VMEM_SPEC] * (1 + len(arrays)),
        out_specs=VMEM_SPEC,
        cost_estimate=SMALL,
        name="mix_columns",
    )(gain, *arrays)


def part_columns(mixed, weights, gain, unit, tail=None):
    count = len(weights)
    rows = weights[0].shape[0]
    tails = [] if tail is None else [tail]
    parts = parts_of([w.shape[1] // 8 for w in weights], [w // 8 for w in tails], unit)

    def body(mixed_ref, gain_ref, *refs):
        ins, outs = refs[:count], refs[count:-1]
        factor = gain_ref[...]
        acc = jnp.zeros((rows, LANES), F32)
        for i, source, width, at in parts:
            value = mixed_ref[:, at : at + width].astype(F32)
            if i < count:
                term = ins[i][:, source : source + width].astype(F32) * value
                for p in range(width // LANES):
                    acc = acc + term[:, p * LANES : (p + 1) * LANES]
                value = value * factor
            outs[i][:, source : source + width] = value
        refs[-1][...] = jnp.sum(acc, axis=1, keepdims=True)

    shapes = [w.shape for w in weights] + [(rows, w) for w in tails] + [(rows, 1)]
    return pl.pallas_call(
        body,
        out_shape=[jax.ShapeDtypeStruct(shape, F32) for shape in shapes],
        in_specs=[VMEM_SPEC] * (2 + count),
        out_specs=[VMEM_SPEC] * len(shapes),
        cost_estimate=SMALL,
        name="part_columns",
    )(mixed, gain, *weights)


def rows_product(array, weights, first, types, at):
    size = array.shape[0] // 8
    depth = array.shape[1]
    count = len(weights)
    each = weights[0].shape[0]
    step = min(512, each)
    inner = each // step

    def body(array_ref, *refs):
        at = pl.program_id(0) // inner
        for i in range(count):

            @pl.when(at == i)
            def _():
                both = dot_nt(array_ref[...], refs[i][...])
                refs[count][...] = both[:size].astype(types[0])
                refs[count + 1][...] = both[size:].astype(types[1])

    def weight_spec(i):
        return pl.BlockSpec((step, depth), lambda j: (jnp.clip(j - i * inner, 0, inner - 1), at))

    return pl.pallas_call(
        body,
        grid=(count * inner,),
        out_shape=[jax.ShapeDtypeStruct((size, count * each), t) for t in types],
        in_specs=[pl.BlockSpec((2 * size, depth), lambda j: (first // 2, 0))] + [weight_spec(i) for i in range(count)],
        out_specs=[pl.BlockSpec((size, step), lambda j: (0, j))] * 2,
        compiler_params=vmem(40),
        cost_estimate=SMALL,
        name="rows_product",
    )(array, *weights)


def parts_product(parts, right, which, pieces, added):
    size = parts[0].shape[0]
    tokens, width = right.shape
    model = parts[0].shape[1] // pieces
    step = 512 if width <= 1024 else 256
    offset = which * (model // step)

    def body(*refs):
        ins, right_ref = refs[:8], refs[8]
        out_ref, stacked = refs[-2], refs[-1]
        for p in range(8):
            stacked[p * size : (p + 1) * size, :] = ins[p][...]
        total = dot_tn(stacked[...], right_ref[...])
        if added is not None:
            total = total + refs[9][...].astype(F32)
        out_ref[...] = total.astype(BF16)

    block = pl.BlockSpec((step, width), lambda j: (j, 0))
    return pl.pallas_call(
        body,
        grid=(model // step,),
        out_shape=jax.ShapeDtypeStruct((model, width), BF16),
        in_specs=[pl.BlockSpec((size, step), lambda j: (0, offset + j))] * 8
        + [pl.BlockSpec((tokens, width), lambda j: (0, 0))]
        + ([block] if added is not None else []),
        out_specs=block,
        scratch_shapes=[pltpu.VMEM((tokens, step), BF16)],
        compiler_params=vmem(48),
        cost_estimate=cost(model * width / 175000),
        name="parts_product",
    )(*parts, right, *([added] if added is not None else []))


def attention_terms(first, right, second, other):
    size, model = first[0].shape
    tokens, width = right.shape
    rest = other.shape[1]
    step = 512

    def body(*refs):
        right_ref, other_ref, out_ref, stacked = refs[16:]
        stack_parts(refs[:8], stacked)
        out_ref[:, :width] = dot_tn(stacked[...], right_ref[...]).astype(BF16)
        stack_parts(refs[8:16], stacked)
        out_ref[:, width:] = dot_tn(stacked[...], other_ref[...]).astype(BF16)

    return pl.pallas_call(
        body,
        grid=(model // step,),
        out_shape=jax.ShapeDtypeStruct((model, width + rest), BF16),
        in_specs=[pl.BlockSpec((size, step), lambda j: (0, j))] * 16 + [whole(right), whole(other)],
        out_specs=pl.BlockSpec((step, width + rest), lambda j: (j, 0)),
        scratch_shapes=[pltpu.VMEM((tokens, step), BF16)],
        compiler_params=vmem(48),
        cost_estimate=cost(14),
        name="attention_terms",
    )(*first, *second, right, other)


UNIT = 256
CHUNK = 512


def whole(part):
    return pl.BlockSpec(part.shape, lambda *at: (0, 0))


def stack_parts(ins, stacked):
    size = ins[0].shape[0]
    for p in range(8):
        stacked[p * size : (p + 1) * size, :] = ins[p][...]


def split_product(stacked, rows, weights):
    depth = weights[0].shape[0]
    total = dot_nn(stacked[rows, :depth], weights[0][...])
    for i in range(1, len(weights)):
        total += dot_nn(stacked[rows, i * depth : (i + 1) * depth], weights[i][...])
    return total


def feed_forward(parts, weights):
    size, model = parts[0].shape
    tokens = 8 * size
    width = weights[0].shape[1]
    count = len(weights)

    def body(*refs):
        ins, ws = refs[:8], refs[8 : 8 + count]
        hidden_ref, slope_ref, stacked = refs[8 + count :]

        @pl.when(pl.program_id(0) == 0)
        def _():
            stack_parts(ins, stacked)

        @pl.loop(0, tokens // CHUNK)
        def _(i):
            rows = pl.ds(pl.multiple_of(i * CHUNK, CHUNK), CHUNK)
            both = split_product(stacked, rows, ws)
            gate, up = both[:, :UNIT], both[:, UNIT:]
            sigmoid = 1.0 / (1.0 + jnp.exp(-gate))
            silu = gate * sigmoid
            hidden_ref[rows, :] = (silu * up).astype(BF16)
            slope_ref[rows, :UNIT] = up * sigmoid * (1.0 + gate * (1.0 - sigmoid))
            slope_ref[rows, UNIT:] = silu

    return pl.pallas_call(
        body,
        grid=(width // (2 * UNIT),),
        out_shape=[jax.ShapeDtypeStruct((tokens, width // 2), BF16), jax.ShapeDtypeStruct((tokens, width), F32)],
        in_specs=[whole(p) for p in parts] + [pl.BlockSpec((w.shape[0], 2 * UNIT), lambda j: (0, j)) for w in weights],
        out_specs=[pl.BlockSpec((tokens, UNIT), lambda j: (0, j)), pl.BlockSpec((tokens, 2 * UNIT), lambda j: (0, j))],
        scratch_shapes=[pltpu.VMEM((tokens, model), BF16)],
        compiler_params=vmem(56),
        cost_estimate=SMALL,
        name="feed_forward",
    )(*parts, *weights)


def feed_back(parts, weights, slope):
    size, model = parts[0].shape
    tokens = 8 * size
    width = slope.shape[1]
    count = len(weights)

    def body(*refs):
        ins, ws = refs[:8], refs[8 : 8 + count]
        slope_ref, out_ref, stacked = refs[8 + count :]

        @pl.when(pl.program_id(0) == 0)
        def _():
            stack_parts(ins, stacked)

        @pl.loop(0, tokens // CHUNK)
        def _(i):
            rows = pl.ds(pl.multiple_of(i * CHUNK, CHUNK), CHUNK)
            grad = split_product(stacked, rows, ws)
            out_ref[rows, :UNIT] = (grad * slope_ref[rows, :UNIT]).astype(BF16)
            out_ref[rows, UNIT:] = (grad * slope_ref[rows, UNIT:]).astype(BF16)

    return pl.pallas_call(
        body,
        grid=(width // (2 * UNIT),),
        out_shape=jax.ShapeDtypeStruct((tokens, width), BF16),
        in_specs=[whole(p) for p in parts]
        + [pl.BlockSpec((w.shape[0], UNIT), lambda j: (0, j)) for w in weights]
        + [pl.BlockSpec((tokens, 2 * UNIT), lambda j: (0, j))],
        out_specs=pl.BlockSpec((tokens, 2 * UNIT), lambda j: (0, j)),
        scratch_shapes=[pltpu.VMEM((tokens, model), BF16)],
        compiler_params=vmem(56),
        cost_estimate=SMALL,
        name="feed_back",
    )(*parts, *weights, slope)


def rope(x, cosine, sine):
    lane = lax.broadcasted_iota(jnp.int32, x.shape, 1)
    other = jnp.where(lane % HD < HD // 2, pltpu.roll(x, LANES - HD // 2, 1), pltpu.roll(x, HD // 2, 1))
    return x * cosine + other * sine


def head_masks(shape):
    lane = lax.broadcasted_iota(jnp.int32, shape, 1)
    return [lane < HD, lane >= HD]


def attend_body(place_ref, *refs, blocks, size):
    ins = refs[:8]
    weight_ref, cos_ref, sin_ref, start_ref, saved_ref, mixed_ref, lse_ref, stacked, proj_ref = refs[8:]

    @pl.when((pl.program_id(0) == 0) & (pl.program_id(1) == 0))
    def _():
        stack_parts(ins, stacked)

    @pl.when(pl.program_id(1) == 0)
    def _():
        @pl.loop(0, stacked.shape[0] // CHUNK)
        def _(i):
            rows = pl.ds(pl.multiple_of(i * CHUNK, CHUNK), CHUNK)
            proj_ref[rows, :] = dot_nn(stacked[rows, :], weight_ref[...])

    base = pl.program_id(1) * blocks

    def token_rows(j):
        return pl.ds(pl.multiple_of(place_ref[base + j] * size, size), size)

    def table_rows(j):
        return pl.ds(pl.multiple_of(place_ref[8 + base + j] * size, size), size)

    for j in range(blocks):
        rows = token_rows(j)
        here = slice(j * size, (j + 1) * size)
        cosine, sine = cos_ref[table_rows(j), :], sin_ref[table_rows(j), :]
        for p in range(2):
            value = proj_ref[rows, p * LANES : (p + 1) * LANES]
            saved_ref[here, p * LANES : (p + 1) * LANES] = rope(value, cosine, sine).astype(BF16)
        saved_ref[here, 2 * LANES :] = proj_ref[rows, 2 * LANES :].astype(BF16)
    for j in range(blocks):
        here = slice(j * size, (j + 1) * size)
        upto = (j + 1) * size
        query = saved_ref[here, :LANES]
        keys = saved_ref[:upto, LANES : 2 * LANES]
        values = saved_ref[:upto, 2 * LANES :]
        row = lax.broadcasted_iota(jnp.int32, (size, upto), 0) + j * size
        col = lax.broadcasted_iota(jnp.int32, (size, upto), 1)
        visible = (col <= row) & (col >= start_ref[table_rows(j), :])
        q_heads = head_masks(query.shape)
        v_heads = head_masks(values.shape)
        mixed, totals = [], []
        for h in range(2):
            scores = dot_nt(jnp.where(q_heads[h], query, jnp.zeros_like(query)), keys) * SCALE
            scores = jnp.where(visible, scores, MASKED_SCORE)
            top = jnp.max(scores, axis=1, keepdims=True)
            weights = jnp.exp(scores - top)
            total = jnp.sum(weights, axis=1, keepdims=True)
            probs = (weights * (1.0 / total)).astype(BF16)
            mixed.append(dot_nn(probs, jnp.where(v_heads[h], values, jnp.zeros_like(values))))
            totals.append(jnp.broadcast_to(top + jnp.log(total), query.shape))
        mixed_ref[token_rows(j), :] = (mixed[0] + mixed[1]).astype(BF16)
        lse_ref[here, :] = jnp.where(q_heads[0], totals[0], totals[1])


def attend_back_body(place_ref, *refs, blocks, size):
    ins = refs[:8]
    weight_ref, saved_ref, lse_ref, cos_ref, sin_ref, start_ref, out_ref, dk_ref, dv_ref, stacked, grad_ref = refs[8:]

    @pl.when((pl.program_id(0) == 0) & (pl.program_id(1) == 0))
    def _():
        stack_parts(ins, stacked)

    @pl.when(pl.program_id(1) == 0)
    def _():
        @pl.loop(0, stacked.shape[0] // CHUNK)
        def _(i):
            rows = pl.ds(pl.multiple_of(i * CHUNK, CHUNK), CHUNK)
            grad_ref[rows, :] = dot_nn(stacked[rows, :], weight_ref[...]).astype(BF16)

    base = pl.program_id(1) * blocks

    def token_rows(j):
        return pl.ds(pl.multiple_of(place_ref[base + j] * size, size), size)

    def table_rows(j):
        return pl.ds(pl.multiple_of(place_ref[8 + base + j] * size, size), size)

    dk_ref[...] = jnp.zeros_like(dk_ref)
    dv_ref[...] = jnp.zeros_like(dv_ref)
    for j in range(blocks):
        here = slice(j * size, (j + 1) * size)
        upto = (j + 1) * size
        rows = token_rows(j)
        query = saved_ref[here, :LANES]
        keys = saved_ref[:upto, LANES : 2 * LANES]
        values = saved_ref[:upto, 2 * LANES :]
        grad = grad_ref[rows, :]
        row = lax.broadcasted_iota(jnp.int32, (size, upto), 0) + j * size
        col = lax.broadcasted_iota(jnp.int32, (size, upto), 1)
        visible = (col <= row) & (col >= start_ref[table_rows(j), :])
        q_heads = head_masks(query.shape)
        k_heads = head_masks(keys.shape)
        dq = jnp.zeros(query.shape, F32)
        dk = jnp.zeros(keys.shape, F32)
        dv = jnp.zeros(keys.shape, F32)
        for h in range(2):
            q_head = jnp.where(q_heads[h], query, jnp.zeros_like(query))
            g_head = jnp.where(q_heads[h], grad, jnp.zeros_like(grad))
            scores = dot_nt(q_head, keys) * SCALE
            log_total = lse_ref[here, h * HD : h * HD + 1]
            probs = jnp.exp(jnp.where(visible, scores, MASKED_SCORE) - log_total)
            d_probs = dot_nt(g_head, values)
            inner = jnp.sum(probs * d_probs, axis=1, keepdims=True)
            d_scores = (probs * (d_probs - inner)).astype(BF16)
            dq += dot_nn(d_scores, jnp.where(k_heads[h], keys, jnp.zeros_like(keys)))
            dk += dot_tn(d_scores, q_head)
            dv += dot_tn(probs.astype(BF16), g_head)
        out_ref[rows, :LANES] = rope(dq * SCALE, cos_ref[table_rows(j), :], -sin_ref[table_rows(j), :]).astype(BF16)
        dk_ref[:upto, :] += dk
        dv_ref[:upto, :] += dv
    for j in range(blocks):
        here = slice(j * size, (j + 1) * size)
        rows = token_rows(j)
        out_ref[rows, LANES : 2 * LANES] = rope(dk_ref[here, :] * SCALE, cos_ref[table_rows(j), :], -sin_ref[table_rows(j), :]).astype(BF16)
        out_ref[rows, 2 * LANES :] = dv_ref[here, :].astype(BF16)


def by_pair(tokens, width):
    return pl.BlockSpec((tokens, width), lambda p, s, places: (0, p))


def by_sequence(length, width):
    return pl.BlockSpec((length, width), lambda p, s, places: (s, p))


def attend(parts, weight, cosine, sine, start, places, length):
    size, model = parts[0].shape
    tokens = 8 * size
    width = weight.shape[1] * 3 // 4
    pairs = width // (3 * LANES)
    return pl.pallas_call(
        functools.partial(attend_body, blocks=length // size, size=size),
        grid_spec=pltpu.PrefetchScalarGridSpec(
            num_scalar_prefetch=1,
            grid=(pairs, tokens // length),
            in_specs=[whole(p) for p in parts] + [by_pair(model, 3 * LANES)] + [whole(t) for t in (cosine, sine, start)],
            out_specs=[by_sequence(length, 3 * LANES), by_pair(tokens, LANES), by_sequence(length, LANES)],
            scratch_shapes=[pltpu.VMEM((tokens, model), BF16), pltpu.VMEM((tokens, 3 * LANES), F32)],
        ),
        out_shape=[
            jax.ShapeDtypeStruct((tokens, width), BF16),
            jax.ShapeDtypeStruct((tokens, pairs * LANES), BF16),
            jax.ShapeDtypeStruct((tokens, pairs * LANES), F32),
        ],
        compiler_params=vmem(56),
        cost_estimate=SMALL,
        name="attend",
    )(places, *parts, weight, cosine, sine, start)


def attend_back(parts, weight, saved, lse, cosine, sine, start, places, length):
    size, model = parts[0].shape
    tokens = 8 * size
    pairs = weight.shape[1] // (4 * LANES)
    return pl.pallas_call(
        functools.partial(attend_back_body, blocks=length // size, size=size),
        grid_spec=pltpu.PrefetchScalarGridSpec(
            num_scalar_prefetch=1,
            grid=(pairs, tokens // length),
            in_specs=[whole(p) for p in parts]
            + [pl.BlockSpec((model, LANES), lambda p, s, places: (0, 3 * pairs + p)), by_sequence(length, 3 * LANES), by_sequence(length, LANES)]
            + [whole(t) for t in (cosine, sine, start)],
            out_specs=by_pair(tokens, 3 * LANES),
            scratch_shapes=[
                pltpu.VMEM((length, LANES), F32),
                pltpu.VMEM((length, LANES), F32),
                pltpu.VMEM((tokens, model), BF16),
                pltpu.VMEM((tokens, LANES), BF16),
            ],
        ),
        out_shape=jax.ShapeDtypeStruct(saved.shape, BF16),
        compiler_params=vmem(56),
        cost_estimate=cost(36),
        name="attend_back",
    )(places, *parts, weight, saved, lse, cosine, sine, start)


def rms_rows(values):
    factor = lax.rsqrt(jnp.mean(values * values, axis=-1, keepdims=True) + EPSILON)
    return values * factor, factor


def norm_input(inner, normed, factor):
    return factor * (inner - normed * jnp.mean(inner * normed, axis=-1, keepdims=True))


def rope_tables(positions):
    inverse_freq = 1.0 / ROPE_BASE ** (jnp.arange(0, HD, 2, dtype=F32) / HD)
    angles = positions.astype(F32)[:, None] * inverse_freq
    cosine, sine = jnp.cos(angles), jnp.sin(angles)
    return (
        jnp.concatenate([cosine] * 4, axis=1),
        jnp.concatenate([-sine, sine, -sine, sine], axis=1),
    )


ATTN = Group("y", "x", None, ("r", "zh", "zl"))
MLP = Group("y", "x", None, ("r", "zh", "zl"))


def local(tokens, positions, attn_gain, w_query, w_key, w_value, w_out, mlp_gain, w_gate, w_up, w_down, out_grad):
    own = tokens.shape[1]
    model = tokens.shape[2]
    length = own * lax.axis_size("x") * lax.axis_size("c")
    outer = lax.axis_size("r")
    shape = tokens.shape
    gain_one = attn_gain.astype(F32)[:, None]
    gain_two = mlp_gain.astype(F32)[:, None]

    attn_mixed = mix_columns([w_query, w_key, w_value], gain_one, LANES, [jnp.transpose(w_out)])
    attn_all = ATTN.gather_weight(ATTN.share_columns(attn_mixed))
    inputs = after(tokens, attn_mixed).reshape(own, model).astype(F32)
    normed_one, factor_one = rms_rows(inputs)
    one_low = normed_one.astype(BF16)
    gate_up_rows = MLP.share_columns(mix_columns([after(w_gate, one_low), w_up], gain_two, UNIT))
    gate_up_all = MLP.gather_weight(gate_up_rows)

    one_all = ATTN.gather_tokens(ATTN.to_slots(one_low, outer))
    where = positions.reshape(own, 1)
    for axis in ("c", "x", "y"):
        where = jnp.concatenate([where, swap(where, axis)], axis=0)
    where = where.reshape(-1)
    cosine, sine = rope_tables(where)
    place = lax.axis_index("x") * 2 + lax.axis_index("c")
    core = lax.axis_index("c")
    slot_part = scalars([jnp.where(core == 0, PLACES[0].index(i), PLACES[1].index(i)) for i in range(8)])
    slots = scalars([s * 4 + (j ^ place) for s in range(2) for j in range(4)])
    places = jnp.concatenate([slot_part[slots], slots])
    row = jnp.arange(2 * length, dtype=jnp.int32)
    start = (((row // own % 4) ^ place) * own + row % own - where)[:, None]
    saved, mixed, lse = attend(after(one_all, gate_up_rows), attn_all[0], cosine, sine, start, places, length)
    down_rows = MLP.share_columns(jnp.transpose(after(w_down, mixed)))
    down_all = MLP.gather_weight(after(down_rows, gate_up_rows))

    attn_out = ATTN.scatter_tokens(mixed, attn_all, 3)
    first_sum = inputs + ATTN.from_slots(attn_out, outer)

    grad_rows = out_grad.reshape(own, model)
    normed_two, factor_two = rms_rows(first_sum)
    two_low = MLP.to_slots(normed_two.astype(BF16), outer)
    two_all = MLP.gather_tokens(two_low)
    dy_all = MLP.gather_tokens(MLP.to_slots(after(grad_rows, one_all), outer))
    hidden, slope = feed_forward(two_all, gate_up_all)
    down_terms = MLP.weight_terms(dy_all, hidden)
    down_grad = MLP.scatter_weight(down_terms)
    d_gate_up = feed_back(after(dy_all, down_terms), down_all, slope)
    inner_sums = MLP.scatter_begin(d_gate_up, gate_up_all)
    gate_up_terms = MLP.weight_terms(two_all, after(d_gate_up, *inner_sums))
    inner_sums = MLP.scatter_near(inner_sums)
    gate_up_grad = MLP.scatter_weight(after(gate_up_terms, down_grad, *inner_sums))
    inner_two = MLP.scatter_end(inner_sums)

    d_first = grad_rows.astype(F32) + norm_input(MLP.from_slots(inner_two, outer), normed_two, factor_two)
    d_attn_all = ATTN.gather_tokens(ATTN.to_slots(d_first.astype(BF16), outer))
    mlp_sums = MLP.scatter_begin(after(hidden, d_first), down_all)
    d_attn_all = after(d_attn_all, *mlp_sums)
    d_qkv = attend_back(d_attn_all, attn_all[0], saved, lse, cosine, sine, start, places, length)
    terms = attention_terms(one_all, d_qkv, d_attn_all, mixed)
    inner_sums = ATTN.scatter_begin(after(d_qkv, terms), attn_all)
    attn_grad = ATTN.scatter_weight(after(terms, gate_up_grad, inner_sums[0]))
    mlp_sums = MLP.scatter_near(after(mlp_sums, *inner_sums))
    gate_up_grad, down_grad = after((gate_up_grad, down_grad), *inner_sums)
    inner_one = ATTN.scatter_end(ATTN.scatter_near(inner_sums))
    tokens_grad = (d_first + norm_input(ATTN.from_slots(inner_one, outer), normed_one, factor_one)).astype(BF16)
    mlp_out = MLP.scatter_end(mlp_sums)
    block_out = (first_sum + MLP.from_slots(mlp_out, outer)).astype(BF16)

    down_w = jnp.transpose(MLP.return_columns(down_grad).astype(F32))
    gate_w, up_w, gain_mlp = part_columns(MLP.return_columns(gate_up_grad), [w_gate, w_up], gain_two, UNIT)
    attn_grad = after(attn_grad, tokens_grad, block_out, down_w)
    query_w, key_w, value_w, out_w, gain_attn = part_columns(
        ATTN.return_columns(attn_grad), [w_query, w_key, w_value], gain_one, LANES, w_out.shape[0]
    )
    return (
        block_out.reshape(shape),
        tokens_grad.reshape(shape),
        gain_attn.reshape(-1),
        query_w,
        key_w,
        value_w,
        jnp.transpose(out_w),
        gain_mlp.reshape(-1),
        gate_w,
        up_w,
        down_w,
    )


def solution(mesh):
    fsdp = mesh.shape["fsdp"]
    sizes = (fsdp // 8, 2, 2, 2, mesh.shape["ctx"] // 2, 2)
    fine = Mesh(mesh.devices.reshape(sizes), AXES)
    rows, cols = AXES[:4], AXES[4:]
    tokens, places, vector = P(rows, cols, None), P(rows, cols), P(AXES)
    first, second = P(AXES, None), P(None, AXES)
    in_specs = (tokens, places, vector, first, first, first, second, vector, first, first, second, tokens)
    out_specs = (tokens, tokens, vector, first, first, first, second, vector, first, first, second)
    return jax.shard_map(local, mesh=fine, in_specs=in_specs, out_specs=out_specs, check_vma=False)
```

```python
import functools

import jax
import jax.numpy as jnp
from jax import lax
from jax.experimental import pallas as pl
from jax.experimental.pallas import tpu as pltpu
from jax.sharding import Mesh
from jax.sharding import PartitionSpec as P

H = 32
HD = 64
EPSILON = 1e-05
ROPE_BASE = 130000.0
MASKED_SCORE = -1e30
SCALE = HD ** (-0.5)
LANES = 128
MIB = 1 << 20
BF16 = jnp.bfloat16
F32 = jnp.float32
AXES = ("r", "zh", "zl", "y", "x", "c")
NT = (((1,), (1,)), ((), ()))
TN = (((0,), (0,)), ((), ()))


def dot_nn(a, b):
    return jnp.dot(a, b, preferred_element_type=F32)


def dot_nt(a, b):
    return lax.dot_general(a, b, NT, preferred_element_type=F32)


def dot_tn(a, b):
    return lax.dot_general(a, b, TN, preferred_element_type=F32)


def flip(x, axes, masks):
    return lax.ppermute(x, axes, [(i, i ^ masks[i & 1]) for i in range(8)])


def swap(x, axis):
    return lax.ppermute(x, axis, [(0, 1), (1, 0)])


def after(x, *others):
    return lax.optimization_barrier((x,) + others)[0]


PLACES = ((0, 1, 2, 3, 5, 4, 6, 7), (0, 1, 4, 5, 3, 2, 6, 7))


class Group:
    def __init__(self, d1, d2, half, spread):
        self.axes = (d1, d2, "c")
        self.half, self.spread = half, spread

    def column_order(self, outer):
        names = ("r", "zh", "zl", "y", "x")
        sizes = dict(zip(names, (outer, 2, 2, 2, 2)))
        sequence = ([self.half] if self.half else []) + list(self.spread) + list(self.axes[:2])
        order = [0]
        for name in sequence:
            step = 1
            for later in names[names.index(name) + 1 :]:
                step *= sizes[later]
            order = [base + step * i for base in order for i in range(sizes[name])]
        return order

    def reorder(self, x, order):
        if order == list(range(len(order))):
            return x
        width = x.shape[1] // len(order)
        return jnp.concatenate([x[:, i * width : (i + 1) * width] for i in order], axis=1)

    def flip_halves(self, x):
        if not self.half:
            return x
        width = x.shape[1] // 2
        at = lax.axis_index(self.half)
        first = lax.dynamic_slice_in_dim(x, at * width, width, axis=1)
        return jnp.concatenate([first, lax.dynamic_slice_in_dim(x, (1 - at) * width, width, axis=1)], axis=1)

    def to_slots(self, x, outer):
        return self.flip_halves(self.reorder(x, self.column_order(outer)))

    def from_slots(self, x, outer):
        order = self.column_order(outer)
        return self.reorder(self.flip_halves(x), [order.index(i) for i in range(len(order))])

    def other_core(self, x):
        return flip(x, self.axes, (1, 1))

    def near(self, x):
        return flip(x, self.axes, (2, 4))

    def far(self, x):
        return flip(x, self.axes, (4, 2))

    def gather_near(self, x):
        partner = self.other_core(x)
        return x, partner, self.near(x), self.near(partner)

    def gather_far(self, parts):
        x, partner, near_one, near_two = parts
        far_one = self.far(near_one)
        parts = [x, partner, near_one, near_two, self.other_core(near_one), self.other_core(near_two)]
        return parts + [far_one, self.other_core(far_one)]

    def gather_tokens(self, x):
        return self.gather_far(self.gather_near(x))

    def scatter_begin(self, array, weights, at=0):
        six, seven = rows_product(array, weights, 6, (F32, BF16), at)
        four, five = rows_product(array, weights, 4, (BF16, BF16), at)
        six = six + self.other_core(seven).astype(F32)
        far_one = self.far(six.astype(BF16)).astype(F32)
        array = after(array, six)
        two, three = rows_product(array, weights, 2, (F32, F32), at)
        zero, one = rows_product(array, weights, 0, (F32, F32), at)
        three = (three + self.other_core(five).astype(F32)).astype(BF16)
        two = (two + self.other_core(four).astype(F32) + far_one).astype(BF16)
        return after((zero, one), two, three) + (two, three)

    def scatter_near(self, sums):
        zero, one, two, three = sums
        return zero, one, self.near(two), self.near(three)

    def scatter_end(self, sums):
        zero, one, two, three = sums
        partner = self.other_core((one + three.astype(F32)).astype(BF16))
        return zero + two.astype(F32) + partner.astype(F32)

    def scatter_tokens(self, array, weights, at=0):
        return self.scatter_end(self.scatter_near(self.scatter_begin(array, weights, at)))

    def share_columns(self, weight):
        return lax.all_to_all(weight, self.axes, split_axis=1, concat_axis=0, tiled=True)

    def gather_weight(self, rows):
        rows = lax.all_gather(rows, self.spread, axis=0, tiled=True)
        return [rows, swap(rows, self.half)] if self.half else [rows]

    def weight_terms(self, parts, right):
        if self.half:
            away = swap(parts_product(parts, right, 1, 2, None), self.half)
            return parts_product(parts, right, 0, 2, away)
        return parts_product(parts, right, 0, 1, None)

    def scatter_weight(self, terms):
        return lax.psum_scatter(terms, self.spread, scatter_dimension=0, tiled=True)

    def return_columns(self, grad):
        return lax.all_to_all(grad, self.axes, split_axis=0, concat_axis=1, tiled=True)


def scalars(values):
    return jnp.stack(values).astype(jnp.int32)


VMEM_SPEC = pl.BlockSpec(memory_space=pltpu.VMEM)


SMALL = pl.CostEstimate(flops=1024, bytes_accessed=1024, transcendentals=0)


def cost(microseconds):
    return pl.CostEstimate(flops=int(microseconds * 1.1e9), bytes_accessed=int(microseconds * 3e6), transcendentals=0)


def vmem(limit):
    return pltpu.CompilerParams(vmem_limit_bytes=limit * MIB)


def parts_of(widths, tails, unit):
    out = []
    at = 0
    for device in range(8):
        for p in range(widths[0] // unit):
            for i, width in enumerate(widths):
                out.append((i, device * width + p * unit, unit, at))
                at += unit
        for i, width in enumerate(tails):
            out.append((len(widths) + i, device * width, width, at))
            at += width
    return out


def mix_columns(weights, gain, unit, tails=()):
    arrays = list(weights) + list(tails)
    rows = arrays[0].shape[0]
    parts = parts_of([w.shape[1] // 8 for w in weights], [w.shape[1] // 8 for w in tails], unit)

    def body(gain_ref, *refs):
        factor = gain_ref[...]
        for i, source, width, at in parts:
            value = refs[i][:, source : source + width]
            if i < len(weights):
                value = (value.astype(F32) * factor).astype(BF16)
            refs[-1][:, at : at + width] = value

    return pl.pallas_call(
        body,
        out_shape=jax.ShapeDtypeStruct((rows, sum(w.shape[1] for w in arrays)), BF16),
        in_specs=[VMEM_SPEC] * (1 + len(arrays)),
        out_specs=VMEM_SPEC,
        cost_estimate=SMALL,
        name="mix_columns",
    )(gain, *arrays)


def part_columns(mixed, weights, gain, unit, tail=None):
    count = len(weights)
    rows = weights[0].shape[0]
    tails = [] if tail is None else [tail]
    parts = parts_of([w.shape[1] // 8 for w in weights], [w // 8 for w in tails], unit)

    def body(mixed_ref, gain_ref, *refs):
        ins, outs = refs[:count], refs[count:-1]
        factor = gain_ref[...]
        acc = jnp.zeros((rows, LANES), F32)
        for i, source, width, at in parts:
            value = mixed_ref[:, at : at + width].astype(F32)
            if i < count:
                term = ins[i][:, source : source + width].astype(F32) * value
                for p in range(width // LANES):
                    acc = acc + term[:, p * LANES : (p + 1) * LANES]
                value = value * factor
            outs[i][:, source : source + width] = value
        refs[-1][...] = jnp.sum(acc, axis=1, keepdims=True)

    shapes = [w.shape for w in weights] + [(rows, w) for w in tails] + [(rows, 1)]
    return pl.pallas_call(
        body,
        out_shape=[jax.ShapeDtypeStruct(shape, F32) for shape in shapes],
        in_specs=[VMEM_SPEC] * (2 + count),
        out_specs=[VMEM_SPEC] * len(shapes),
        cost_estimate=SMALL,
        name="part_columns",
    )(mixed, gain, *weights)


def rows_product(array, weights, first, types, at):
    size = array.shape[0] // 8
    depth = array.shape[1]
    count = len(weights)
    each = weights[0].shape[0]
    step = min(512, each)
    inner = each // step

    def body(array_ref, *refs):
        at = pl.program_id(0) // inner
        for i in range(count):

            @pl.when(at == i)
            def _():
                both = dot_nt(array_ref[...], refs[i][...])
                refs[count][...] = both[:size].astype(types[0])
                refs[count + 1][...] = both[size:].astype(types[1])

    def weight_spec(i):
        return pl.BlockSpec((step, depth), lambda j: (jnp.clip(j - i * inner, 0, inner - 1), at))

    return pl.pallas_call(
        body,
        grid=(count * inner,),
        out_shape=[jax.ShapeDtypeStruct((size, count * each), t) for t in types],
        in_specs=[pl.BlockSpec((2 * size, depth), lambda j: (first // 2, 0))] + [weight_spec(i) for i in range(count)],
        out_specs=[pl.BlockSpec((size, step), lambda j: (0, j))] * 2,
        compiler_params=vmem(40),
        cost_estimate=SMALL,
        name="rows_product",
    )(array, *weights)


def parts_product(parts, right, which, pieces, added):
    size = parts[0].shape[0]
    tokens, width = right.shape
    model = parts[0].shape[1] // pieces
    step = 512 if width <= 1024 else 256
    offset = which * (model // step)

    def body(*refs):
        ins, right_ref = refs[:8], refs[8]
        out_ref, stacked = refs[-2], refs[-1]
        for p in range(8):
            stacked[p * size : (p + 1) * size, :] = ins[p][...]
        total = dot_tn(stacked[...], right_ref[...])
        if added is not None:
            total = total + refs[9][...].astype(F32)
        out_ref[...] = total.astype(BF16)

    block = pl.BlockSpec((step, width), lambda j: (j, 0))
    return pl.pallas_call(
        body,
        grid=(model // step,),
        out_shape=jax.ShapeDtypeStruct((model, width), BF16),
        in_specs=[pl.BlockSpec((size, step), lambda j: (0, offset + j))] * 8
        + [pl.BlockSpec((tokens, width), lambda j: (0, 0))]
        + ([block] if added is not None else []),
        out_specs=block,
        scratch_shapes=[pltpu.VMEM((tokens, step), BF16)],
        compiler_params=vmem(48),
        cost_estimate=cost(model * width / 175000),
        name="parts_product",
    )(*parts, right, *([added] if added is not None else []))


def attention_terms(first, right, second, other):
    size, model = first[0].shape
    tokens, width = right.shape
    rest = other.shape[1]
    step = 512

    def body(*refs):
        right_ref, other_ref, out_ref, stacked = refs[16:]
        stack_parts(refs[:8], stacked)
        out_ref[:, :width] = dot_tn(stacked[...], right_ref[...]).astype(BF16)
        stack_parts(refs[8:16], stacked)
        out_ref[:, width:] = dot_tn(stacked[...], other_ref[...]).astype(BF16)

    return pl.pallas_call(
        body,
        grid=(model // step,),
        out_shape=jax.ShapeDtypeStruct((model, width + rest), BF16),
        in_specs=[pl.BlockSpec((size, step), lambda j: (0, j))] * 16 + [whole(right), whole(other)],
        out_specs=pl.BlockSpec((step, width + rest), lambda j: (j, 0)),
        scratch_shapes=[pltpu.VMEM((tokens, step), BF16)],
        compiler_params=vmem(48),
        cost_estimate=cost(14),
        name="attention_terms",
    )(*first, *second, right, other)


UNIT = 256
CHUNK = 512


def whole(part):
    return pl.BlockSpec(part.shape, lambda *at: (0, 0))


def stack_parts(ins, stacked):
    size = ins[0].shape[0]
    for p in range(8):
        stacked[p * size : (p + 1) * size, :] = ins[p][...]


def split_product(stacked, rows, weights):
    depth = weights[0].shape[0]
    total = dot_nn(stacked[rows, :depth], weights[0][...])
    for i in range(1, len(weights)):
        total += dot_nn(stacked[rows, i * depth : (i + 1) * depth], weights[i][...])
    return total


def feed_forward(parts, weights):
    size, model = parts[0].shape
    tokens = 8 * size
    width = weights[0].shape[1]
    count = len(weights)

    def body(*refs):
        ins, ws = refs[:8], refs[8 : 8 + count]
        hidden_ref, slope_ref, stacked = refs[8 + count :]

        @pl.when(pl.program_id(0) == 0)
        def _():
            stack_parts(ins, stacked)

        @pl.loop(0, tokens // CHUNK)
        def _(i):
            rows = pl.ds(pl.multiple_of(i * CHUNK, CHUNK), CHUNK)
            both = split_product(stacked, rows, ws)
            gate, up = both[:, :UNIT], both[:, UNIT:]
            sigmoid = 1.0 / (1.0 + jnp.exp(-gate))
            silu = gate * sigmoid
            hidden_ref[rows, :] = (silu * up).astype(BF16)
            slope_ref[rows, :UNIT] = up * sigmoid * (1.0 + gate * (1.0 - sigmoid))
            slope_ref[rows, UNIT:] = silu

    return pl.pallas_call(
        body,
        grid=(width // (2 * UNIT),),
        out_shape=[jax.ShapeDtypeStruct((tokens, width // 2), BF16), jax.ShapeDtypeStruct((tokens, width), F32)],
        in_specs=[whole(p) for p in parts] + [pl.BlockSpec((w.shape[0], 2 * UNIT), lambda j: (0, j)) for w in weights],
        out_specs=[pl.BlockSpec((tokens, UNIT), lambda j: (0, j)), pl.BlockSpec((tokens, 2 * UNIT), lambda j: (0, j))],
        scratch_shapes=[pltpu.VMEM((tokens, model), BF16)],
        compiler_params=vmem(56),
        cost_estimate=SMALL,
        name="feed_forward",
    )(*parts, *weights)


def feed_back(parts, weights, slope):
    size, model = parts[0].shape
    tokens = 8 * size
    width = slope.shape[1]
    count = len(weights)

    def body(*refs):
        ins, ws = refs[:8], refs[8 : 8 + count]
        slope_ref, out_ref, stacked = refs[8 + count :]

        @pl.when(pl.program_id(0) == 0)
        def _():
            stack_parts(ins, stacked)

        @pl.loop(0, tokens // CHUNK)
        def _(i):
            rows = pl.ds(pl.multiple_of(i * CHUNK, CHUNK), CHUNK)
            grad = split_product(stacked, rows, ws)
            out_ref[rows, :UNIT] = (grad * slope_ref[rows, :UNIT]).astype(BF16)
            out_ref[rows, UNIT:] = (grad * slope_ref[rows, UNIT:]).astype(BF16)

    return pl.pallas_call(
        body,
        grid=(width // (2 * UNIT),),
        out_shape=jax.ShapeDtypeStruct((tokens, width), BF16),
        in_specs=[whole(p) for p in parts]
        + [pl.BlockSpec((w.shape[0], UNIT), lambda j: (0, j)) for w in weights]
        + [pl.BlockSpec((tokens, 2 * UNIT), lambda j: (0, j))],
        out_specs=pl.BlockSpec((tokens, 2 * UNIT), lambda j: (0, j)),
        scratch_shapes=[pltpu.VMEM((tokens, model), BF16)],
        compiler_params=vmem(56),
        cost_estimate=SMALL,
        name="feed_back",
    )(*parts, *weights, slope)


def rope(x, cosine, sine):
    lane = lax.broadcasted_iota(jnp.int32, x.shape, 1)
    other = jnp.where(lane % HD < HD // 2, pltpu.roll(x, LANES - HD // 2, 1), pltpu.roll(x, HD // 2, 1))
    return x * cosine + other * sine


def head_masks(shape):
    lane = lax.broadcasted_iota(jnp.int32, shape, 1)
    return [lane < HD, lane >= HD]


def attend_body(place_ref, *refs, blocks, size):
    ins = refs[:8]
    weight_ref, cos_ref, sin_ref, start_ref, saved_ref, mixed_ref, lse_ref, stacked, proj_ref = refs[8:]

    @pl.when((pl.program_id(0) == 0) & (pl.program_id(1) == 0))
    def _():
        stack_parts(ins, stacked)

    @pl.when(pl.program_id(1) == 0)
    def _():
        @pl.loop(0, stacked.shape[0] // CHUNK)
        def _(i):
            rows = pl.ds(pl.multiple_of(i * CHUNK, CHUNK), CHUNK)
            proj_ref[rows, :] = dot_nn(stacked[rows, :], weight_ref[...])

    base = pl.program_id(1) * blocks

    def token_rows(j):
        return pl.ds(pl.multiple_of(place_ref[base + j] * size, size), size)

    def table_rows(j):
        return pl.ds(pl.multiple_of(place_ref[8 + base + j] * size, size), size)

    for j in range(blocks):
        rows = token_rows(j)
        here = slice(j * size, (j + 1) * size)
        cosine, sine = cos_ref[table_rows(j), :], sin_ref[table_rows(j), :]
        for p in range(2):
            value = proj_ref[rows, p * LANES : (p + 1) * LANES]
            saved_ref[here, p * LANES : (p + 1) * LANES] = rope(value, cosine, sine).astype(BF16)
        saved_ref[here, 2 * LANES :] = proj_ref[rows, 2 * LANES :].astype(BF16)
    for j in range(blocks):
        here = slice(j * size, (j + 1) * size)
        upto = (j + 1) * size
        query = saved_ref[here, :LANES]
        keys = saved_ref[:upto, LANES : 2 * LANES]
        values = saved_ref[:upto, 2 * LANES :]
        row = lax.broadcasted_iota(jnp.int32, (size, upto), 0) + j * size
        col = lax.broadcasted_iota(jnp.int32, (size, upto), 1)
        visible = (col <= row) & (col >= start_ref[table_rows(j), :])
        q_heads = head_masks(query.shape)
        v_heads = head_masks(values.shape)
        mixed, totals = [], []
        for h in range(2):
            scores = dot_nt(jnp.where(q_heads[h], query, jnp.zeros_like(query)), keys) * SCALE
            scores = jnp.where(visible, scores, MASKED_SCORE)
            top = jnp.max(scores, axis=1, keepdims=True)
            weights = jnp.exp(scores - top)
            total = jnp.sum(weights, axis=1, keepdims=True)
            probs = (weights * (1.0 / total)).astype(BF16)
            mixed.append(dot_nn(probs, jnp.where(v_heads[h], values, jnp.zeros_like(values))))
            totals.append(jnp.broadcast_to(top + jnp.log(total), query.shape))
        mixed_ref[token_rows(j), :] = (mixed[0] + mixed[1]).astype(BF16)
        lse_ref[here, :] = jnp.where(q_heads[0], totals[0], totals[1])


def attend_back_body(place_ref, *refs, blocks, size):
    ins = refs[:8]
    weight_ref, saved_ref, lse_ref, cos_ref, sin_ref, start_ref, out_ref, dk_ref, dv_ref, stacked, grad_ref = refs[8:]

    @pl.when((pl.program_id(0) == 0) & (pl.program_id(1) == 0))
    def _():
        stack_parts(ins, stacked)

    @pl.when(pl.program_id(1) == 0)
    def _():
        @pl.loop(0, stacked.shape[0] // CHUNK)
        def _(i):
            rows = pl.ds(pl.multiple_of(i * CHUNK, CHUNK), CHUNK)
            grad_ref[rows, :] = dot_nn(stacked[rows, :], weight_ref[...]).astype(BF16)

    base = pl.program_id(1) * blocks

    def token_rows(j):
        return pl.ds(pl.multiple_of(place_ref[base + j] * size, size), size)

    def table_rows(j):
        return pl.ds(pl.multiple_of(place_ref[8 + base + j] * size, size), size)

    dk_ref[...] = jnp.zeros_like(dk_ref)
    dv_ref[...] = jnp.zeros_like(dv_ref)
    for j in range(blocks):
        here = slice(j * size, (j + 1) * size)
        upto = (j + 1) * size
        rows = token_rows(j)
        query = saved_ref[here, :LANES]
        keys = saved_ref[:upto, LANES : 2 * LANES]
        values = saved_ref[:upto, 2 * LANES :]
        grad = grad_ref[rows, :]
        row = lax.broadcasted_iota(jnp.int32, (size, upto), 0) + j * size
        col = lax.broadcasted_iota(jnp.int32, (size, upto), 1)
        visible = (col <= row) & (col >= start_ref[table_rows(j), :])
        q_heads = head_masks(query.shape)
        k_heads = head_masks(keys.shape)
        dq = jnp.zeros(query.shape, F32)
        dk = jnp.zeros(keys.shape, F32)
        dv = jnp.zeros(keys.shape, F32)
        for h in range(2):
            q_head = jnp.where(q_heads[h], query, jnp.zeros_like(query))
            g_head = jnp.where(q_heads[h], grad, jnp.zeros_like(grad))
            scores = dot_nt(q_head, keys) * SCALE
            log_total = lse_ref[here, h * HD : h * HD + 1]
            probs = jnp.exp(jnp.where(visible, scores, MASKED_SCORE) - log_total)
            d_probs = dot_nt(g_head, values)
            inner = jnp.sum(probs * d_probs, axis=1, keepdims=True)
            d_scores = (probs * (d_probs - inner)).astype(BF16)
            dq += dot_nn(d_scores, jnp.where(k_heads[h], keys, jnp.zeros_like(keys)))
            dk += dot_tn(d_scores, q_head)
            dv += dot_tn(probs.astype(BF16), g_head)
        out_ref[rows, :LANES] = rope(dq * SCALE, cos_ref[table_rows(j), :], -sin_ref[table_rows(j), :]).astype(BF16)
        dk_ref[:upto, :] += dk
        dv_ref[:upto, :] += dv
    for j in range(blocks):
        here = slice(j * size, (j + 1) * size)
        rows = token_rows(j)
        out_ref[rows, LANES : 2 * LANES] = rope(dk_ref[here, :] * SCALE, cos_ref[table_rows(j), :], -sin_ref[table_rows(j), :]).astype(BF16)
        out_ref[rows, 2 * LANES :] = dv_ref[here, :].astype(BF16)


def by_pair(tokens, width):
    return pl.BlockSpec((tokens, width), lambda p, s, places: (0, p))


def by_sequence(length, width):
    return pl.BlockSpec((length, width), lambda p, s, places: (s, p))


def attend(parts, weight, cosine, sine, start, places, length):
    size, model = parts[0].shape
    tokens = 8 * size
    width = weight.shape[1]
    pairs = width // (3 * LANES)
    return pl.pallas_call(
        functools.partial(attend_body, blocks=length // size, size=size),
        grid_spec=pltpu.PrefetchScalarGridSpec(
            num_scalar_prefetch=1,
            grid=(pairs, tokens // length),
            in_specs=[whole(p) for p in parts] + [by_pair(model, 3 * LANES)] + [whole(t) for t in (cosine, sine, start)],
            out_specs=[by_sequence(length, 3 * LANES), by_pair(tokens, LANES), by_sequence(length, LANES)],
            scratch_shapes=[pltpu.VMEM((tokens, model), BF16), pltpu.VMEM((tokens, 3 * LANES), F32)],
        ),
        out_shape=[
            jax.ShapeDtypeStruct((tokens, width), BF16),
            jax.ShapeDtypeStruct((tokens, pairs * LANES), BF16),
            jax.ShapeDtypeStruct((tokens, pairs * LANES), F32),
        ],
        compiler_params=vmem(56),
        cost_estimate=SMALL,
        name="attend",
    )(places, *parts, weight, cosine, sine, start)


def attend_back(parts, weight, saved, lse, cosine, sine, start, places, length):
    size, model = parts[0].shape
    tokens = 8 * size
    pairs = weight.shape[1] // LANES
    return pl.pallas_call(
        functools.partial(attend_back_body, blocks=length // size, size=size),
        grid_spec=pltpu.PrefetchScalarGridSpec(
            num_scalar_prefetch=1,
            grid=(pairs, tokens // length),
            in_specs=[whole(p) for p in parts]
            + [by_pair(model, LANES), by_sequence(length, 3 * LANES), by_sequence(length, LANES)]
            + [whole(t) for t in (cosine, sine, start)],
            out_specs=by_pair(tokens, 3 * LANES),
            scratch_shapes=[
                pltpu.VMEM((length, LANES), F32),
                pltpu.VMEM((length, LANES), F32),
                pltpu.VMEM((tokens, model), BF16),
                pltpu.VMEM((tokens, LANES), BF16),
            ],
        ),
        out_shape=jax.ShapeDtypeStruct(saved.shape, BF16),
        compiler_params=vmem(56),
        cost_estimate=cost(36),
        name="attend_back",
    )(places, *parts, weight, saved, lse, cosine, sine, start)


def rms_rows(values):
    factor = lax.rsqrt(jnp.mean(values * values, axis=-1, keepdims=True) + EPSILON)
    return values * factor, factor


def norm_input(inner, normed, factor):
    return factor * (inner - normed * jnp.mean(inner * normed, axis=-1, keepdims=True))


def rope_tables(positions):
    inverse_freq = 1.0 / ROPE_BASE ** (jnp.arange(0, HD, 2, dtype=F32) / HD)
    angles = positions.astype(F32)[:, None] * inverse_freq
    cosine, sine = jnp.cos(angles), jnp.sin(angles)
    return (
        jnp.concatenate([cosine] * 4, axis=1),
        jnp.concatenate([-sine, sine, -sine, sine], axis=1),
    )


ATTN = Group("y", "x", None, ("r", "zh", "zl"))
MLP = Group("y", "x", None, ("r", "zh", "zl"))


def local(tokens, positions, attn_gain, w_query, w_key, w_value, w_out, mlp_gain, w_gate, w_up, w_down, out_grad):
    own = tokens.shape[1]
    model = tokens.shape[2]
    length = own * lax.axis_size("x") * lax.axis_size("c")
    outer = lax.axis_size("r")
    shape = tokens.shape
    gain_one = attn_gain.astype(F32)[:, None]
    gain_two = mlp_gain.astype(F32)[:, None]

    where = positions.reshape(own, 1)
    for axis in ("c", "x", "y"):
        where = jnp.concatenate([where, swap(where, axis)], axis=0)
    where = where.reshape(-1)
    cosine, sine = rope_tables(where)
    place = lax.axis_index("x") * 2 + lax.axis_index("c")
    core = lax.axis_index("c")
    slot_part = scalars([jnp.where(core == 0, PLACES[0].index(i), PLACES[1].index(i)) for i in range(8)])
    slots = scalars([s * 4 + (j ^ place) for s in range(2) for j in range(4)])
    places = jnp.concatenate([slot_part[slots], slots])
    row = jnp.arange(2 * length, dtype=jnp.int32)
    start = (((row // own % 4) ^ place) * own + row % own - where)[:, None]

    out_rows = jnp.transpose(w_out)
    (out_all,) = ATTN.gather_weight(out_rows)
    qkv_mixed = mix_columns([w_query, w_key, w_value], gain_one, LANES)
    qkv_all = ATTN.gather_weight(after(ATTN.share_columns(qkv_mixed), out_all))
    inputs = after(tokens, qkv_mixed).reshape(own, model).astype(F32)
    normed_one, factor_one = rms_rows(inputs)
    one_low = normed_one.astype(BF16)
    count = w_gate.shape[0]
    out_blocks = [out_all[i * count : (i + 1) * count] for i in range(out_all.shape[0] // count)]
    rows_mixed = mix_columns(
        [after(w_gate, one_low, cosine, sine, start, places), w_up], gain_two, UNIT, out_blocks
    )

    one_all = ATTN.gather_tokens(ATTN.to_slots(one_low, outer))
    rows_shared = MLP.share_columns(rows_mixed)
    split = w_gate.shape[1] // 4
    width = w_out.shape[0] // 8
    gate_up_rows = rows_shared[:, :split]
    out_all = [
        jnp.concatenate(
            [rows_shared[:, split + i * width : split + (i + 1) * width] for i in range(len(out_blocks))], axis=0
        )
    ]
    gate_up_all = MLP.gather_weight(gate_up_rows)
    saved, mixed, lse = attend(after(one_all, gate_up_rows), qkv_all[0], cosine, sine, start, places, length)
    grad_rows = out_grad.reshape(own, model)
    dy_near = MLP.gather_near(MLP.to_slots(after(grad_rows, gate_up_rows), outer))
    dy_all = MLP.gather_far(after(dy_near, mixed))
    down_rows = MLP.share_columns(jnp.transpose(after(w_down, mixed)))
    down_all = MLP.gather_weight(after(down_rows, gate_up_rows))

    attn_out = ATTN.scatter_tokens(after(mixed, *dy_near), out_all)
    first_sum = inputs + ATTN.from_slots(attn_out, outer)

    normed_two, factor_two = rms_rows(first_sum)
    two_low = MLP.to_slots(normed_two.astype(BF16), outer)
    two_all = MLP.gather_tokens(after(two_low, *dy_all))
    hidden, slope = feed_forward(two_all, gate_up_all)
    down_terms = MLP.weight_terms(dy_all, hidden)
    down_grad = MLP.scatter_weight(down_terms)
    d_gate_up = feed_back(after(dy_all, down_terms), down_all, slope)
    inner_sums = MLP.scatter_begin(d_gate_up, gate_up_all)
    gate_up_terms = MLP.weight_terms(two_all, after(d_gate_up, *inner_sums))
    inner_sums = MLP.scatter_near(inner_sums)
    gate_up_grad = MLP.scatter_weight(after(gate_up_terms, down_grad, *inner_sums))
    inner_two = MLP.scatter_end(inner_sums)

    d_first = grad_rows.astype(F32) + norm_input(MLP.from_slots(inner_two, outer), normed_two, factor_two)
    d_attn_all = ATTN.gather_tokens(ATTN.to_slots(d_first.astype(BF16), outer))
    mlp_sums = MLP.scatter_begin(after(hidden, d_first), down_all)
    d_attn_all = after(d_attn_all, *mlp_sums)
    d_qkv = attend_back(d_attn_all, out_all[0], saved, lse, cosine, sine, start, places, length)
    terms = attention_terms(one_all, d_qkv, d_attn_all, mixed)
    inner_sums = ATTN.scatter_begin(after(d_qkv, terms), qkv_all)
    attn_grad = ATTN.scatter_weight(after(terms, gate_up_grad, inner_sums[0]))
    mlp_sums = MLP.scatter_near(after(mlp_sums, *inner_sums))
    gate_up_grad, down_grad = after((gate_up_grad, down_grad), *inner_sums)
    inner_one = ATTN.scatter_end(ATTN.scatter_near(inner_sums))
    tokens_grad = (d_first + norm_input(ATTN.from_slots(inner_one, outer), normed_one, factor_one)).astype(BF16)
    mlp_out = MLP.scatter_end(mlp_sums)
    block_out = (first_sum + MLP.from_slots(mlp_out, outer)).astype(BF16)

    down_w = jnp.transpose(MLP.return_columns(down_grad).astype(F32))
    gate_w, up_w, gain_mlp = part_columns(MLP.return_columns(gate_up_grad), [w_gate, w_up], gain_two, UNIT)
    attn_grad = after(attn_grad, tokens_grad, block_out, down_w)
    query_w, key_w, value_w, out_w, gain_attn = part_columns(
        ATTN.return_columns(attn_grad), [w_query, w_key, w_value], gain_one, LANES, w_out.shape[0]
    )
    return (
        block_out.reshape(shape),
        tokens_grad.reshape(shape),
        gain_attn.reshape(-1),
        query_w,
        key_w,
        value_w,
        jnp.transpose(out_w),
        gain_mlp.reshape(-1),
        gate_w,
        up_w,
        down_w,
    )


def solution(mesh):
    fsdp = mesh.shape["fsdp"]
    sizes = (fsdp // 8, 2, 2, 2, mesh.shape["ctx"] // 2, 2)
    fine = Mesh(mesh.devices.reshape(sizes), AXES)
    rows, cols = AXES[:4], AXES[4:]
    tokens, places, vector = P(rows, cols, None), P(rows, cols), P(AXES)
    first, second = P(AXES, None), P(None, AXES)
    in_specs = (tokens, places, vector, first, first, first, second, vector, first, first, second, tokens)
    out_specs = (tokens, tokens, vector, first, first, first, second, vector, first, first, second)
    return jax.shard_map(local, mesh=fine, in_specs=in_specs, out_specs=out_specs, check_vma=False)
```

```python
import functools

import jax
import jax.numpy as jnp
from jax import lax
from jax.experimental import pallas as pl
from jax.experimental.pallas import tpu as pltpu
from jax.sharding import Mesh
from jax.sharding import PartitionSpec as P

H = 32
HD = 64
EPSILON = 1e-05
ROPE_BASE = 130000.0
MASKED_SCORE = -1e30
SCALE = HD ** (-0.5)
LANES = 128
MIB = 1 << 20
BF16 = jnp.bfloat16
F32 = jnp.float32
AXES = ("r", "zh", "zl", "y", "x", "c")
NT = (((1,), (1,)), ((), ()))
TN = (((0,), (0,)), ((), ()))


def dot_nn(a, b):
    return jnp.dot(a, b, preferred_element_type=F32)


def dot_nt(a, b):
    return lax.dot_general(a, b, NT, preferred_element_type=F32)


def dot_tn(a, b):
    return lax.dot_general(a, b, TN, preferred_element_type=F32)


def flip(x, axes, masks):
    return lax.ppermute(x, axes, [(i, i ^ masks[i & 1]) for i in range(8)])


def swap(x, axis):
    return lax.ppermute(x, axis, [(0, 1), (1, 0)])


def after(x, *others):
    return lax.optimization_barrier((x,) + others)[0]


PLACES = ((0, 1, 2, 3, 5, 4, 6, 7), (0, 1, 4, 5, 3, 2, 6, 7))


class Group:
    def __init__(self, d1, d2, half, spread):
        self.axes = (d1, d2, "c")
        self.half, self.spread = half, spread

    def column_order(self, outer):
        names = ("r", "zh", "zl", "y", "x")
        sizes = dict(zip(names, (outer, 2, 2, 2, 2)))
        sequence = ([self.half] if self.half else []) + list(self.spread) + list(self.axes[:2])
        order = [0]
        for name in sequence:
            step = 1
            for later in names[names.index(name) + 1 :]:
                step *= sizes[later]
            order = [base + step * i for base in order for i in range(sizes[name])]
        return order

    def reorder(self, x, order):
        if order == list(range(len(order))):
            return x
        width = x.shape[1] // len(order)
        return jnp.concatenate([x[:, i * width : (i + 1) * width] for i in order], axis=1)

    def flip_halves(self, x):
        if not self.half:
            return x
        width = x.shape[1] // 2
        at = lax.axis_index(self.half)
        first = lax.dynamic_slice_in_dim(x, at * width, width, axis=1)
        return jnp.concatenate([first, lax.dynamic_slice_in_dim(x, (1 - at) * width, width, axis=1)], axis=1)

    def to_slots(self, x, outer):
        return self.flip_halves(self.reorder(x, self.column_order(outer)))

    def from_slots(self, x, outer):
        order = self.column_order(outer)
        return self.reorder(self.flip_halves(x), [order.index(i) for i in range(len(order))])

    def other_core(self, x):
        return flip(x, self.axes, (1, 1))

    def near(self, x):
        return flip(x, self.axes, (2, 4))

    def far(self, x):
        return flip(x, self.axes, (4, 2))

    def gather_near(self, x):
        partner = self.other_core(x)
        return x, partner, self.near(x), self.near(partner)

    def gather_far(self, parts):
        x, partner, near_one, near_two = parts
        far_one = self.far(near_one)
        parts = [x, partner, near_one, near_two, self.other_core(near_one), self.other_core(near_two)]
        return parts + [far_one, self.other_core(far_one)]

    def gather_tokens(self, x):
        return self.gather_far(self.gather_near(x))

    def scatter_begin(self, array, weights, at=0):
        six, seven = rows_product(array, weights, 6, (F32, BF16), at)
        four, five = rows_product(array, weights, 4, (BF16, BF16), at)
        six = six + self.other_core(seven).astype(F32)
        far_one = self.far(six.astype(BF16)).astype(F32)
        array = after(array, six)
        two, three = rows_product(array, weights, 2, (F32, F32), at)
        zero, one = rows_product(array, weights, 0, (F32, F32), at)
        three = (three + self.other_core(five).astype(F32)).astype(BF16)
        two = (two + self.other_core(four).astype(F32) + far_one).astype(BF16)
        return after((zero, one), two, three) + (two, three)

    def scatter_near(self, sums):
        zero, one, two, three = sums
        return zero, one, self.near(two), self.near(three)

    def scatter_end(self, sums):
        zero, one, two, three = sums
        partner = self.other_core((one + three.astype(F32)).astype(BF16))
        return zero + two.astype(F32) + partner.astype(F32)

    def scatter_tokens(self, array, weights, at=0):
        return self.scatter_end(self.scatter_near(self.scatter_begin(array, weights, at)))

    def share_columns(self, weight):
        return lax.all_to_all(weight, self.axes, split_axis=1, concat_axis=0, tiled=True)

    def gather_weight(self, rows):
        rows = lax.all_gather(rows, self.spread, axis=0, tiled=True)
        return [rows, swap(rows, self.half)] if self.half else [rows]

    def weight_terms(self, parts, right):
        if self.half:
            away = swap(parts_product(parts, right, 1, 2, None), self.half)
            return parts_product(parts, right, 0, 2, away)
        return parts_product(parts, right, 0, 1, None)

    def scatter_weight(self, terms):
        return lax.psum_scatter(terms, self.spread, scatter_dimension=0, tiled=True)

    def return_columns(self, grad):
        return lax.all_to_all(grad, self.axes, split_axis=0, concat_axis=1, tiled=True)


def scalars(values):
    return jnp.stack(values).astype(jnp.int32)


VMEM_SPEC = pl.BlockSpec(memory_space=pltpu.VMEM)


SMALL = pl.CostEstimate(flops=1024, bytes_accessed=1024, transcendentals=0)


def cost(microseconds):
    return pl.CostEstimate(flops=int(microseconds * 1.1e9), bytes_accessed=int(microseconds * 3e6), transcendentals=0)


def vmem(limit):
    return pltpu.CompilerParams(vmem_limit_bytes=limit * MIB)


def parts_of(widths, tails, unit):
    out = []
    at = 0
    for device in range(8):
        for p in range(widths[0] // unit):
            for i, width in enumerate(widths):
                out.append((i, device * width + p * unit, unit, at))
                at += unit
        for i, width in enumerate(tails):
            out.append((len(widths) + i, device * width, width, at))
            at += width
    return out


def mix_columns(weights, gain, unit, tails=()):
    arrays = list(weights) + list(tails)
    rows = arrays[0].shape[0]
    parts = parts_of([w.shape[1] // 8 for w in weights], [w.shape[1] // 8 for w in tails], unit)

    def body(gain_ref, *refs):
        factor = gain_ref[...]
        for i, source, width, at in parts:
            value = refs[i][:, source : source + width]
            if i < len(weights):
                value = (value.astype(F32) * factor).astype(BF16)
            refs[-1][:, at : at + width] = value

    return pl.pallas_call(
        body,
        out_shape=jax.ShapeDtypeStruct((rows, sum(w.shape[1] for w in arrays)), BF16),
        in_specs=[VMEM_SPEC] * (1 + len(arrays)),
        out_specs=VMEM_SPEC,
        cost_estimate=SMALL,
        name="mix_columns",
    )(gain, *arrays)


def part_columns(mixed, weights, gain, unit, tail=None):
    count = len(weights)
    rows = weights[0].shape[0]
    tails = [] if tail is None else [tail]
    parts = parts_of([w.shape[1] // 8 for w in weights], [w // 8 for w in tails], unit)

    def body(mixed_ref, gain_ref, *refs):
        ins, outs = refs[:count], refs[count:-1]
        factor = gain_ref[...]
        acc = jnp.zeros((rows, LANES), F32)
        for i, source, width, at in parts:
            value = mixed_ref[:, at : at + width].astype(F32)
            if i < count:
                term = ins[i][:, source : source + width].astype(F32) * value
                for p in range(width // LANES):
                    acc = acc + term[:, p * LANES : (p + 1) * LANES]
                value = value * factor
            outs[i][:, source : source + width] = value
        refs[-1][...] = jnp.sum(acc, axis=1, keepdims=True)

    shapes = [w.shape for w in weights] + [(rows, w) for w in tails] + [(rows, 1)]
    return pl.pallas_call(
        body,
        out_shape=[jax.ShapeDtypeStruct(shape, F32) for shape in shapes],
        in_specs=[VMEM_SPEC] * (2 + count),
        out_specs=[VMEM_SPEC] * len(shapes),
        cost_estimate=SMALL,
        name="part_columns",
    )(mixed, gain, *weights)


def rows_product(array, weights, first, types, at):
    size = array.shape[0] // 8
    depth = array.shape[1]
    count = len(weights)
    each = weights[0].shape[0]
    step = min(512, each)
    inner = each // step

    def body(array_ref, *refs):
        at = pl.program_id(0) // inner
        for i in range(count):

            @pl.when(at == i)
            def _():
                both = dot_nt(array_ref[...], refs[i][...])
                refs[count][...] = both[:size].astype(types[0])
                refs[count + 1][...] = both[size:].astype(types[1])

    def weight_spec(i):
        return pl.BlockSpec((step, depth), lambda j: (jnp.clip(j - i * inner, 0, inner - 1), at))

    return pl.pallas_call(
        body,
        grid=(count * inner,),
        out_shape=[jax.ShapeDtypeStruct((size, count * each), t) for t in types],
        in_specs=[pl.BlockSpec((2 * size, depth), lambda j: (first // 2, 0))] + [weight_spec(i) for i in range(count)],
        out_specs=[pl.BlockSpec((size, step), lambda j: (0, j))] * 2,
        compiler_params=vmem(40),
        cost_estimate=SMALL,
        name="rows_product",
    )(array, *weights)


def parts_product(parts, right, which, pieces, added):
    size = parts[0].shape[0]
    tokens, width = right.shape
    model = parts[0].shape[1] // pieces
    step = 512 if width <= 1024 else 256
    offset = which * (model // step)

    def body(*refs):
        ins, right_ref = refs[:8], refs[8]
        out_ref, stacked = refs[-2], refs[-1]
        for p in range(8):
            stacked[p * size : (p + 1) * size, :] = ins[p][...]
        total = dot_tn(stacked[...], right_ref[...])
        if added is not None:
            total = total + refs[9][...].astype(F32)
        out_ref[...] = total.astype(BF16)

    block = pl.BlockSpec((step, width), lambda j: (j, 0))
    return pl.pallas_call(
        body,
        grid=(model // step,),
        out_shape=jax.ShapeDtypeStruct((model, width), BF16),
        in_specs=[pl.BlockSpec((size, step), lambda j: (0, offset + j))] * 8
        + [pl.BlockSpec((tokens, width), lambda j: (0, 0))]
        + ([block] if added is not None else []),
        out_specs=block,
        scratch_shapes=[pltpu.VMEM((tokens, step), BF16)],
        compiler_params=vmem(48),
        cost_estimate=cost(model * width / 175000),
        name="parts_product",
    )(*parts, right, *([added] if added is not None else []))


def attention_terms(first, right, second, other):
    size, model = first[0].shape
    tokens, width = right.shape
    rest = other.shape[1]
    step = 512

    def body(*refs):
        right_ref, other_ref, out_ref, stacked = refs[16:]
        stack_parts(refs[:8], stacked)
        out_ref[:, :width] = dot_tn(stacked[...], right_ref[...]).astype(BF16)
        stack_parts(refs[8:16], stacked)
        out_ref[:, width:] = dot_tn(stacked[...], other_ref[...]).astype(BF16)

    return pl.pallas_call(
        body,
        grid=(model // step,),
        out_shape=jax.ShapeDtypeStruct((model, width + rest), BF16),
        in_specs=[pl.BlockSpec((size, step), lambda j: (0, j))] * 16 + [whole(right), whole(other)],
        out_specs=pl.BlockSpec((step, width + rest), lambda j: (j, 0)),
        scratch_shapes=[pltpu.VMEM((tokens, step), BF16)],
        compiler_params=vmem(48),
        cost_estimate=cost(14),
        name="attention_terms",
    )(*first, *second, right, other)


UNIT = 256
CHUNK = 512


def whole(part):
    return pl.BlockSpec(part.shape, lambda *at: (0, 0))


def stack_parts(ins, stacked):
    size = ins[0].shape[0]
    for p in range(8):
        stacked[p * size : (p + 1) * size, :] = ins[p][...]


def split_product(stacked, rows, weights):
    depth = weights[0].shape[0]
    total = dot_nn(stacked[rows, :depth], weights[0][...])
    for i in range(1, len(weights)):
        total += dot_nn(stacked[rows, i * depth : (i + 1) * depth], weights[i][...])
    return total


def feed_forward(parts, weights):
    size, model = parts[0].shape
    tokens = 8 * size
    width = weights[0].shape[1]
    count = len(weights)

    def body(*refs):
        ins, ws = refs[:8], refs[8 : 8 + count]
        hidden_ref, slope_ref, stacked = refs[8 + count :]

        @pl.when(pl.program_id(0) == 0)
        def _():
            stack_parts(ins, stacked)

        @pl.loop(0, tokens // CHUNK)
        def _(i):
            rows = pl.ds(pl.multiple_of(i * CHUNK, CHUNK), CHUNK)
            both = split_product(stacked, rows, ws)
            gate, up = both[:, :UNIT], both[:, UNIT:]
            sigmoid = 1.0 / (1.0 + jnp.exp(-gate))
            silu = gate * sigmoid
            hidden_ref[rows, :] = (silu * up).astype(BF16)
            slope_ref[rows, :UNIT] = up * sigmoid * (1.0 + gate * (1.0 - sigmoid))
            slope_ref[rows, UNIT:] = silu

    return pl.pallas_call(
        body,
        grid=(width // (2 * UNIT),),
        out_shape=[jax.ShapeDtypeStruct((tokens, width // 2), BF16), jax.ShapeDtypeStruct((tokens, width), F32)],
        in_specs=[whole(p) for p in parts] + [pl.BlockSpec((w.shape[0], 2 * UNIT), lambda j: (0, j)) for w in weights],
        out_specs=[pl.BlockSpec((tokens, UNIT), lambda j: (0, j)), pl.BlockSpec((tokens, 2 * UNIT), lambda j: (0, j))],
        scratch_shapes=[pltpu.VMEM((tokens, model), BF16)],
        compiler_params=vmem(56),
        cost_estimate=SMALL,
        name="feed_forward",
    )(*parts, *weights)


def feed_back(parts, weights, slope):
    size, model = parts[0].shape
    tokens = 8 * size
    width = slope.shape[1]
    count = len(weights)

    def body(*refs):
        ins, ws = refs[:8], refs[8 : 8 + count]
        slope_ref, out_ref, stacked = refs[8 + count :]

        @pl.when(pl.program_id(0) == 0)
        def _():
            stack_parts(ins, stacked)

        @pl.loop(0, tokens // CHUNK)
        def _(i):
            rows = pl.ds(pl.multiple_of(i * CHUNK, CHUNK), CHUNK)
            grad = split_product(stacked, rows, ws)
            out_ref[rows, :UNIT] = (grad * slope_ref[rows, :UNIT]).astype(BF16)
            out_ref[rows, UNIT:] = (grad * slope_ref[rows, UNIT:]).astype(BF16)

    return pl.pallas_call(
        body,
        grid=(width // (2 * UNIT),),
        out_shape=jax.ShapeDtypeStruct((tokens, width), BF16),
        in_specs=[whole(p) for p in parts]
        + [pl.BlockSpec((w.shape[0], UNIT), lambda j: (0, j)) for w in weights]
        + [pl.BlockSpec((tokens, 2 * UNIT), lambda j: (0, j))],
        out_specs=pl.BlockSpec((tokens, 2 * UNIT), lambda j: (0, j)),
        scratch_shapes=[pltpu.VMEM((tokens, model), BF16)],
        compiler_params=vmem(56),
        cost_estimate=SMALL,
        name="feed_back",
    )(*parts, *weights, slope)


def rope(x, cosine, sine):
    lane = lax.broadcasted_iota(jnp.int32, x.shape, 1)
    other = jnp.where(lane % HD < HD // 2, pltpu.roll(x, LANES - HD // 2, 1), pltpu.roll(x, HD // 2, 1))
    return x * cosine + other * sine


def head_masks(shape):
    lane = lax.broadcasted_iota(jnp.int32, shape, 1)
    return [lane < HD, lane >= HD]


def attend_body(place_ref, *refs, blocks, size):
    ins = refs[:8]
    weight_ref, cos_ref, sin_ref, start_ref, saved_ref, mixed_ref, lse_ref, stacked, proj_ref = refs[8:]

    @pl.when((pl.program_id(0) == 0) & (pl.program_id(1) == 0))
    def _():
        stack_parts(ins, stacked)

    @pl.when(pl.program_id(1) == 0)
    def _():
        @pl.loop(0, stacked.shape[0] // CHUNK)
        def _(i):
            rows = pl.ds(pl.multiple_of(i * CHUNK, CHUNK), CHUNK)
            proj_ref[rows, :] = dot_nn(stacked[rows, :], weight_ref[...])

    base = pl.program_id(1) * blocks

    def token_rows(j):
        return pl.ds(pl.multiple_of(place_ref[base + j] * size, size), size)

    def table_rows(j):
        return pl.ds(pl.multiple_of(place_ref[8 + base + j] * size, size), size)

    for j in range(blocks):
        rows = token_rows(j)
        here = slice(j * size, (j + 1) * size)
        cosine, sine = cos_ref[table_rows(j), :], sin_ref[table_rows(j), :]
        for p in range(2):
            value = proj_ref[rows, p * LANES : (p + 1) * LANES]
            saved_ref[here, p * LANES : (p + 1) * LANES] = rope(value, cosine, sine).astype(BF16)
        saved_ref[here, 2 * LANES :] = proj_ref[rows, 2 * LANES :].astype(BF16)
    for j in range(blocks):
        here = slice(j * size, (j + 1) * size)
        upto = (j + 1) * size
        query = saved_ref[here, :LANES]
        keys = saved_ref[:upto, LANES : 2 * LANES]
        values = saved_ref[:upto, 2 * LANES :]
        row = lax.broadcasted_iota(jnp.int32, (size, upto), 0) + j * size
        col = lax.broadcasted_iota(jnp.int32, (size, upto), 1)
        visible = (col <= row) & (col >= start_ref[table_rows(j), :])
        q_heads = head_masks(query.shape)
        v_heads = head_masks(values.shape)
        mixed, totals = [], []
        for h in range(2):
            scores = dot_nt(jnp.where(q_heads[h], query, jnp.zeros_like(query)), keys) * SCALE
            scores = jnp.where(visible, scores, MASKED_SCORE)
            top = jnp.max(scores, axis=1, keepdims=True)
            weights = jnp.exp(scores - top)
            total = jnp.sum(weights, axis=1, keepdims=True)
            probs = (weights * (1.0 / total)).astype(BF16)
            mixed.append(dot_nn(probs, jnp.where(v_heads[h], values, jnp.zeros_like(values))))
            totals.append(jnp.broadcast_to(top + jnp.log(total), query.shape))
        mixed_ref[token_rows(j), :] = (mixed[0] + mixed[1]).astype(BF16)
        lse_ref[here, :] = jnp.where(q_heads[0], totals[0], totals[1])


def attend_back_body(place_ref, *refs, blocks, size):
    ins = refs[:8]
    weight_ref, saved_ref, lse_ref, cos_ref, sin_ref, start_ref, out_ref, dk_ref, dv_ref, stacked, grad_ref = refs[8:]

    @pl.when((pl.program_id(0) == 0) & (pl.program_id(1) == 0))
    def _():
        stack_parts(ins, stacked)

    @pl.when(pl.program_id(1) == 0)
    def _():
        @pl.loop(0, stacked.shape[0] // CHUNK)
        def _(i):
            rows = pl.ds(pl.multiple_of(i * CHUNK, CHUNK), CHUNK)
            grad_ref[rows, :] = dot_nn(stacked[rows, :], weight_ref[...]).astype(BF16)

    base = pl.program_id(1) * blocks

    def token_rows(j):
        return pl.ds(pl.multiple_of(place_ref[base + j] * size, size), size)

    def table_rows(j):
        return pl.ds(pl.multiple_of(place_ref[8 + base + j] * size, size), size)

    dk_ref[...] = jnp.zeros_like(dk_ref)
    dv_ref[...] = jnp.zeros_like(dv_ref)
    for j in range(blocks):
        here = slice(j * size, (j + 1) * size)
        upto = (j + 1) * size
        rows = token_rows(j)
        query = saved_ref[here, :LANES]
        keys = saved_ref[:upto, LANES : 2 * LANES]
        values = saved_ref[:upto, 2 * LANES :]
        grad = grad_ref[rows, :]
        row = lax.broadcasted_iota(jnp.int32, (size, upto), 0) + j * size
        col = lax.broadcasted_iota(jnp.int32, (size, upto), 1)
        visible = (col <= row) & (col >= start_ref[table_rows(j), :])
        q_heads = head_masks(query.shape)
        k_heads = head_masks(keys.shape)
        dq = jnp.zeros(query.shape, F32)
        dk = jnp.zeros(keys.shape, F32)
        dv = jnp.zeros(keys.shape, F32)
        for h in range(2):
            q_head = jnp.where(q_heads[h], query, jnp.zeros_like(query))
            g_head = jnp.where(q_heads[h], grad, jnp.zeros_like(grad))
            scores = dot_nt(q_head, keys) * SCALE
            log_total = lse_ref[here, h * HD : h * HD + 1]
            probs = jnp.exp(jnp.where(visible, scores, MASKED_SCORE) - log_total)
            d_probs = dot_nt(g_head, values)
            inner = jnp.sum(probs * d_probs, axis=1, keepdims=True)
            d_scores = (probs * (d_probs - inner)).astype(BF16)
            dq += dot_nn(d_scores, jnp.where(k_heads[h], keys, jnp.zeros_like(keys)))
            dk += dot_tn(d_scores, q_head)
            dv += dot_tn(probs.astype(BF16), g_head)
        out_ref[rows, :LANES] = rope(dq * SCALE, cos_ref[table_rows(j), :], -sin_ref[table_rows(j), :]).astype(BF16)
        dk_ref[:upto, :] += dk
        dv_ref[:upto, :] += dv
    for j in range(blocks):
        here = slice(j * size, (j + 1) * size)
        rows = token_rows(j)
        out_ref[rows, LANES : 2 * LANES] = rope(dk_ref[here, :] * SCALE, cos_ref[table_rows(j), :], -sin_ref[table_rows(j), :]).astype(BF16)
        out_ref[rows, 2 * LANES :] = dv_ref[here, :].astype(BF16)


def by_pair(tokens, width):
    return pl.BlockSpec((tokens, width), lambda p, s, places: (0, p))


def by_sequence(length, width):
    return pl.BlockSpec((length, width), lambda p, s, places: (s, p))


def attend(parts, weight, cosine, sine, start, places, length):
    size, model = parts[0].shape
    tokens = 8 * size
    width = weight.shape[1]
    pairs = width // (3 * LANES)
    return pl.pallas_call(
        functools.partial(attend_body, blocks=length // size, size=size),
        grid_spec=pltpu.PrefetchScalarGridSpec(
            num_scalar_prefetch=1,
            grid=(pairs, tokens // length),
            in_specs=[whole(p) for p in parts] + [by_pair(model, 3 * LANES)] + [whole(t) for t in (cosine, sine, start)],
            out_specs=[by_sequence(length, 3 * LANES), by_pair(tokens, LANES), by_sequence(length, LANES)],
            scratch_shapes=[pltpu.VMEM((tokens, model), BF16), pltpu.VMEM((tokens, 3 * LANES), F32)],
        ),
        out_shape=[
            jax.ShapeDtypeStruct((tokens, width), BF16),
            jax.ShapeDtypeStruct((tokens, pairs * LANES), BF16),
            jax.ShapeDtypeStruct((tokens, pairs * LANES), F32),
        ],
        compiler_params=vmem(56),
        cost_estimate=SMALL,
        name="attend",
    )(places, *parts, weight, cosine, sine, start)


def attend_back(parts, weight, saved, lse, cosine, sine, start, places, length):
    size, model = parts[0].shape
    tokens = 8 * size
    pairs = weight.shape[1] // LANES
    return pl.pallas_call(
        functools.partial(attend_back_body, blocks=length // size, size=size),
        grid_spec=pltpu.PrefetchScalarGridSpec(
            num_scalar_prefetch=1,
            grid=(pairs, tokens // length),
            in_specs=[whole(p) for p in parts]
            + [by_pair(model, LANES), by_sequence(length, 3 * LANES), by_sequence(length, LANES)]
            + [whole(t) for t in (cosine, sine, start)],
            out_specs=by_pair(tokens, 3 * LANES),
            scratch_shapes=[
                pltpu.VMEM((length, LANES), F32),
                pltpu.VMEM((length, LANES), F32),
                pltpu.VMEM((tokens, model), BF16),
                pltpu.VMEM((tokens, LANES), BF16),
            ],
        ),
        out_shape=jax.ShapeDtypeStruct(saved.shape, BF16),
        compiler_params=vmem(56),
        cost_estimate=cost(36),
        name="attend_back",
    )(places, *parts, weight, saved, lse, cosine, sine, start)


def rms_rows(values):
    factor = lax.rsqrt(jnp.mean(values * values, axis=-1, keepdims=True) + EPSILON)
    return values * factor, factor


def norm_input(inner, normed, factor):
    return factor * (inner - normed * jnp.mean(inner * normed, axis=-1, keepdims=True))


def rope_tables(positions):
    inverse_freq = 1.0 / ROPE_BASE ** (jnp.arange(0, HD, 2, dtype=F32) / HD)
    angles = positions.astype(F32)[:, None] * inverse_freq
    cosine, sine = jnp.cos(angles), jnp.sin(angles)
    return (
        jnp.concatenate([cosine] * 4, axis=1),
        jnp.concatenate([-sine, sine, -sine, sine], axis=1),
    )


ATTN = Group("y", "x", None, ("r", "zh", "zl"))
MLP = Group("y", "x", None, ("r", "zh", "zl"))


def local(tokens, positions, attn_gain, w_query, w_key, w_value, w_out, mlp_gain, w_gate, w_up, w_down, out_grad):
    own = tokens.shape[1]
    model = tokens.shape[2]
    length = own * lax.axis_size("x") * lax.axis_size("c")
    outer = lax.axis_size("r")
    shape = tokens.shape
    gain_one = attn_gain.astype(F32)[:, None]
    gain_two = mlp_gain.astype(F32)[:, None]

    where = positions.reshape(own, 1)
    for axis in ("c", "x", "y"):
        where = jnp.concatenate([where, swap(where, axis)], axis=0)
    where = where.reshape(-1)
    cosine, sine = rope_tables(where)
    place = lax.axis_index("x") * 2 + lax.axis_index("c")
    core = lax.axis_index("c")
    slot_part = scalars([jnp.where(core == 0, PLACES[0].index(i), PLACES[1].index(i)) for i in range(8)])
    slots = scalars([s * 4 + (j ^ place) for s in range(2) for j in range(4)])
    places = jnp.concatenate([slot_part[slots], slots])
    row = jnp.arange(2 * length, dtype=jnp.int32)
    start = (((row // own % 4) ^ place) * own + row % own - where)[:, None]

    out_rows = jnp.transpose(w_out)
    (out_all,) = ATTN.gather_weight(out_rows)
    qkv_mixed = mix_columns([w_query, w_key, w_value], gain_one, LANES)
    qkv_all = ATTN.gather_weight(after(ATTN.share_columns(qkv_mixed), out_all))
    inputs = after(tokens, qkv_mixed).reshape(own, model).astype(F32)
    normed_one, factor_one = rms_rows(inputs)
    one_low = normed_one.astype(BF16)
    count = w_gate.shape[0]
    out_blocks = [out_all[i * count : (i + 1) * count] for i in range(out_all.shape[0] // count)]
    rows_mixed = mix_columns(
        [after(w_gate, one_low, cosine, sine, start, places), w_up], gain_two, UNIT, out_blocks
    )

    one_all = ATTN.gather_tokens(ATTN.to_slots(one_low, outer))
    rows_shared = MLP.share_columns(rows_mixed)
    split = w_gate.shape[1] // 4
    width = w_out.shape[0] // 8
    gate_up_rows = rows_shared[:, :split]
    out_all = [
        jnp.concatenate(
            [rows_shared[:, split + i * width : split + (i + 1) * width] for i in range(len(out_blocks))], axis=0
        )
    ]
    gate_up_all = MLP.gather_weight(gate_up_rows)
    saved, mixed, lse = attend(after(one_all, gate_up_rows), qkv_all[0], cosine, sine, start, places, length)
    grad_rows = out_grad.reshape(own, model)
    dy_near = MLP.gather_near(MLP.to_slots(after(grad_rows, gate_up_rows), outer))
    dy_all = MLP.gather_far(after(dy_near, mixed))
    down_rows = MLP.share_columns(jnp.transpose(after(w_down, mixed)))
    down_all = MLP.gather_weight(after(down_rows, gate_up_rows))

    attn_out = ATTN.scatter_tokens(after(mixed, *dy_near), out_all)
    first_sum = inputs + ATTN.from_slots(attn_out, outer)

    normed_two, factor_two = rms_rows(first_sum)
    two_low = MLP.to_slots(normed_two.astype(BF16), outer)
    two_all = MLP.gather_tokens(after(two_low, *dy_all))
    hidden, slope = feed_forward(two_all, gate_up_all)
    down_terms = MLP.weight_terms(dy_all, hidden)
    down_grad = MLP.scatter_weight(down_terms)
    d_gate_up = feed_back(after(dy_all, down_terms), down_all, slope)
    inner_sums = MLP.scatter_begin(d_gate_up, gate_up_all)
    gate_up_terms = MLP.weight_terms(two_all, after(d_gate_up, *inner_sums))
    inner_sums = MLP.scatter_near(inner_sums)
    gate_up_grad = MLP.scatter_weight(after(gate_up_terms, down_grad, *inner_sums))
    inner_two = MLP.scatter_end(inner_sums)

    d_first = grad_rows.astype(F32) + norm_input(MLP.from_slots(inner_two, outer), normed_two, factor_two)
    d_attn_all = ATTN.gather_tokens(ATTN.to_slots(d_first.astype(BF16), outer))
    mlp_sums = MLP.scatter_begin(after(hidden, d_first), down_all)
    d_attn_all = after(d_attn_all, *mlp_sums)
    d_qkv = attend_back(d_attn_all, out_all[0], saved, lse, cosine, sine, start, places, length)
    terms = attention_terms(one_all, d_qkv, d_attn_all, mixed)
    inner_sums = ATTN.scatter_begin(after(d_qkv, terms), qkv_all)
    attn_grad = ATTN.scatter_weight(after(terms, gate_up_grad, inner_sums[0]))
    mlp_sums = MLP.scatter_near(after(mlp_sums, *inner_sums))
    gate_up_grad, down_grad = after((gate_up_grad, down_grad), *inner_sums)
    inner_one = ATTN.scatter_end(ATTN.scatter_near(inner_sums))
    tokens_grad = (d_first + norm_input(ATTN.from_slots(inner_one, outer), normed_one, factor_one)).astype(BF16)
    mlp_out = MLP.scatter_end(mlp_sums)
    block_out = (first_sum + MLP.from_slots(mlp_out, outer)).astype(BF16)

    gate_up_back = MLP.return_columns(gate_up_grad)
    down_w = jnp.transpose(MLP.return_columns(after(down_grad, gate_up_back)).astype(F32))
    gate_w, up_w, gain_mlp = part_columns(gate_up_back, [w_gate, w_up], gain_two, UNIT)
    attn_grad = after(attn_grad, tokens_grad, block_out, down_w, gate_w)
    query_w, key_w, value_w, out_w, gain_attn = part_columns(
        ATTN.return_columns(attn_grad), [w_query, w_key, w_value], gain_one, LANES, w_out.shape[0]
    )
    return (
        block_out.reshape(shape),
        tokens_grad.reshape(shape),
        gain_attn.reshape(-1),
        query_w,
        key_w,
        value_w,
        jnp.transpose(out_w),
        gain_mlp.reshape(-1),
        gate_w,
        up_w,
        down_w,
    )


def solution(mesh):
    fsdp = mesh.shape["fsdp"]
    sizes = (fsdp // 8, 2, 2, 2, mesh.shape["ctx"] // 2, 2)
    fine = Mesh(mesh.devices.reshape(sizes), AXES)
    rows, cols = AXES[:4], AXES[4:]
    tokens, places, vector = P(rows, cols, None), P(rows, cols), P(AXES)
    first, second = P(AXES, None), P(None, AXES)
    in_specs = (tokens, places, vector, first, first, first, second, vector, first, first, second, tokens)
    out_specs = (tokens, tokens, vector, first, first, first, second, vector, first, first, second)
    return jax.shard_map(local, mesh=fine, in_specs=in_specs, out_specs=out_specs, check_vma=False)
```

```python
import functools

import jax
import jax.numpy as jnp
from jax import lax
from jax.experimental import pallas as pl
from jax.experimental.pallas import tpu as pltpu
from jax.sharding import Mesh
from jax.sharding import PartitionSpec as P

H = 32
HD = 64
EPSILON = 1e-05
ROPE_BASE = 130000.0
MASKED_SCORE = -1e30
SCALE = HD ** (-0.5)
LANES = 128
MIB = 1 << 20
BF16 = jnp.bfloat16
F32 = jnp.float32
AXES = ("r", "zh", "zl", "y", "x", "c")
NT = (((1,), (1,)), ((), ()))
TN = (((0,), (0,)), ((), ()))


def dot_nn(a, b):
    return jnp.dot(a, b, preferred_element_type=F32)


def dot_nt(a, b):
    return lax.dot_general(a, b, NT, preferred_element_type=F32)


def dot_tn(a, b):
    return lax.dot_general(a, b, TN, preferred_element_type=F32)


def flip(x, axes, masks):
    return lax.ppermute(x, axes, [(i, i ^ masks[i & 1]) for i in range(8)])


def swap(x, axis):
    return lax.ppermute(x, axis, [(0, 1), (1, 0)])


def after(x, *others):
    return lax.optimization_barrier((x,) + others)[0]


PLACES = ((0, 1, 2, 3, 5, 4, 6, 7), (0, 1, 4, 5, 3, 2, 6, 7))


class Group:
    def __init__(self, d1, d2, half, spread):
        self.axes = (d1, d2, "c")
        self.half, self.spread = half, spread

    def column_order(self, outer):
        names = ("r", "zh", "zl", "y", "x")
        sizes = dict(zip(names, (outer, 2, 2, 2, 2)))
        sequence = ([self.half] if self.half else []) + list(self.spread) + list(self.axes[:2])
        order = [0]
        for name in sequence:
            step = 1
            for later in names[names.index(name) + 1 :]:
                step *= sizes[later]
            order = [base + step * i for base in order for i in range(sizes[name])]
        return order

    def reorder(self, x, order):
        if order == list(range(len(order))):
            return x
        width = x.shape[1] // len(order)
        return jnp.concatenate([x[:, i * width : (i + 1) * width] for i in order], axis=1)

    def flip_halves(self, x):
        if not self.half:
            return x
        width = x.shape[1] // 2
        at = lax.axis_index(self.half)
        first = lax.dynamic_slice_in_dim(x, at * width, width, axis=1)
        return jnp.concatenate([first, lax.dynamic_slice_in_dim(x, (1 - at) * width, width, axis=1)], axis=1)

    def to_slots(self, x, outer):
        return self.flip_halves(self.reorder(x, self.column_order(outer)))

    def from_slots(self, x, outer):
        order = self.column_order(outer)
        return self.reorder(self.flip_halves(x), [order.index(i) for i in range(len(order))])

    def other_core(self, x):
        return flip(x, self.axes, (1, 1))

    def near(self, x):
        return flip(x, self.axes, (2, 4))

    def far(self, x):
        return flip(x, self.axes, (4, 2))

    def gather_near(self, x):
        partner = self.other_core(x)
        return x, partner, self.near(x), self.near(partner)

    def gather_far(self, parts):
        x, partner, near_one, near_two = parts
        far_one = self.far(near_one)
        parts = [x, partner, near_one, near_two, self.other_core(near_one), self.other_core(near_two)]
        return parts + [far_one, self.other_core(far_one)]

    def gather_tokens(self, x):
        return self.gather_far(self.gather_near(x))

    def scatter_begin(self, array, weights, at=0):
        six, seven = rows_product(array, weights, 6, (F32, BF16), at)
        four, five = rows_product(array, weights, 4, (BF16, BF16), at)
        six = six + self.other_core(seven).astype(F32)
        far_one = self.far(six.astype(BF16)).astype(F32)
        array = after(array, six)
        two, three = rows_product(array, weights, 2, (F32, F32), at)
        zero, one = rows_product(array, weights, 0, (F32, F32), at)
        three = (three + self.other_core(five).astype(F32)).astype(BF16)
        two = (two + self.other_core(four).astype(F32) + far_one).astype(BF16)
        return after((zero, one), two, three) + (two, three)

    def scatter_near(self, sums):
        zero, one, two, three = sums
        return zero, one, self.near(two), self.near(three)

    def scatter_end(self, sums):
        zero, one, two, three = sums
        partner = self.other_core((one + three.astype(F32)).astype(BF16))
        return zero + two.astype(F32) + partner.astype(F32)

    def scatter_tokens(self, array, weights, at=0):
        return self.scatter_end(self.scatter_near(self.scatter_begin(array, weights, at)))

    def share_columns(self, weight):
        return lax.all_to_all(weight, self.axes, split_axis=1, concat_axis=0, tiled=True)

    def gather_weight(self, rows):
        rows = lax.all_gather(rows, self.spread, axis=0, tiled=True)
        return [rows, swap(rows, self.half)] if self.half else [rows]

    def weight_terms(self, parts, right):
        if self.half:
            away = swap(parts_product(parts, right, 1, 2, None), self.half)
            return parts_product(parts, right, 0, 2, away)
        return parts_product(parts, right, 0, 1, None)

    def scatter_weight(self, terms):
        return lax.psum_scatter(terms, self.spread, scatter_dimension=0, tiled=True)

    def return_columns(self, grad):
        return lax.all_to_all(grad, self.axes, split_axis=0, concat_axis=1, tiled=True)


def scalars(values):
    return jnp.stack(values).astype(jnp.int32)


VMEM_SPEC = pl.BlockSpec(memory_space=pltpu.VMEM)


SMALL = pl.CostEstimate(flops=1024, bytes_accessed=1024, transcendentals=0)


def cost(microseconds):
    return pl.CostEstimate(flops=int(microseconds * 1.1e9), bytes_accessed=int(microseconds * 3e6), transcendentals=0)


def vmem(limit):
    return pltpu.CompilerParams(vmem_limit_bytes=limit * MIB)


def parts_of(widths, tails, unit):
    out = []
    at = 0
    for device in range(8):
        for p in range(widths[0] // unit):
            for i, width in enumerate(widths):
                out.append((i, device * width + p * unit, unit, at))
                at += unit
        for i, width in enumerate(tails):
            out.append((len(widths) + i, device * width, width, at))
            at += width
    return out


def mix_columns(weights, gain, unit, tails=()):
    arrays = list(weights) + list(tails)
    rows = arrays[0].shape[0]
    parts = parts_of([w.shape[1] // 8 for w in weights], [w.shape[1] // 8 for w in tails], unit)

    def body(gain_ref, *refs):
        factor = gain_ref[...]
        for i, source, width, at in parts:
            value = refs[i][:, source : source + width]
            if i < len(weights):
                value = (value.astype(F32) * factor).astype(BF16)
            refs[-1][:, at : at + width] = value

    return pl.pallas_call(
        body,
        out_shape=jax.ShapeDtypeStruct((rows, sum(w.shape[1] for w in arrays)), BF16),
        in_specs=[VMEM_SPEC] * (1 + len(arrays)),
        out_specs=VMEM_SPEC,
        cost_estimate=SMALL,
        name="mix_columns",
    )(gain, *arrays)


def part_columns(mixed, weights, gain, unit, tail=None):
    count = len(weights)
    rows = weights[0].shape[0]
    tails = [] if tail is None else [tail]
    parts = parts_of([w.shape[1] // 8 for w in weights], [w // 8 for w in tails], unit)

    def body(mixed_ref, gain_ref, *refs):
        ins, outs = refs[:count], refs[count:-1]
        factor = gain_ref[...]
        acc = jnp.zeros((rows, LANES), F32)
        for i, source, width, at in parts:
            value = mixed_ref[:, at : at + width].astype(F32)
            if i < count:
                term = ins[i][:, source : source + width].astype(F32) * value
                for p in range(width // LANES):
                    acc = acc + term[:, p * LANES : (p + 1) * LANES]
                value = value * factor
            outs[i][:, source : source + width] = value
        refs[-1][...] = jnp.sum(acc, axis=1, keepdims=True)

    shapes = [w.shape for w in weights] + [(rows, w) for w in tails] + [(rows, 1)]
    return pl.pallas_call(
        body,
        out_shape=[jax.ShapeDtypeStruct(shape, F32) for shape in shapes],
        in_specs=[VMEM_SPEC] * (2 + count),
        out_specs=[VMEM_SPEC] * len(shapes),
        cost_estimate=SMALL,
        name="part_columns",
    )(mixed, gain, *weights)


def rows_product(array, weights, first, types, at):
    size = array.shape[0] // 8
    depth = array.shape[1]
    count = len(weights)
    each = weights[0].shape[0]
    step = min(512, each)
    inner = each // step

    def body(array_ref, *refs):
        at = pl.program_id(0) // inner
        for i in range(count):

            @pl.when(at == i)
            def _():
                both = dot_nt(array_ref[...], refs[i][...])
                refs[count][...] = both[:size].astype(types[0])
                refs[count + 1][...] = both[size:].astype(types[1])

    def weight_spec(i):
        return pl.BlockSpec((step, depth), lambda j: (jnp.clip(j - i * inner, 0, inner - 1), at))

    return pl.pallas_call(
        body,
        grid=(count * inner,),
        out_shape=[jax.ShapeDtypeStruct((size, count * each), t) for t in types],
        in_specs=[pl.BlockSpec((2 * size, depth), lambda j: (first // 2, 0))] + [weight_spec(i) for i in range(count)],
        out_specs=[pl.BlockSpec((size, step), lambda j: (0, j))] * 2,
        compiler_params=vmem(40),
        cost_estimate=SMALL,
        name="rows_product",
    )(array, *weights)


def parts_product(parts, right, which, pieces, added):
    size = parts[0].shape[0]
    tokens, width = right.shape
    model = parts[0].shape[1] // pieces
    step = 512 if width <= 1024 else 256
    offset = which * (model // step)

    def body(*refs):
        ins, right_ref = refs[:8], refs[8]
        out_ref, stacked = refs[-2], refs[-1]
        for p in range(8):
            stacked[p * size : (p + 1) * size, :] = ins[p][...]
        total = dot_tn(stacked[...], right_ref[...])
        if added is not None:
            total = total + refs[9][...].astype(F32)
        out_ref[...] = total.astype(BF16)

    block = pl.BlockSpec((step, width), lambda j: (j, 0))
    return pl.pallas_call(
        body,
        grid=(model // step,),
        out_shape=jax.ShapeDtypeStruct((model, width), BF16),
        in_specs=[pl.BlockSpec((size, step), lambda j: (0, offset + j))] * 8
        + [pl.BlockSpec((tokens, width), lambda j: (0, 0))]
        + ([block] if added is not None else []),
        out_specs=block,
        scratch_shapes=[pltpu.VMEM((tokens, step), BF16)],
        compiler_params=vmem(48),
        cost_estimate=cost(model * width / 175000),
        name="parts_product",
    )(*parts, right, *([added] if added is not None else []))


def attention_terms(first, right, second, other):
    size, model = first[0].shape
    tokens, width = right.shape
    rest = other.shape[1]
    step = 512

    def body(*refs):
        right_ref, other_ref, out_ref, stacked = refs[16:]
        stack_parts(refs[:8], stacked)
        out_ref[:, :width] = dot_tn(stacked[...], right_ref[...]).astype(BF16)
        stack_parts(refs[8:16], stacked)
        out_ref[:, width:] = dot_tn(stacked[...], other_ref[...]).astype(BF16)

    return pl.pallas_call(
        body,
        grid=(model // step,),
        out_shape=jax.ShapeDtypeStruct((model, width + rest), BF16),
        in_specs=[pl.BlockSpec((size, step), lambda j: (0, j))] * 16 + [whole(right), whole(other)],
        out_specs=pl.BlockSpec((step, width + rest), lambda j: (j, 0)),
        scratch_shapes=[pltpu.VMEM((tokens, step), BF16)],
        compiler_params=vmem(48),
        cost_estimate=cost(14),
        name="attention_terms",
    )(*first, *second, right, other)


UNIT = 256
CHUNK = 512


def whole(part):
    return pl.BlockSpec(part.shape, lambda *at: (0, 0))


def stack_parts(ins, stacked):
    size = ins[0].shape[0]
    for p in range(8):
        stacked[p * size : (p + 1) * size, :] = ins[p][...]


def split_product(stacked, rows, weights):
    depth = weights[0].shape[0]
    total = dot_nn(stacked[rows, :depth], weights[0][...])
    for i in range(1, len(weights)):
        total += dot_nn(stacked[rows, i * depth : (i + 1) * depth], weights[i][...])
    return total


def feed_forward(parts, weights):
    size, model = parts[0].shape
    tokens = 8 * size
    width = weights[0].shape[1]
    count = len(weights)

    def body(*refs):
        ins, ws = refs[:8], refs[8 : 8 + count]
        hidden_ref, slope_ref, stacked = refs[8 + count :]

        @pl.when(pl.program_id(0) == 0)
        def _():
            stack_parts(ins, stacked)

        @pl.loop(0, tokens // CHUNK)
        def _(i):
            rows = pl.ds(pl.multiple_of(i * CHUNK, CHUNK), CHUNK)
            both = split_product(stacked, rows, ws)
            gate, up = both[:, :UNIT], both[:, UNIT:]
            sigmoid = 1.0 / (1.0 + jnp.exp(-gate))
            silu = gate * sigmoid
            hidden_ref[rows, :] = (silu * up).astype(BF16)
            slope_ref[rows, :UNIT] = up * sigmoid * (1.0 + gate * (1.0 - sigmoid))
            slope_ref[rows, UNIT:] = silu

    return pl.pallas_call(
        body,
        grid=(width // (2 * UNIT),),
        out_shape=[jax.ShapeDtypeStruct((tokens, width // 2), BF16), jax.ShapeDtypeStruct((tokens, width), F32)],
        in_specs=[whole(p) for p in parts] + [pl.BlockSpec((w.shape[0], 2 * UNIT), lambda j: (0, j)) for w in weights],
        out_specs=[pl.BlockSpec((tokens, UNIT), lambda j: (0, j)), pl.BlockSpec((tokens, 2 * UNIT), lambda j: (0, j))],
        scratch_shapes=[pltpu.VMEM((tokens, model), BF16)],
        compiler_params=vmem(56),
        cost_estimate=SMALL,
        name="feed_forward",
    )(*parts, *weights)


def feed_back(parts, weights, slope):
    size, model = parts[0].shape
    tokens = 8 * size
    width = slope.shape[1]
    count = len(weights)

    def body(*refs):
        ins, ws = refs[:8], refs[8 : 8 + count]
        slope_ref, out_ref, stacked = refs[8 + count :]

        @pl.when(pl.program_id(0) == 0)
        def _():
            stack_parts(ins, stacked)

        @pl.loop(0, tokens // CHUNK)
        def _(i):
            rows = pl.ds(pl.multiple_of(i * CHUNK, CHUNK), CHUNK)
            grad = split_product(stacked, rows, ws)
            out_ref[rows, :UNIT] = (grad * slope_ref[rows, :UNIT]).astype(BF16)
            out_ref[rows, UNIT:] = (grad * slope_ref[rows, UNIT:]).astype(BF16)

    return pl.pallas_call(
        body,
        grid=(width // (2 * UNIT),),
        out_shape=jax.ShapeDtypeStruct((tokens, width), BF16),
        in_specs=[whole(p) for p in parts]
        + [pl.BlockSpec((w.shape[0], UNIT), lambda j: (0, j)) for w in weights]
        + [pl.BlockSpec((tokens, 2 * UNIT), lambda j: (0, j))],
        out_specs=pl.BlockSpec((tokens, 2 * UNIT), lambda j: (0, j)),
        scratch_shapes=[pltpu.VMEM((tokens, model), BF16)],
        compiler_params=vmem(56),
        cost_estimate=SMALL,
        name="feed_back",
    )(*parts, *weights, slope)


def rope(x, cosine, sine):
    lane = lax.broadcasted_iota(jnp.int32, x.shape, 1)
    other = jnp.where(lane % HD < HD // 2, pltpu.roll(x, LANES - HD // 2, 1), pltpu.roll(x, HD // 2, 1))
    return x * cosine + other * sine


def head_masks(shape):
    lane = lax.broadcasted_iota(jnp.int32, shape, 1)
    return [lane < HD, lane >= HD]


def attend_body(place_ref, *refs, blocks, size):
    ins = refs[:8]
    weight_ref, cos_ref, sin_ref, start_ref, saved_ref, mixed_ref, lse_ref, stacked, proj_ref = refs[8:]

    @pl.when((pl.program_id(0) == 0) & (pl.program_id(1) == 0))
    def _():
        stack_parts(ins, stacked)

    @pl.when(pl.program_id(1) == 0)
    def _():
        @pl.loop(0, stacked.shape[0] // CHUNK)
        def _(i):
            rows = pl.ds(pl.multiple_of(i * CHUNK, CHUNK), CHUNK)
            proj_ref[rows, :] = dot_nn(stacked[rows, :], weight_ref[...])

    base = pl.program_id(1) * blocks

    def token_rows(j):
        return pl.ds(pl.multiple_of(place_ref[base + j] * size, size), size)

    def table_rows(j):
        return pl.ds(pl.multiple_of(place_ref[8 + base + j] * size, size), size)

    for j in range(blocks):
        rows = token_rows(j)
        here = slice(j * size, (j + 1) * size)
        cosine, sine = cos_ref[table_rows(j), :], sin_ref[table_rows(j), :]
        for p in range(2):
            value = proj_ref[rows, p * LANES : (p + 1) * LANES]
            saved_ref[here, p * LANES : (p + 1) * LANES] = rope(value, cosine, sine).astype(BF16)
        saved_ref[here, 2 * LANES :] = proj_ref[rows, 2 * LANES :].astype(BF16)
    for j in range(blocks):
        here = slice(j * size, (j + 1) * size)
        upto = (j + 1) * size
        query = saved_ref[here, :LANES]
        keys = saved_ref[:upto, LANES : 2 * LANES]
        values = saved_ref[:upto, 2 * LANES :]
        row = lax.broadcasted_iota(jnp.int32, (size, upto), 0) + j * size
        col = lax.broadcasted_iota(jnp.int32, (size, upto), 1)
        visible = (col <= row) & (col >= start_ref[table_rows(j), :])
        q_heads = head_masks(query.shape)
        v_heads = head_masks(values.shape)
        mixed, totals = [], []
        for h in range(2):
            scores = dot_nt(jnp.where(q_heads[h], query, jnp.zeros_like(query)), keys) * SCALE
            scores = jnp.where(visible, scores, MASKED_SCORE)
            top = jnp.max(scores, axis=1, keepdims=True)
            weights = jnp.exp(scores - top)
            total = jnp.sum(weights, axis=1, keepdims=True)
            probs = (weights * (1.0 / total)).astype(BF16)
            mixed.append(dot_nn(probs, jnp.where(v_heads[h], values, jnp.zeros_like(values))))
            totals.append(jnp.broadcast_to(top + jnp.log(total), query.shape))
        mixed_ref[token_rows(j), :] = (mixed[0] + mixed[1]).astype(BF16)
        lse_ref[here, :] = jnp.where(q_heads[0], totals[0], totals[1])


def attend_back_body(place_ref, *refs, blocks, size):
    ins = refs[:8]
    weight_ref, saved_ref, lse_ref, cos_ref, sin_ref, start_ref, out_ref, dk_ref, dv_ref, stacked, grad_ref = refs[8:]

    @pl.when((pl.program_id(0) == 0) & (pl.program_id(1) == 0))
    def _():
        stack_parts(ins, stacked)

    @pl.when(pl.program_id(1) == 0)
    def _():
        @pl.loop(0, stacked.shape[0] // CHUNK)
        def _(i):
            rows = pl.ds(pl.multiple_of(i * CHUNK, CHUNK), CHUNK)
            grad_ref[rows, :] = dot_nn(stacked[rows, :], weight_ref[...]).astype(BF16)

    base = pl.program_id(1) * blocks

    def token_rows(j):
        return pl.ds(pl.multiple_of(place_ref[base + j] * size, size), size)

    def table_rows(j):
        return pl.ds(pl.multiple_of(place_ref[8 + base + j] * size, size), size)

    dk_ref[...] = jnp.zeros_like(dk_ref)
    dv_ref[...] = jnp.zeros_like(dv_ref)
    for j in range(blocks):
        here = slice(j * size, (j + 1) * size)
        upto = (j + 1) * size
        rows = token_rows(j)
        query = saved_ref[here, :LANES]
        keys = saved_ref[:upto, LANES : 2 * LANES]
        values = saved_ref[:upto, 2 * LANES :]
        grad = grad_ref[rows, :]
        row = lax.broadcasted_iota(jnp.int32, (size, upto), 0) + j * size
        col = lax.broadcasted_iota(jnp.int32, (size, upto), 1)
        visible = (col <= row) & (col >= start_ref[table_rows(j), :])
        q_heads = head_masks(query.shape)
        k_heads = head_masks(keys.shape)
        dq = jnp.zeros(query.shape, F32)
        dk = jnp.zeros(keys.shape, F32)
        dv = jnp.zeros(keys.shape, F32)
        for h in range(2):
            q_head = jnp.where(q_heads[h], query, jnp.zeros_like(query))
            g_head = jnp.where(q_heads[h], grad, jnp.zeros_like(grad))
            scores = dot_nt(q_head, keys) * SCALE
            log_total = lse_ref[here, h * HD : h * HD + 1]
            probs = jnp.exp(jnp.where(visible, scores, MASKED_SCORE) - log_total)
            d_probs = dot_nt(g_head, values)
            inner = jnp.sum(probs * d_probs, axis=1, keepdims=True)
            d_scores = (probs * (d_probs - inner)).astype(BF16)
            dq += dot_nn(d_scores, jnp.where(k_heads[h], keys, jnp.zeros_like(keys)))
            dk += dot_tn(d_scores, q_head)
            dv += dot_tn(probs.astype(BF16), g_head)
        out_ref[rows, :LANES] = rope(dq * SCALE, cos_ref[table_rows(j), :], -sin_ref[table_rows(j), :]).astype(BF16)
        dk_ref[:upto, :] += dk
        dv_ref[:upto, :] += dv
    for j in range(blocks):
        here = slice(j * size, (j + 1) * size)
        rows = token_rows(j)
        out_ref[rows, LANES : 2 * LANES] = rope(dk_ref[here, :] * SCALE, cos_ref[table_rows(j), :], -sin_ref[table_rows(j), :]).astype(BF16)
        out_ref[rows, 2 * LANES :] = dv_ref[here, :].astype(BF16)


def by_pair(tokens, width):
    return pl.BlockSpec((tokens, width), lambda p, s, places: (0, p))


def by_sequence(length, width):
    return pl.BlockSpec((length, width), lambda p, s, places: (s, p))


def attend(parts, weight, cosine, sine, start, places, length):
    size, model = parts[0].shape
    tokens = 8 * size
    width = weight.shape[1]
    pairs = width // (3 * LANES)
    return pl.pallas_call(
        functools.partial(attend_body, blocks=length // size, size=size),
        grid_spec=pltpu.PrefetchScalarGridSpec(
            num_scalar_prefetch=1,
            grid=(pairs, tokens // length),
            in_specs=[whole(p) for p in parts] + [by_pair(model, 3 * LANES)] + [whole(t) for t in (cosine, sine, start)],
            out_specs=[by_sequence(length, 3 * LANES), by_pair(tokens, LANES), by_sequence(length, LANES)],
            scratch_shapes=[pltpu.VMEM((tokens, model), BF16), pltpu.VMEM((tokens, 3 * LANES), F32)],
        ),
        out_shape=[
            jax.ShapeDtypeStruct((tokens, width), BF16),
            jax.ShapeDtypeStruct((tokens, pairs * LANES), BF16),
            jax.ShapeDtypeStruct((tokens, pairs * LANES), F32),
        ],
        compiler_params=vmem(56),
        cost_estimate=SMALL,
        name="attend",
    )(places, *parts, weight, cosine, sine, start)


def attend_back(parts, weight, saved, lse, cosine, sine, start, places, length):
    size, model = parts[0].shape
    tokens = 8 * size
    pairs = weight.shape[1] // LANES
    return pl.pallas_call(
        functools.partial(attend_back_body, blocks=length // size, size=size),
        grid_spec=pltpu.PrefetchScalarGridSpec(
            num_scalar_prefetch=1,
            grid=(pairs, tokens // length),
            in_specs=[whole(p) for p in parts]
            + [by_pair(model, LANES), by_sequence(length, 3 * LANES), by_sequence(length, LANES)]
            + [whole(t) for t in (cosine, sine, start)],
            out_specs=by_pair(tokens, 3 * LANES),
            scratch_shapes=[
                pltpu.VMEM((length, LANES), F32),
                pltpu.VMEM((length, LANES), F32),
                pltpu.VMEM((tokens, model), BF16),
                pltpu.VMEM((tokens, LANES), BF16),
            ],
        ),
        out_shape=jax.ShapeDtypeStruct(saved.shape, BF16),
        compiler_params=vmem(56),
        cost_estimate=cost(36),
        name="attend_back",
    )(places, *parts, weight, saved, lse, cosine, sine, start)


def rms_rows(values):
    factor = lax.rsqrt(jnp.mean(values * values, axis=-1, keepdims=True) + EPSILON)
    return values * factor, factor


def norm_input(inner, normed, factor):
    return factor * (inner - normed * jnp.mean(inner * normed, axis=-1, keepdims=True))


def rope_tables(positions):
    inverse_freq = 1.0 / ROPE_BASE ** (jnp.arange(0, HD, 2, dtype=F32) / HD)
    angles = positions.astype(F32)[:, None] * inverse_freq
    cosine, sine = jnp.cos(angles), jnp.sin(angles)
    return (
        jnp.concatenate([cosine] * 4, axis=1),
        jnp.concatenate([-sine, sine, -sine, sine], axis=1),
    )


ATTN = Group("y", "x", None, ("r", "zh", "zl"))
MLP = Group("y", "x", None, ("r", "zh", "zl"))


def local(tokens, positions, attn_gain, w_query, w_key, w_value, w_out, mlp_gain, w_gate, w_up, w_down, out_grad):
    own = tokens.shape[1]
    model = tokens.shape[2]
    length = own * lax.axis_size("x") * lax.axis_size("c")
    outer = lax.axis_size("r")
    shape = tokens.shape
    gain_one = attn_gain.astype(F32)[:, None]
    gain_two = mlp_gain.astype(F32)[:, None]

    where = positions.reshape(own, 1)
    for axis in ("c", "x", "y"):
        where = jnp.concatenate([where, swap(where, axis)], axis=0)
    where = where.reshape(-1)
    cosine, sine = rope_tables(where)
    place = lax.axis_index("x") * 2 + lax.axis_index("c")
    core = lax.axis_index("c")
    slot_part = scalars([jnp.where(core == 0, PLACES[0].index(i), PLACES[1].index(i)) for i in range(8)])
    slots = scalars([s * 4 + (j ^ place) for s in range(2) for j in range(4)])
    places = jnp.concatenate([slot_part[slots], slots])
    row = jnp.arange(2 * length, dtype=jnp.int32)
    start = (((row // own % 4) ^ place) * own + row % own - where)[:, None]

    out_rows = jnp.transpose(w_out)
    (out_all,) = ATTN.gather_weight(out_rows)
    qkv_mixed = mix_columns([w_query, w_key, w_value], gain_one, LANES)
    qkv_all = ATTN.gather_weight(after(ATTN.share_columns(qkv_mixed), out_all))
    inputs = after(tokens, qkv_mixed).reshape(own, model).astype(F32)
    normed_one, factor_one = rms_rows(inputs)
    one_low = normed_one.astype(BF16)
    count = w_gate.shape[0]
    out_blocks = [out_all[i * count : (i + 1) * count] for i in range(out_all.shape[0] // count)]
    rows_mixed = mix_columns(
        [after(w_gate, one_low, cosine, sine, start, places), w_up], gain_two, UNIT, out_blocks
    )

    one_all = ATTN.gather_tokens(ATTN.to_slots(one_low, outer))
    rows_shared = MLP.share_columns(rows_mixed)
    split = w_gate.shape[1] // 4
    width = w_out.shape[0] // 8
    gate_up_rows = rows_shared[:, :split]
    out_all = [
        jnp.concatenate(
            [rows_shared[:, split + i * width : split + (i + 1) * width] for i in range(len(out_blocks))], axis=0
        )
    ]
    gate_up_all = MLP.gather_weight(gate_up_rows)
    saved, mixed, lse = attend(after(one_all, gate_up_rows), qkv_all[0], cosine, sine, start, places, length)
    grad_rows = out_grad.reshape(own, model)
    dy_near = MLP.gather_near(MLP.to_slots(after(grad_rows, gate_up_rows), outer))
    dy_all = MLP.gather_far(after(dy_near, mixed))
    down_rows = MLP.share_columns(jnp.transpose(after(w_down, mixed)))
    down_all = MLP.gather_weight(after(down_rows, gate_up_rows))

    attn_out = ATTN.scatter_tokens(after(mixed, *dy_near), out_all)
    first_sum = inputs + ATTN.from_slots(attn_out, outer)

    normed_two, factor_two = rms_rows(first_sum)
    two_low = MLP.to_slots(normed_two.astype(BF16), outer)
    two_all = MLP.gather_tokens(after(two_low, *dy_all))
    hidden, slope = feed_forward(two_all, gate_up_all)
    down_terms = MLP.weight_terms(dy_all, hidden)
    down_grad = MLP.scatter_weight(down_terms)
    d_gate_up = feed_back(after(dy_all, down_terms), down_all, slope)
    inner_sums = MLP.scatter_begin(d_gate_up, gate_up_all)
    gate_up_terms = MLP.weight_terms(two_all, after(d_gate_up, *inner_sums))
    inner_sums = MLP.scatter_near(inner_sums)
    gate_up_grad = MLP.scatter_weight(after(gate_up_terms, down_grad, *inner_sums))
    inner_two = MLP.scatter_end(inner_sums)

    d_first = grad_rows.astype(F32) + norm_input(MLP.from_slots(inner_two, outer), normed_two, factor_two)
    d_attn_all = ATTN.gather_tokens(ATTN.to_slots(d_first.astype(BF16), outer))
    mlp_sums = MLP.scatter_begin(after(hidden, d_first), down_all)
    d_attn_all = after(d_attn_all, *mlp_sums)
    d_qkv = attend_back(d_attn_all, out_all[0], saved, lse, cosine, sine, start, places, length)
    terms = attention_terms(one_all, d_qkv, d_attn_all, mixed)
    inner_sums = ATTN.scatter_begin(after(d_qkv, terms), qkv_all)
    attn_grad = ATTN.scatter_weight(after(terms, gate_up_grad, inner_sums[0]))
    mlp_sums = MLP.scatter_near(after(mlp_sums, *inner_sums))
    gate_up_grad, down_grad = after((gate_up_grad, down_grad), *inner_sums)
    inner_one = ATTN.scatter_end(ATTN.scatter_near(inner_sums))
    tokens_grad = (d_first + norm_input(ATTN.from_slots(inner_one, outer), normed_one, factor_one)).astype(BF16)
    mlp_out = MLP.scatter_end(mlp_sums)
    block_out = (first_sum + MLP.from_slots(mlp_out, outer)).astype(BF16)

    gate_up_back = MLP.return_columns(gate_up_grad)
    down_w = jnp.transpose(MLP.return_columns(after(down_grad, gate_up_back)).astype(F32))
    gate_w, up_w, gain_mlp = part_columns(gate_up_back, [w_gate, w_up], gain_two, UNIT)
    attn_grad = after(attn_grad, tokens_grad, block_out, gate_w)
    query_w, key_w, value_w, out_w, gain_attn = part_columns(
        ATTN.return_columns(attn_grad), [w_query, w_key, w_value], gain_one, LANES, w_out.shape[0]
    )
    return (
        block_out.reshape(shape),
        tokens_grad.reshape(shape),
        gain_attn.reshape(-1),
        query_w,
        key_w,
        value_w,
        jnp.transpose(out_w),
        gain_mlp.reshape(-1),
        gate_w,
        up_w,
        down_w,
    )


def solution(mesh):
    fsdp = mesh.shape["fsdp"]
    sizes = (fsdp // 8, 2, 2, 2, mesh.shape["ctx"] // 2, 2)
    fine = Mesh(mesh.devices.reshape(sizes), AXES)
    rows, cols = AXES[:4], AXES[4:]
    tokens, places, vector = P(rows, cols, None), P(rows, cols), P(AXES)
    first, second = P(AXES, None), P(None, AXES)
    in_specs = (tokens, places, vector, first, first, first, second, vector, first, first, second, tokens)
    out_specs = (tokens, tokens, vector, first, first, first, second, vector, first, first, second)
    return jax.shard_map(local, mesh=fine, in_specs=in_specs, out_specs=out_specs, check_vma=False)
```
